32 devices in a mesh: dp: 8 (over y, x, core), expert: 4 (over z).
Axes of the slice: x: 2, y: 2, z: 4, core: 2. Of those that a mesh axis runs over, the one named last changes fastest.
Arguments:
- tokens: bfloat16 [8192, 1536], P(('dp', 'expert')), may hold values from -6 to 6
- segment_ids: int32 [32, 256], P(('dp', 'expert')), may hold values from 0 to 3, never falling along the last dimension, each value on 1 to 192 neighbouring positions
- expert_choices: int32 [8192, 8], P(('dp', 'expert')), may hold values from 0 to 19, all different within a row; in each aligned block of 256 rows (0 to 255, 256 to 511, ...) at most 116 rows name the same one
- attn_gain: bfloat16 [1536], P('dp'), may hold values from 0.099609375 to 1.8984375
- query_weight: bfloat16 [1536, 1536], P('dp'), may hold values from -0.15625 to 0.15625
- key_weight: bfloat16 [1536, 512], P('dp'), may hold values from -0.15625 to 0.15625
- value_weight: bfloat16 [1536, 512], P('dp'), may hold values from -0.15625 to 0.15625
- output_weight: bfloat16 [1536, 1536], P('dp'), may hold values from -0.625 to 0.625
- ffn_gain: bfloat16 [1536], P('dp'), may hold values from 0.099609375 to 1.8984375
- router_weight: bfloat16 [1536, 20], P('dp'), may hold values from -0.078125 to 0.078125
- expert_gate: bfloat16 [20, 1536, 512], P('expert', 'dp'), may hold values from -0.15625 to 0.15625
- expert_up: bfloat16 [20, 1536, 512], P('expert', 'dp'), may hold values from -0.15625 to 0.15625
- expert_down: bfloat16 [20, 512, 1536], P('expert', None, 'dp'), may hold values from -1.5 to 1.5
- cotangent: bfloat16 [8192, 1536], P(('dp', 'expert')), may hold values from -6 to 6
Outputs:
- mixed: bfloat16 [8192, 1536], P(('dp', 'expert'))
- grad_tokens: float32 [8192, 1536], P(('dp', 'expert'))
- grad_attn_gain: float32 [1536], P('dp')
- grad_query: float32 [1536, 1536], P('dp')
- grad_key: float32 [1536, 512], P('dp')
- grad_value: float32 [1536, 512], P('dp')
- grad_output: float32 [1536, 1536], P('dp')
- grad_ffn_gain: float32 [1536], P('dp')
- grad_router: float32 [1536, 20], P('dp')
- grad_expert_gate: float32 [20, 1536, 512], P('expert', 'dp')
- grad_expert_up: float32 [20, 1536, 512], P('expert', 'dp')
- grad_expert_down: float32 [20, 512, 1536], P('expert', None, 'dp')
The draws below stay inside these ranges and needn't reach their ends.
Inputs may be any that keep to these rules, and one draw needn't show every extreme that they name: `expert_choices`: each row names 8 different experts. Within the 256 tokens of one sequence no expert is named more than 116 times, a bound that some block reaches. `segment_ids`: within a sequence the numbers never fall; a document is a run of equal numbers of at most 192 tokens, one of them exactly 192.
All inputs are finite; a program needn't handle non-finite values.
Results may differ from the reference program's by a relative error of at most 0.02.
Values may be sent and summed in bfloat16 or wider, within the bound.
No kernel may reach another device: no remote copies, remote signals or barrier semaphores. Data moves between devices by JAX's collectives and lax.ppermute only.
A program may use at most 192 MiB of HBM per device.

```python
import math
import jax
import jax.numpy as jnp
import numpy as np
from jax import lax

D = 1536
HEADS = 24
KV_HEADS = 8
HEAD_DIM = 64
FF = 512
TOP = 8
TOK_DEV = 256
DOCS = 4
DOC_MOST = 192
SEQS = 32
TOKENS = 8192
EXPERTS = 20
CAP = 116


def spiked(values, own_key, source, target, blocks, factor):
    def block_of(dim):
        return (jnp.arange(values.shape[dim]) // (values.shape[dim] // blocks)).reshape((-1,) + (1,) * (values.ndim - 1 - dim))

    first = jax.random.permutation(own_key, blocks)[block_of(target)]
    other_side = (block_of(target) + blocks // 2) % blocks
    return jnp.where((block_of(source) == first) | (block_of(source) == other_side), factor * values, values)


def shard_levels(rng, extent, split, low, high):
    level = 1.0
    for dim, blocks in split:
        steps = jax.random.uniform(jax.random.fold_in(jax.random.fold_in(rng, 6), dim), (blocks,), jnp.float32, low / len(split), high / len(split))
        level = level * jnp.repeat(jnp.exp(steps), extent[dim] // blocks).reshape((-1,) + (1,) * (len(extent) - 1 - dim))
    return level


def split_up(amount, total, limit, slope):
    loads = [(1 << 20) // math.isqrt(standing ** slope) + 1 for standing in range(2, amount + 1)]
    spare, counts = total - limit - (amount - 1), [1] * (amount - 1)
    while spare > 0:
        movable = [i for i in range(amount - 1) if counts[i] < limit]
        pool, left = sum([loads[i] for i in movable]), spare
        for i in movable:
            extra = min(limit - counts[i], max(1, left * loads[i] // pool), spare)
            counts[i] = counts[i] + extra
            spare = spare - extra
    return np.array([limit] + counts)


def uneven(stream_key, amount, total, most, lean):
    if amount == 2:
        one = jax.random.randint(stream_key, (), max(1, total - most), min(most, total - 1) + 1)
        return jnp.stack([one, total - one])
    tallies = jnp.asarray(split_up(amount, total, most, lean), jnp.int32)
    twos = (amount - 1) // 2
    giver, sink = tallies[1:1 + 2 * twos:2], tallies[2:2 + 2 * twos:2]
    slack = jnp.minimum(giver - 1, most - sink)
    moved = jax.random.randint(jax.random.fold_in(stream_key, 1), (twos,), 0, 1 << 20) % (slack + 1)
    tallies = tallies.at[1:1 + 2 * twos:2].set(giver - moved).at[2:2 + 2 * twos:2].set(sink + moved)
    return tallies[jax.random.permutation(jax.random.fold_in(stream_key, 2), amount)]


def deal_out(rng, own, number, rows, count, top, limit, skew):
    sequence = jax.random.permutation(rng, count)
    crowded, common = shares(count, rows * top, limit, skew, True), shares(count, rows * top, limit, skew, False)
    places = jnp.arange(count)

    def named(lengths, offset_by):
        used = int((lengths > 0).sum())
        fixed = max(1, used // 4)
        passed = fixed + (places - fixed + offset_by * (used - fixed)) % max(1, count - fixed)
        return jnp.zeros((count,), jnp.int32).at[sequence[jnp.where(places < fixed, places, passed)]].set(jnp.asarray(lengths, jnp.int32))

    lengths = jnp.where(number % 4 == 0, named(crowded, number // 4), named(common, number - number // 4 - 1))
    mixed = jax.random.permutation(jax.random.fold_in(own, 3), count)
    donor, receiver = mixed[0:count // 2 * 2:2], mixed[1:count // 2 * 2:2]
    margin = jnp.minimum(lengths[donor] - 1, limit - lengths[receiver]) // 2
    margin = jnp.where((donor == sequence[0]) | (receiver == sequence[0]) | (lengths[receiver] == 0), 0, jnp.maximum(margin, 0))
    passed = jax.random.randint(jax.random.fold_in(own, 4), (count // 2,), 0, 1 << 20) % (margin + 1)
    lengths = lengths.at[donor].add(-passed).at[receiver].add(passed)
    items = jnp.searchsorted(jnp.cumsum(lengths), jnp.arange(rows * top), side="right").astype(jnp.int32)
    table = items.reshape(top, rows).T
    table = table[jax.random.permutation(jax.random.fold_in(own, 1), rows)]
    offset_by = jax.random.randint(jax.random.fold_in(own, 2), (rows, 1), 0, top)
    return jnp.take_along_axis(table, (jnp.arange(top)[None, :] + offset_by) % top, axis=1)


def shares(number_of, total, limit, slope, full):
    portions = [(1 << 20) // math.isqrt(rank ** slope) + 1 for rank in range(1, number_of + 1)]
    largest = limit if full else min(limit, max(-(-total // number_of), total * portions[0] // sum(portions)))
    least = 1 if total - largest >= number_of - 1 else 0
    given, surplus = [largest] + [least] * (number_of - 1), total - largest - least * (number_of - 1)
    while surplus > 0:
        candidates = [i for i in range(1, number_of) if given[i] < largest] or [i for i in range(1, number_of) if given[i] < limit]
        mass, remaining = sum([portions[i] for i in candidates]), surplus
        for i in candidates:
            addition = min(limit - given[i], max(1, remaining * portions[i] // mass), surplus)
            given[i] = given[i] + addition
            surplus = surplus - addition
    return np.array(given)


def scatter_about(key, extent, spread, bound, cuts=(), held_as=jnp.bfloat16):
    level = shard_levels(key, extent, cuts, -0.22, 0.18) if cuts else 1.0
    entries = jax.random.normal(key, extent, jnp.float32) * spread * level
    return jnp.minimum(jnp.maximum(entries, -bound), bound).astype(held_as)


def heavy_noise(stream_key, dims, deviation, limit, shards, heavy, kind=jnp.bfloat16):
    values = deviation * jax.random.normal(stream_key, dims, jnp.float32)
    if shards:
        values = values * shard_levels(stream_key, dims, shards, -0.22, 0.18)
    return jnp.clip(spiked(values, jax.random.fold_in(stream_key, 3), *heavy), -limit, limit).astype(kind)


def setup_inputs(seed: int = 0) -> dict:
    splits = jax.random.split(jax.random.key(seed), 15)
    tokens = heavy_noise(splits[0], (TOKENS, D), 1.0, 6.0, ((0, 32),), (0, 1, 32, 2.75))
    segment_ids = jax.vmap(lambda own: jnp.searchsorted(jnp.cumsum(uneven(own, DOCS, TOK_DEV, DOC_MOST, 1)), jnp.arange(TOK_DEV), side="right"))(jax.random.split(splits[1], SEQS)).reshape((SEQS, TOK_DEV)).astype(jnp.int32)
    expert_choices_keys = jax.random.split(jax.random.fold_in(splits[2], 1), TOKENS // TOK_DEV)
    expert_choices_turns = jax.random.permutation(jax.random.fold_in(splits[2], 3), TOKENS // TOK_DEV)
    expert_choices = jax.vmap(lambda own, number: deal_out(jax.random.fold_in(splits[2], 2), own, number, TOK_DEV, EXPERTS, TOP, CAP, 1))(expert_choices_keys, expert_choices_turns).reshape((TOKENS, TOP))
    attn_gain = jnp.clip(1.0 + 0.18 * jax.random.normal(splits[3], (D,), jnp.float32), 0.099609375, 1.8984375).astype(jnp.bfloat16)
    query_weight = scatter_about(splits[4], (D, HEADS * HEAD_DIM), D ** -0.5, 0.15625, ((0, 8),))
    key_weight = scatter_about(splits[5], (D, KV_HEADS * HEAD_DIM), D ** -0.5, 0.15625, ((0, 8),))
    value_weight = scatter_about(splits[6], (D, KV_HEADS * HEAD_DIM), D ** -0.5, 0.15625, ((0, 8),))
    output_weight = scatter_about(splits[7], (HEADS * HEAD_DIM, D), (HEADS * HEAD_DIM // 16) ** -0.5, 0.625, ((0, 8),))
    ffn_gain = jnp.clip(1.0 + 0.18 * jax.random.normal(splits[8], (D,), jnp.float32), 0.099609375, 1.8984375).astype(jnp.bfloat16)
    router_weight = scatter_about(splits[9], (D, EXPERTS), (4 * D) ** -0.5, 0.078125, ((0, 8),))
    expert_gate = scatter_about(splits[10], (EXPERTS, D, FF), D ** -0.5, 0.15625, ((0, 4), (1, 8)))
    expert_up = scatter_about(splits[11], (EXPERTS, D, FF), D ** -0.5, 0.15625, ((0, 4), (1, 8)))
    expert_down = scatter_about(splits[12], (EXPERTS, FF, D), (FF // 32) ** -0.5, 1.5, ((0, 4), (2, 8)))
    cotangent = scatter_about(splits[13], (TOKENS, D), 1.0, 6.0, ((0, 32),))
    return {"tokens": tokens, "segment_ids": segment_ids, "expert_choices": expert_choices, "attn_gain": attn_gain, "query_weight": query_weight, "key_weight": key_weight, "value_weight": value_weight, "output_weight": output_weight, "ffn_gain": ffn_gain, "router_weight": router_weight, "expert_gate": expert_gate, "expert_up": expert_up, "expert_down": expert_down, "cotangent": cotangent}


@jax.custom_vjp
def low(v):
    return lax.optimization_barrier(v.astype(jnp.bfloat16)).astype(jnp.float32)

@jax.custom_vjp
def low_back(v):
    return v

def low_keep(v):
    return (low(v), None)

def low_pass(kept, grad):
    return (grad,)

def back_keep(v):
    return (v, None)

def back_low(kept, grad):
    return (low(grad),)
low.defvjp(low_keep, low_pass)
low_back.defvjp(back_keep, back_low)
HIGHEST = lax.Precision.HIGHEST
norm_eps = 1e-06

def product(left, right):
    return jnp.matmul(left, right, precision=HIGHEST)

def rms_scale(values, gain):
    factor = lax.rsqrt(lax.optimization_barrier(jnp.mean(values * values, axis=-1, keepdims=True)) + norm_eps)
    return values * factor * gain

def softmax_rows(scores):
    top_score = lax.optimization_barrier(jnp.max(scores, axis=-1, keepdims=True))
    shifted = jnp.exp(scores - top_score)
    return shifted / lax.optimization_barrier(jnp.sum(shifted, axis=-1, keepdims=True))

def attend(pieces):
    queries, key_rows, value_rows, doc_ids = pieces
    scores = jnp.einsum('bqkgd,btkd->bkgqt', queries, key_rows, precision=HIGHEST) * HEAD_DIM ** (-0.5)
    scores = low_back(scores)
    positions = jnp.arange(TOK_DEV, dtype=jnp.int32)
    allowed = (doc_ids[:, :, None] == doc_ids[:, None, :]) & (positions[None, :, None] >= positions[None, None, :])
    scores = jnp.where(allowed[:, None, None, :, :], scores, -1e+30)
    weights = softmax_rows(scores)
    context = jnp.einsum('bkgqt,btkd->bqkgd', low(weights), value_rows, precision=HIGHEST)
    return low_back(low(context))

def reference(tokens, segment_ids, expert_choices, attn_gain, query_weight, key_weight, value_weight, output_weight, ffn_gain, router_weight, expert_gate, expert_up, expert_down, cotangent):
    groups = HEADS // KV_HEADS
    bunch_size = math.gcd(SEQS, max(1, 4096 // TOK_DEV))
    rounds = SEQS // bunch_size
    flat_experts = expert_choices.reshape(SEQS, TOK_DEV * TOP).astype(jnp.int32)
    expert_ids = jnp.arange(EXPERTS, dtype=jnp.int32)
    pair_hot = (flat_experts[:, :, None] == expert_ids[None, None, :]).astype(jnp.int32)
    earlier = jnp.cumsum(pair_hot, axis=1) - pair_hot
    slot_idx = lax.optimization_barrier(jnp.sum(earlier * pair_hot, axis=2)).astype(jnp.int32)
    row_idx = (jnp.arange(SEQS, dtype=jnp.int32)[:, None] * CAP + slot_idx).reshape(-1).astype(jnp.int32)
    token_idx = jnp.arange(TOKENS * TOP, dtype=jnp.int32) // TOP
    pair_expert = flat_experts.reshape(-1)
    slot_table = jnp.full((EXPERTS, SEQS * CAP), TOKENS, dtype=jnp.int32).at[pair_expert, row_idx].set(token_idx)
    choice_hot = expert_choices[:, :, None] == expert_ids[None, None, :]
    doc_ids = segment_ids.reshape(rounds, bunch_size, TOK_DEV)

    def layer(inputs, gain_one, w_query, w_key, w_value, w_output, gain_two, w_router, w_gate, w_up, w_down):
        normed_one = low(rms_scale(inputs, gain_one))
        queries = low_back(low(product(normed_one, w_query)))
        key_rows = low_back(low(product(normed_one, w_key)))
        value_rows = low_back(low(product(normed_one, w_value)))
        shaped_q = queries.reshape(rounds, bunch_size, TOK_DEV, KV_HEADS, groups, HEAD_DIM)
        shaped_k = key_rows.reshape(rounds, bunch_size, TOK_DEV, KV_HEADS, HEAD_DIM)
        shaped_v = value_rows.reshape(rounds, bunch_size, TOK_DEV, KV_HEADS, HEAD_DIM)
        context = lax.map(jax.checkpoint(attend), (shaped_q, shaped_k, shaped_v, doc_ids))
        context = context.reshape(TOKENS, HEADS * HEAD_DIM)
        mixed_one = inputs + low_back(product(context, w_output))
        normed_two = low(rms_scale(mixed_one, gain_two))
        logits = low_back(product(normed_two, w_router))
        chosen = lax.optimization_barrier(jnp.sum(jnp.where(choice_hot, logits[:, None, :], 0.0), axis=2))
        gate_probs = softmax_rows(chosen)

        def expert_step(carried, pieces):
            rows_of, gate_w, up_w, down_w = pieces
            present = rows_of < TOKENS
            picked = jnp.minimum(rows_of, TOKENS - 1)
            row_block = low_back(jnp.where(present[:, None], normed_two[picked], 0.0))
            gate_pre = low_back(product(row_block, gate_w))
            up_pre = low_back(product(row_block, up_w))
            hidden = low(gate_pre * jax.nn.sigmoid(gate_pre) * up_pre)
            return (carried, low_back(low(product(hidden, down_w))))
        carry_zero = jnp.zeros((), jnp.float32)
        unused, outputs = lax.scan(jax.checkpoint(expert_step), carry_zero, (slot_table, w_gate, w_up, w_down))
        returned = outputs[pair_expert, row_idx].reshape(TOKENS, TOP, D)
        combined = jnp.einsum('tc,tcd->td', gate_probs, returned, precision=HIGHEST)
        return mixed_one + combined
    result, pullback = jax.vjp(layer, tokens.astype(jnp.float32), attn_gain.astype(jnp.float32), query_weight.astype(jnp.float32), key_weight.astype(jnp.float32), value_weight.astype(jnp.float32), output_weight.astype(jnp.float32), ffn_gain.astype(jnp.float32), router_weight.astype(jnp.float32), expert_gate.astype(jnp.float32), expert_up.astype(jnp.float32), expert_down.astype(jnp.float32))
    grad_tok, grad_g1, grad_q, grad_k, grad_v, grad_o, grad_g2, grad_r, grad_eg, grad_eu, grad_ed = pullback(cotangent.astype(jnp.float32))
    return (result.astype(jnp.bfloat16), grad_tok, grad_g1, grad_q, grad_k, grad_v, grad_o, grad_g2, grad_r, grad_eg, grad_eu, grad_ed)
```

```python
import functools

import jax
import jax.numpy as jnp
from jax import lax
from jax.experimental import pallas as pl
from jax.experimental.pallas import tpu as pltpu
from jax.sharding import PartitionSpec as P

HEADS = 24
KV_HEADS = 8
HEAD_DIM = 64
TOP = 8
GROUPS = HEADS // KV_HEADS
QW = HEADS * HEAD_DIM
KW = KV_HEADS * HEAD_DIM
QKV = QW + 2 * KW
EXT = 128
HALVES = 2

norm_eps = 1e-06
masked_score = -1e30
BF = jnp.bfloat16
F32 = jnp.float32
ANY = pl.BlockSpec(memory_space=pl.ANY)
VMEM = pl.BlockSpec(memory_space=pltpu.VMEM)
SMEM = pl.BlockSpec(memory_space=pltpu.SMEM)
VMEM_LIMIT = 56 * 1024 * 1024


def dot(a, b, ca=1, cb=0):
    return lax.dot_general(a, b, (((ca,), (cb,)), ((), ())), preferred_element_type=F32)


def params():
    return pltpu.CompilerParams(vmem_limit_bytes=VMEM_LIMIT)


def cost(flops, nbytes, trans=0):
    return pl.CostEstimate(flops=int(flops), bytes_accessed=int(nbytes), transcendentals=int(trans))


def sds(shape, dtype):
    return jax.ShapeDtypeStruct(shape, dtype)


def swap(value, bit, size):
    return lax.ppermute(value, "dp", [(i, i ^ bit) for i in range(size)])


def gather_shards(shard, route, size):
    if size != 8:
        return [lax.all_gather(shard, "dp", axis=0, tiled=False)]
    across = swap(shard, 2, size)
    along = swap(shard, 4, size)
    corner = swap(across, 4, size) if route == 0 else swap(along, 2, size)
    found = {0: shard, 2: across, 4: along, 6: corner}
    for near in (0, 2, 4, 6):
        found[near + 1] = swap(found[near], 1, size)
    return [found[m] for m in range(8)]


def reduce_shards(parts, route, size):
    if size != 8:
        total = lax.psum_scatter(parts[0], "dp", scatter_dimension=0, tiled=True)
        return total[0].astype(F32)

    def add(a, b):
        return (a.astype(F32) + b.astype(F32)).astype(BF)

    own, other = parts
    other = swap(other, 1, size)
    if route == 0:
        sent = swap(add(own[1::2], other[1::2]), 2, size)
        kept = add(own[0::2], other[0::2])
        last = swap(add(kept[1], sent[1]), 4, size)
    else:
        sent = swap(add(own[2:], other[2:]), 4, size)
        kept = add(own[:2], other[:2])
        last = swap(add(kept[1], sent[1]), 2, size)
    return kept[0].astype(F32) + sent[0].astype(F32) + last.astype(F32)


def part_shapes(size, shape):
    if size != 8:
        return [sds((size,) + shape, BF)]
    return [sds((4,) + shape, BF), sds((4,) + shape, BF)]


def send_along(value, step):
    count = lax.axis_size("expert")
    return lax.ppermute(value, "expert", [(i, (i + step) % count) for i in range(count)])


def fetch(me, refs, target, sems, rows, size):
    copies = []
    for i in range(size):
        if len(refs) == 1:
            source, at = refs[0].at[i], i * rows
        else:
            source, at = refs[i], pl.multiple_of(jnp.bitwise_xor(me, i) * rows, rows)
        copies.append(pltpu.make_async_copy(source, target(pl.ds(at, rows)), sems.at[i]))
    for c in copies:
        c.start()
    return copies


def store_parts(me, source, outs, sems, rows, size):
    copies = []
    for i in range(size):
        if len(outs) == 1:
            target, at = outs[0].at[i], i * rows
        else:
            target = outs[i % 2].at[i // 2]
            at = pl.multiple_of(jnp.bitwise_xor(me, i) * rows, rows)
        copies.append(pltpu.make_async_copy(source(pl.ds(at, rows)), target, sems.at[i]))
    for c in copies:
        c.start()
    return copies


def attention_kernel(size, rows, me, tok, seg_row, seg_col, *rest):
    count = 1 if size != 8 else size
    refs, rest = rest[:count], rest[count:]
    low_out, qkv_out, ctx_out, prob_out, ext_out, w, sems = rest
    copies = fetch(me[0], refs, lambda s: w.at[s], sems, rows, size)
    seq = tok.shape[0]
    x = tok[...].astype(F32)
    factor = lax.rsqrt(jnp.mean(x * x, axis=-1, keepdims=True) + norm_eps)
    normed = x * factor
    same = seg_col[...] == seg_row[...]
    key_at = lax.broadcasted_iota(jnp.int32, (seq, seq), 0)
    query_at = lax.broadcasted_iota(jnp.int32, (seq, seq), 1)
    allowed = jnp.where(same & (key_at <= query_at), 0.0, masked_score)
    allowed = jnp.concatenate([allowed] * GROUPS, axis=1)
    for c in copies:
        c.wait()
    ext = w[:, QKV:].astype(F32).T[: ext_out.shape[0], :]
    ext_out[...] = ext
    experts_pad = ext_out.shape[0] - 16
    gain = ext[experts_pad : experts_pad + 1, :]
    low = (normed * gain).astype(BF)
    low_out[...] = low
    step = 512
    for j in range(QKV // step):
        part = dot(low, w[:, j * step : (j + 1) * step])
        qkv_out[j * step : (j + 1) * step, :] = part.T.astype(BF)
    for h in range(KV_HEADS):
        q = jnp.concatenate(
            [
                qkv_out[(GROUPS * h + g) * HEAD_DIM : (GROUPS * h + g + 1) * HEAD_DIM, :]
                for g in range(GROUPS)
            ],
            axis=1,
        )
        k = qkv_out[QW + h * HEAD_DIM : QW + (h + 1) * HEAD_DIM, :]
        v = qkv_out[QW + KW + h * HEAD_DIM : QW + KW + (h + 1) * HEAD_DIM, :]
        scores = dot(k, q, 0, 0) * HEAD_DIM ** (-0.5)
        scores = jnp.where(allowed < 0.0, masked_score, scores)
        top = jnp.max(scores, axis=0, keepdims=True)
        shifted = jnp.exp(scores - top)
        probs = (shifted * (1.0 / jnp.sum(shifted, axis=0, keepdims=True))).astype(BF)
        prob_out[h] = probs
        ctx = dot(v, probs).astype(BF)
        for g in range(GROUPS):
            at = (GROUPS * h + g) * HEAD_DIM
            ctx_out[at : at + HEAD_DIM, :] = ctx[:, g * seq : (g + 1) * seq]


def run_attention(me, tokens, seg_row, seg_col, pieces, size, ext_rows):
    seq, width = tokens.shape
    rows = width // size
    cols = QKV + EXT
    return pl.pallas_call(
        functools.partial(attention_kernel, size, rows),
        name="attention",
        out_shape=[
            sds((seq, width), BF),
            sds((QKV, seq), BF),
            sds((QW, seq), BF),
            sds((KV_HEADS, seq, GROUPS * seq), BF),
            sds((ext_rows, width), F32),
        ],
        in_specs=[SMEM, VMEM, VMEM, VMEM] + [ANY] * len(pieces),
        out_specs=[VMEM] * 5,
        scratch_shapes=[pltpu.VMEM((width, cols), BF), pltpu.SemaphoreType.DMA((size,))],
        compiler_params=params(),
        cost_estimate=cost(4e9, 16e6, 2e6),
    )(me, tokens, seg_row, seg_col, *pieces)


def residual_kernel(size, rows, me, tok, ctx, ext, *rest):
    count = 1 if size != 8 else size
    refs, rest = rest[:count], rest[count:]
    res_out, low_out, w, sems = rest
    copies = fetch(me[0], refs, lambda s: w.at[s], sems, rows, size)
    experts_pad = ext.shape[0] - 16
    for c in copies:
        c.wait()
    res = tok[...].astype(F32) + dot(ctx[...], w[...], 0, 0)
    res_out[...] = res
    factor = lax.rsqrt(jnp.mean(res * res, axis=-1, keepdims=True) + norm_eps)
    low_out[...] = (res * factor * ext[experts_pad + 8 : experts_pad + 9, :]).astype(BF)


def run_residual(me, tokens, ctx, ext, pieces, size):
    seq, width = tokens.shape
    rows = QW // size
    return pl.pallas_call(
        functools.partial(residual_kernel, size, rows),
        name="residual",
        out_shape=[sds((seq, width), F32), sds((seq, width), BF)],
        in_specs=[SMEM, VMEM, VMEM, VMEM] + [ANY] * len(pieces),
        out_specs=[VMEM] * 2,
        scratch_shapes=[pltpu.VMEM((QW, width), BF), pltpu.SemaphoreType.DMA((size,))],
        compiler_params=params(),
        cost_estimate=cost(1.2e9, 8e6),
    )(me, tokens, ctx, ext, *pieces)


def router_kernel(owners, per, z, ext, *rest):
    rows, rest = rest[:owners], rest[owners:]
    pos, rest = rest[:owners], rest[owners:]
    pos_out, p_out, own_out, gather_p, gather_pos = rest
    experts_pad = ext.shape[0] - 16
    router = ext[:experts_pad, :].astype(BF)
    at = z[0] * per
    for r in range(owners):
        logits = dot(router, rows[r][...], 1, 1)
        place = pos[r][...]
        named = place >= 0.0
        logits = jnp.where(named, logits, masked_score)
        top = jnp.max(logits, axis=0, keepdims=True)
        shifted = jnp.where(named, jnp.exp(logits - top), 0.0)
        probs = shifted / jnp.sum(shifted, axis=0, keepdims=True)
        if r == 0:
            own_out[...] = probs
        gather_p[...] = probs
        gather_pos[...] = place
        for l in range(per):
            p_out[l, r : r + 1, :] = gather_p[pl.ds(at + l, 1), :]
            pos_out[l, r : r + 1, :] = gather_pos[pl.ds(at + l, 1), :].astype(jnp.int32)


def run_router(z, ext, rows, pos, per):
    owners = len(rows)
    seq = rows[0].shape[0]
    experts_pad = ext.shape[0] - 16
    return pl.pallas_call(
        functools.partial(router_kernel, owners, per),
        name="router",
        out_shape=[
            sds((per, owners, seq), jnp.int32),
            sds((per, owners, seq), F32),
            sds((experts_pad, seq), F32),
        ],
        in_specs=[SMEM, VMEM] + [VMEM] * (2 * owners),
        out_specs=[VMEM] * 3,
        scratch_shapes=[pltpu.VMEM((experts_pad, seq), F32)] * 2,
        compiler_params=params(),
        cost_estimate=cost(1e8, 4e6),
    )(z, ext, *rows, *pos)


def expert_kernel(size, rows, owners, cap, number, me, pos, p, *rest):
    count = 1 if size != 8 else size
    outs_count = 1 if size != 8 else 2
    xs, rest = rest[:owners], rest[owners:]
    cs, rest = rest[:owners], rest[owners:]
    refs, rest = rest[:count], rest[count:]
    out_rows, back_rows, gate_out = rest[:3]
    rest = rest[3:]
    grads, rest = rest[:outs_count], rest[outs_count:]
    xv, cv, w, xr, cr, prow, hp, gg, ug, gate, ov, bv, g, sem_x, sem_c, sem_w, sem_o = rest
    ff = w.shape[2]
    copies_x = [pltpu.make_async_copy(xs[r], xv.at[r], sem_x.at[r]) for r in range(owners)]
    copies_c = [pltpu.make_async_copy(cs[r], cv.at[r], sem_c.at[r]) for r in range(owners)]
    for a, b in zip(copies_x, copies_c):
        a.start()
        b.start()
    copies_w = fetch(me[0], refs, lambda s: w.at[:, s, :], sem_w, rows, size)
    seq = xv.shape[1]
    slot = lax.broadcasted_iota(jnp.int32, (cap, seq), 0)
    for r in range(owners):
        copies_x[r].wait()
        copies_c[r].wait()
        hot = pos[number, r : r + 1, :] == slot
        low_hot = jnp.where(hot, 1.0, 0.0).astype(BF)
        at = pl.ds(r * cap, cap)
        xr[at, :] = dot(low_hot, xv[r]).astype(BF)
        cr[at, :] = dot(low_hot, cv[r]).astype(BF)
        prow[at, :] = jnp.sum(jnp.where(hot, p[number, r : r + 1, :], 0.0), axis=1, keepdims=True)
    for c in copies_w:
        c.wait()
    step = ff // HALVES
    gate[...] = jnp.zeros_like(gate)
    for j in range(HALVES):
        cols = slice(j * step, (j + 1) * step)
        gate_pre = dot(xr[...], w[0, :, cols])
        up_pre = dot(xr[...], w[1, :, cols])
        back = dot(cr[...], w[2, :, cols])
        probs = prow[...]
        s = jax.nn.sigmoid(gate_pre)
        silu = gate_pre * s
        hidden = silu * up_pre
        gate[...] += jnp.sum(hidden * back, axis=1, keepdims=True)
        hp[:, cols] = (hidden * probs).astype(BF)
        back = back * probs
        gg[:, cols] = (back * up_pre * (s + silu * (1.0 - s))).astype(BF)
        ug[:, cols] = (back * silu).astype(BF)
    for r in range(owners):
        hot = pos[number, r : r + 1, :] == slot
        at = pl.ds(r * cap, cap)
        gate_out[r : r + 1, :] = jnp.sum(jnp.where(hot, gate[at, :], 0.0), axis=0, keepdims=True)
    width = w.shape[1]
    tile = width // HALVES
    for j in range(HALVES):
        cols = slice(j * tile, (j + 1) * tile)
        g[0, cols, :] = dot(xr[:, cols], gg[...], 0, 0).astype(BF)
        g[1, cols, :] = dot(xr[:, cols], ug[...], 0, 0).astype(BF)
        g[2, cols, :] = dot(cr[:, cols], hp[...], 0, 0).astype(BF)
    copies_g = store_parts(me[0], lambda s: g.at[:, s, :], grads, sem_w, rows, size)
    for j in range(HALVES):
        cols = slice(j * tile, (j + 1) * tile)
        bv[:, cols] = (dot(gg[...], w[0, cols, :], 1, 1) + dot(ug[...], w[1, cols, :], 1, 1)).astype(BF)
    copy_b = pltpu.make_async_copy(bv, back_rows, sem_o.at[0])
    copy_b.start()
    for j in range(HALVES):
        cols = slice(j * tile, (j + 1) * tile)
        ov[:, cols] = dot(hp[...], w[2, cols, :], 1, 1).astype(BF)
    copy_o = pltpu.make_async_copy(ov, out_rows, sem_o.at[1])
    copy_o.start()
    for c in copies_g + [copy_b, copy_o]:
        c.wait()


def run_expert(me, pos, p, xs, cs, pieces, size, number, cap):
    owners = len(xs)
    seq, width = xs[0].shape
    ff = pieces[0].shape[-1]
    rows = width // size
    total = owners * cap
    grads = part_shapes(size, (3, rows, ff))
    return pl.pallas_call(
        functools.partial(expert_kernel, size, rows, owners, cap, number),
        name="expert",
        out_shape=[sds((total, width), BF), sds((total, width), BF), sds((owners, seq), F32)] + grads,
        in_specs=[SMEM, VMEM, VMEM] + [ANY] * (2 * owners + len(pieces)),
        out_specs=[ANY, ANY, VMEM] + [ANY] * len(grads),
        scratch_shapes=[
            pltpu.VMEM((owners, seq, width), BF),
            pltpu.VMEM((owners, seq, width), BF),
            pltpu.VMEM((3, width, ff), BF),
            pltpu.VMEM((total, width), BF),
            pltpu.VMEM((total, width), BF),
            pltpu.VMEM((total, 1), F32),
            pltpu.VMEM((total, ff), BF),
            pltpu.VMEM((total, ff), BF),
            pltpu.VMEM((total, ff), BF),
            pltpu.VMEM((total, 1), F32),
            pltpu.VMEM((total, width), BF),
            pltpu.VMEM((total, width), BF),
            pltpu.VMEM((3, width, ff), BF),
            pltpu.SemaphoreType.DMA((owners,)),
            pltpu.SemaphoreType.DMA((owners,)),
            pltpu.SemaphoreType.DMA((size,)),
            pltpu.SemaphoreType.DMA((2,)),
        ],
        compiler_params=params(),
        cost_estimate=cost(9e9, 20e6, 3e5),
    )(me, pos, p, *xs, *cs, *pieces)


def combine_kernel(owners, per, cap, pos, *rest):
    rows, rest = rest[:per], rest[per:]
    gates, outs = rest[: len(rest) - 2 * owners], rest[len(rest) - 2 * owners :]
    if not gates:
        gates, outs = (), rest
    r = pl.program_id(0)
    seq = pos.shape[2]
    slot = lax.broadcasted_iota(jnp.int32, (cap, seq), 0)
    hot = jnp.concatenate(
        [jnp.where(pos[l, pl.ds(r, 1), :] == slot, 1.0, 0.0).astype(BF) for l in range(per)], axis=0
    )
    stacked = jnp.concatenate([rows[l][...] for l in range(per)], axis=0)
    total = dot(hot, stacked, 0, 0).astype(BF)
    for o in range(owners):

        @pl.when(r == o)
        def _():
            outs[o][...] = total
            if gates:
                for l in range(per):
                    outs[owners + o][l : l + 1, :] = gates[l][o : o + 1, :]


def run_combine(pos, rows, gates, cap):
    per, owners, seq = pos.shape
    width = rows[0].shape[1]
    gate_rows = -(-per // 8) * 8
    shapes = [sds((seq, width), BF)] * owners
    if gates:
        shapes = shapes + [sds((gate_rows, seq), F32)] * owners

    def whole(shape):
        return pl.BlockSpec(shape, lambda r: (0,) * len(shape))

    return pl.pallas_call(
        functools.partial(combine_kernel, owners, per, cap),
        name="combine",
        grid=(owners,),
        out_shape=shapes,
        in_specs=[whole(pos.shape)]
        + [pl.BlockSpec((cap, width), lambda r: (r, 0))] * per
        + [whole((owners, seq))] * len(gates),
        out_specs=[whole(s.shape) for s in shapes],
        compiler_params=params(),
        cost_estimate=cost(2e9, 12e6),
    )(pos, *rows, *gates)


def second_kernel(size, rows, owners, per, me, z, own_p, ext, low_two, res, cot, ctx, *rest):
    backs, rest = rest[:owners], rest[owners:]
    gates, rest = rest[:owners], rest[owners:]
    count = 1 if size != 8 else size
    outs_count = 1 if size != 8 else 2
    refs, rest = rest[:count], rest[count:]
    res_grad, ctx_grad, ext_grad = rest[:3]
    rest = rest[3:]
    grads, rest = rest[:outs_count], rest[outs_count:]
    w, g, gate, sems, sems_g = rest
    copies = fetch(me[0], refs, lambda s: w.at[s], sems, rows, size)
    experts_pad = own_p.shape[0]
    gate[...] = jnp.zeros_like(gate)
    for r in range(owners):
        at = lax.rem(z[0] + r, owners) * per
        for l in range(per):
            gate[pl.ds(at + l, 1), :] = gates[r][l : l + 1, :]
    p = own_p[...]
    gate_grad = gate[...]
    weighted = jnp.sum(p * gate_grad, axis=0, keepdims=True)
    logit_grad = (p * (gate_grad - weighted)).astype(BF)
    router = ext[:experts_pad, :].astype(BF)
    ext_grad[:experts_pad, :] = dot(logit_grad, low_two[...])
    two = dot(logit_grad, router, 0, 0)
    for r in range(owners):
        two = two + backs[r][...].astype(F32)
    values = res[...]
    factor = lax.rsqrt(jnp.mean(values * values, axis=-1, keepdims=True) + norm_eps)
    normed = values * factor
    ext_grad[experts_pad:, :] = jnp.broadcast_to(
        jnp.sum(two * normed, axis=0, keepdims=True), (16, normed.shape[1])
    )
    scaled = two * ext[experts_pad + 8 : experts_pad + 9, :]
    inward = factor * (scaled - normed * jnp.mean(scaled * normed, axis=-1, keepdims=True))
    total = cot[...].astype(F32) + inward
    res_grad[...] = total
    low = total.astype(BF)
    step = QW // 4
    for j in range(4):
        at = slice(j * step, (j + 1) * step)
        g[at, :] = dot(ctx[at, :], low).astype(BF)
    copies_g = store_parts(me[0], lambda s: g.at[s], grads, sems_g, rows, size)
    for c in copies:
        c.wait()
    for j in range(4):
        at = slice(j * step, (j + 1) * step)
        ctx_grad[at, :] = dot(w[at, :], low, 1, 1).astype(BF)
    for c in copies_g:
        c.wait()


def run_second(me, z, own_p, ext, low_two, res, cot, ctx, backs, gates, pieces, size, per):
    seq, width = res.shape
    rows = QW // size
    grads = part_shapes(size, (rows, width))
    experts_pad = own_p.shape[0]
    return pl.pallas_call(
        functools.partial(second_kernel, size, rows, len(backs), per),
        name="second_back",
        out_shape=[sds((seq, width), F32), sds((QW, seq), BF), sds((experts_pad + 16, width), F32)] + grads,
        in_specs=[SMEM, SMEM] + [VMEM] * (6 + 2 * len(backs)) + [ANY] * len(pieces),
        out_specs=[VMEM] * 3 + [ANY] * len(grads),
        scratch_shapes=[
            pltpu.VMEM((QW, width), BF),
            pltpu.VMEM((QW, width), BF),
            pltpu.VMEM((experts_pad, seq), F32),
            pltpu.SemaphoreType.DMA((size,)),
            pltpu.SemaphoreType.DMA((size,)),
        ],
        compiler_params=params(),
        cost_estimate=cost(2.4e9, 20e6),
    )(me, z, own_p, ext, low_two, res, cot, ctx, *backs, *gates, *pieces)


def first_kernel(size, rows, me, ctx_grad, qkv, probs, low_one, tok, ext, ext_grad, res_grad, *rest):
    count = 1 if size != 8 else size
    outs_count = 1 if size != 8 else 2
    refs, rest = rest[:count], rest[count:]
    tok_grad, rest = rest[0], rest[1:]
    grads, rest = rest[:outs_count], rest[outs_count:]
    w, g, back, back_rows, sems, sems_g = rest
    copies = fetch(me[0], refs, lambda s: w.at[s], sems, rows, size)
    seq = tok.shape[0]
    scale = HEAD_DIM ** (-0.5)
    for h in range(KV_HEADS):

        def heads(ref):
            return jnp.concatenate(
                [
                    ref[(GROUPS * h + i) * HEAD_DIM : (GROUPS * h + i + 1) * HEAD_DIM, :]
                    for i in range(GROUPS)
                ],
                axis=1,
            )

        upstream = heads(ctx_grad)
        q = heads(qkv)
        k = qkv[QW + h * HEAD_DIM : QW + (h + 1) * HEAD_DIM, :]
        v = qkv[QW + KW + h * HEAD_DIM : QW + KW + (h + 1) * HEAD_DIM, :]
        low_p = probs[h]
        weights = low_p.astype(F32)
        prob_grad = dot(v, upstream, 0, 0)
        inner = jnp.sum(prob_grad * weights, axis=0, keepdims=True)
        score_grad = (weights * (prob_grad - inner)).astype(BF)
        value_grad = dot(upstream, low_p, 1, 1)
        key_grad = dot(q, score_grad, 1, 1) * scale
        query_grad = dot(k, score_grad) * scale
        back[QW + h * HEAD_DIM : QW + (h + 1) * HEAD_DIM, :] = key_grad.astype(BF)
        back[QW + KW + h * HEAD_DIM : QW + KW + (h + 1) * HEAD_DIM, :] = value_grad.astype(BF)
        for i in range(GROUPS):
            at = (GROUPS * h + i) * HEAD_DIM
            back[at : at + HEAD_DIM, :] = query_grad[:, i * seq : (i + 1) * seq].astype(BF)
    step = 512
    for j in range(QKV // step):
        at = slice(j * step, (j + 1) * step)
        back_rows[:, at] = back[at, :].astype(F32).T.astype(BF)
    for c in copies:
        c.wait()
    one = dot(back_rows[...], w[:, :QKV], 1, 1)
    x = tok[...].astype(F32)
    factor = lax.rsqrt(jnp.mean(x * x, axis=-1, keepdims=True) + norm_eps)
    normed = x * factor
    experts_pad = ext.shape[0] - 16
    gain = ext[experts_pad : experts_pad + 1, :]
    gain_grad = jnp.sum(one * normed, axis=0, keepdims=True)
    scaled = one * gain
    inward = factor * (scaled - normed * jnp.mean(scaled * normed, axis=-1, keepdims=True))
    tok_grad[...] = res_grad[...] + inward
    packed = jnp.concatenate(
        [
            ext_grad[:experts_pad, :],
            jnp.broadcast_to(gain_grad, (8, gain_grad.shape[1])),
            ext_grad[experts_pad + 8 :, :],
            jnp.zeros((EXT - experts_pad - 16, gain_grad.shape[1]), F32),
        ],
        axis=0,
    )
    g[:, QKV:] = packed.T.astype(BF)
    for j in range(QKV // step):
        at = slice(j * step, (j + 1) * step)
        g[:, at] = dot(low_one[...], back_rows[:, at], 0, 0).astype(BF)
    copies_g = store_parts(me[0], lambda s: g.at[s], grads, sems_g, rows, size)
    for c in copies_g:
        c.wait()


def run_first(me, ctx_grad, qkv, probs, low_one, tokens, ext, ext_grad, res_grad, pieces, size):
    seq, width = tokens.shape
    rows = width // size
    cols = QKV + EXT
    grads = part_shapes(size, (rows, cols))
    return pl.pallas_call(
        functools.partial(first_kernel, size, rows),
        name="first_back",
        out_shape=[sds((seq, width), F32)] + grads,
        in_specs=[SMEM] + [VMEM] * 8 + [ANY] * len(pieces),
        out_specs=[VMEM] + [ANY] * len(grads),
        scratch_shapes=[
            pltpu.VMEM((width, cols), BF),
            pltpu.VMEM((width, cols), BF),
            pltpu.VMEM((QKV, seq), BF),
            pltpu.VMEM((seq, QKV), BF),
            pltpu.SemaphoreType.DMA((size,)),
            pltpu.SemaphoreType.DMA((size,)),
        ],
        compiler_params=params(),
        cost_estimate=cost(6e9, 30e6),
    )(me, ctx_grad, qkv, probs, low_one, tokens, ext, ext_grad, res_grad, *pieces)


def body(
    tokens,
    segment_ids,
    expert_choices,
    attn_gain,
    query_weight,
    key_weight,
    value_weight,
    output_weight,
    ffn_gain,
    router_weight,
    expert_gate,
    expert_up,
    expert_down,
    cotangent,
):
    size = lax.axis_size("dp")
    owners = lax.axis_size("expert")
    me = lax.axis_index("dp").astype(jnp.int32).reshape(1)
    z = lax.axis_index("expert").astype(jnp.int32).reshape(1)
    seq, width = tokens.shape
    per = expert_gate.shape[0]
    experts = per * owners
    experts_pad = -(-experts // 8) * 8
    capacity = (seq * TOP * 9 + 8 * experts - 1) // (8 * experts)
    cap = -(-capacity // 16) * 16
    slim = query_weight.shape[0]

    ext = jnp.concatenate(
        [
            router_weight,
            jnp.zeros((slim, experts_pad - experts), BF),
            jnp.broadcast_to(attn_gain[:, None], (slim, 8)),
            jnp.broadcast_to(ffn_gain[:, None], (slim, 8)),
            jnp.zeros((slim, EXT - experts_pad - 16), BF),
        ],
        axis=1,
    )
    qkv_shard = jnp.concatenate([query_weight, key_weight, value_weight, ext], axis=1)
    qkv_pieces = gather_shards(qkv_shard, 0, size)
    out_pieces = gather_shards(output_weight, 1, size)
    expert_pieces = []
    for l in range(per):
        shard = jnp.stack([expert_gate[l], expert_up[l], expert_down[l].T])
        expert_pieces.append(gather_shards(shard, (l + 1) % 2, size))

    ids = jnp.arange(experts_pad, dtype=jnp.int32)
    hot = jnp.any(expert_choices[:, None, :] == ids[None, :, None], axis=2)
    hot = hot.astype(BF).T
    at = jnp.arange(seq, dtype=jnp.int32)
    earlier = (at[:, None] < at[None, :]).astype(BF)
    place = jnp.dot(hot, earlier, preferred_element_type=F32)
    place = jnp.where(hot > 0, place, -1.0)

    cots = [cotangent] + [send_along(cotangent, r) for r in range(1, owners)]
    places = [place] + [send_along(place, r) for r in range(1, owners)]

    low_one, qkv, ctx, probs, extra = run_attention(
        me, tokens, segment_ids, segment_ids.reshape(seq, 1), qkv_pieces, size, experts_pad + 16
    )
    res, low_two = run_residual(me, tokens, ctx, extra, out_pieces, size)
    xs = [low_two] + [send_along(low_two, r) for r in range(1, owners)]
    pos, p, own_p = run_router(z, extra, xs, places, per)

    out_rows, back_rows, gate_rows, totals = [], [], [], []
    for l in range(per):
        results = run_expert(me, pos, p, xs, cots, expert_pieces[l], size, l, cap)
        out_rows.append(results[0])
        back_rows.append(results[1])
        gate_rows.append(results[2])
        totals.append(results[3:])
    combined = run_combine(pos, back_rows, gate_rows, cap)
    backs, gates = combined[:owners], combined[owners:]
    backs = [backs[0]] + [send_along(backs[r], -r) for r in range(1, owners)]
    gates = [gates[0]] + [send_along(gates[r], -r) for r in range(1, owners)]
    outs = run_combine(pos, out_rows, [], cap)
    outs = [outs[0]] + [send_along(outs[r], -r) for r in range(1, owners)]
    mixed = res
    for r in range(owners):
        mixed = mixed + outs[r].astype(F32)
    mixed = mixed.astype(BF)

    results = run_second(
        me, z, own_p, extra, low_two, res, cotangent, ctx, backs, gates, out_pieces, size, per
    )
    res_grad, ctx_grad, ext_grad = results[:3]
    out_grads = results[3:]
    results = run_first(
        me, ctx_grad, qkv, probs, low_one, tokens, extra, ext_grad, res_grad, qkv_pieces, size
    )
    grad_tokens, qkv_grads = results[0], results[1:]

    expert_totals = [reduce_shards(totals[l], l % 2, size) for l in range(per)]
    out_total = reduce_shards(out_grads, 1, size)
    out_total = lax.psum(out_total.astype(BF), "expert").astype(F32)
    qkv_total = reduce_shards(qkv_grads, 0, size)
    qkv_total = lax.psum(qkv_total.astype(BF), "expert").astype(F32)

    stacked = jnp.stack(expert_totals)
    return (
        mixed,
        grad_tokens,
        qkv_total[:, QKV + experts_pad],
        qkv_total[:, :QW],
        qkv_total[:, QW : QW + KW],
        qkv_total[:, QW + KW : QKV],
        out_total,
        qkv_total[:, QKV + experts_pad + 8],
        qkv_total[:, QKV : QKV + experts],
        stacked[:, 0],
        stacked[:, 1],
        jnp.swapaxes(stacked[:, 2], 1, 2),
    )


def solution(mesh):
    return jax.shard_map(
        body,
        mesh=mesh,
        in_specs=(
            P(("dp", "expert"), None),
            P(("dp", "expert"), None),
            P(("dp", "expert"), None),
            P("dp"),
            P("dp", None),
            P("dp", None),
            P("dp", None),
            P("dp", None),
            P("dp"),
            P("dp", None),
            P("expert", "dp", None),
            P("expert", "dp", None),
            P("expert", None, "dp"),
            P(("dp", "expert"), None),
        ),
        out_specs=(
            P(("dp", "expert"), None),
            P(("dp", "expert"), None),
            P("dp"),
            P("dp", None),
            P("dp", None),
            P("dp", None),
            P("dp", None),
            P("dp"),
            P("dp", None),
            P("expert", "dp", None),
            P("expert", "dp", None),
            P("expert", None, "dp"),
        ),
        check_vma=False,
    )
```

```python
import functools

import jax
import jax.numpy as jnp
from jax import lax
from jax.experimental import pallas as pl
from jax.experimental.pallas import tpu as pltpu
from jax.sharding import PartitionSpec as P

HEADS = 24
KV_HEADS = 8
HEAD_DIM = 64
TOP = 8
GROUPS = HEADS // KV_HEADS
QW = HEADS * HEAD_DIM
KW = KV_HEADS * HEAD_DIM
QKV = QW + 2 * KW
EXT = 128
HALVES = 2
EXTRA = 16
COST_SCALE = 1.0

norm_eps = 1e-06
masked_score = -1e30
BF = jnp.bfloat16
F32 = jnp.float32
ANY = pl.BlockSpec(memory_space=pl.ANY)
VMEM = pl.BlockSpec(memory_space=pltpu.VMEM)
SMEM = pl.BlockSpec(memory_space=pltpu.SMEM)
VMEM_LIMIT = 56 * 1024 * 1024


def dot(a, b, ca=1, cb=0):
    return lax.dot_general(a, b, (((ca,), (cb,)), ((), ())), preferred_element_type=F32)


def params():
    return pltpu.CompilerParams(vmem_limit_bytes=VMEM_LIMIT)


def cost(us):
    return pl.CostEstimate(
        flops=int(us * 1e8), bytes_accessed=int(us * 3.6e6 * COST_SCALE), transcendentals=0
    )


def sds(shape, dtype):
    return jax.ShapeDtypeStruct(shape, dtype)


def swap(value, bit, size):
    return lax.ppermute(value, "dp", [(i, i ^ bit) for i in range(size)])


def after(value, *others):
    if not others:
        return value
    return lax.optimization_barrier((value,) + others)[0]


def gather_shards(shard, route, size, name):
    rows = shard.shape[-2]
    if size != 8:
        return [lax.all_gather(shard, "dp", axis=0, tiled=False)], [(i, 0, rows) for i in range(size)]
    half = rows // 2
    with jax.named_scope(name):
        across = swap(shard, 2, size)
        along = swap(shard, 4, size)
        arrays, plan = [shard, across, along], [(0, 0, rows), (2, 0, rows), (4, 0, rows)]
        if route == 0:
            arrays.append(swap(across, 4, size))
            plan.append((6, 0, rows))
        elif route == 1:
            arrays.append(swap(along, 2, size))
            plan.append((6, 0, rows))
        else:
            arrays.append(swap(across[..., :half, :], 4, size))
            arrays.append(swap(along[..., half:, :], 2, size))
            plan += [(6, 0, half), (6, half, rows - half)]
        for array, (mask, start, count) in list(zip(arrays, plan)):
            arrays.append(swap(array, 1, size))
            plan.append((mask + 1, start, count))
    return arrays, plan


def add(a, b):
    return (a.astype(F32) + b.astype(F32)).astype(BF)


def pair_sum(parts, route, *earlier):
    own, other = parts
    other = after(swap(other, 1, 8), *earlier)
    if route == 0:
        return add(own[1::2], other[1::2]), add(own[0::2], other[0::2])
    return add(own[2:], other[2:]), add(own[:2], other[:2])


def link_sum(sent, kept, route, *earlier):
    sent = after(swap(sent, 2 if route == 0 else 4, 8), *earlier)
    return add(kept[1], sent[1]), add(kept[0], sent[0])


def last_sum(sent, kept, route, *earlier):
    sent = after(swap(sent, 4 if route == 0 else 2, 8), *earlier)
    return add(kept, sent)


def owner_at(z, r, owners):
    return jnp.bitwise_xor(z, r) if owners == 4 else lax.rem(z - r + owners, owners)


def along(value, pairs):
    return lax.ppermute(value, "expert", pairs)


def cross(value, bit):
    return along(value, [(i, i ^ bit) for i in range(4)])


def gather_owners(value, z, owners, due):
    if owners != 4:
        turns = [[(i, (i + r) % owners) for i in range(owners)] for r in range(1, owners)]
        return [value] + [along(value, pairs) for pairs in turns]
    far, near = cross(value, 2), cross(value, 1)
    middle = along(after(value, far, near, *due), [(1, 2), (2, 1)])
    passed = along(far, [(2, 3), (1, 0)])
    inner = (z == 1) | (z == 2)
    return [value, near, far, jnp.where(inner, middle, passed)]


def return_owners(parts, owners):
    if owners != 4:
        turns = [[(i, (i - r) % owners) for i in range(owners)] for r in range(1, owners)]
        return [parts[0]] + [along(v, pairs) for v, pairs in zip(parts[1:], turns)]
    passed = along(parts[3], [(3, 2), (0, 1)])
    middle = along(parts[3], [(1, 2), (2, 1)])
    relay = (parts[2].astype(F32) + passed.astype(F32)).astype(BF)
    return [parts[0], cross(parts[1], 1), cross(relay, 2), middle]


def exchange(value):
    return lax.all_to_all(value, "expert", split_axis=0, concat_axis=0, tiled=True)


def spread(value):
    owners = lax.axis_size("expert")
    return exchange(jnp.concatenate([value] * owners, axis=0))


def owner_sum(low):
    owners = lax.axis_size("expert")
    parts = exchange(low).reshape(owners, -1, low.shape[1]).astype(F32)
    return jnp.sum(parts, axis=0).astype(BF)


def plain_sum(parts):
    total = lax.psum_scatter(parts[0], "dp", scatter_dimension=0, tiled=True)
    return lax.psum(total[0], "expert").astype(F32)


def part_shapes(size, shape):
    if size != 8:
        return [sds((size,) + shape, BF)]
    return [sds((4,) + shape, BF), sds((4,) + shape, BF)]


def fetch(me, refs, plan, target, sems, rows, size):
    copies = []
    for n, (i, start, count) in enumerate(plan):
        source = refs[0].at[i] if len(refs) == 1 else refs[n]
        at = (jnp.bitwise_xor(me, i) if size == 8 else i) * rows + start
        if size == 8:
            at = pl.multiple_of(at, rows // 2)
        copies.append(pltpu.make_async_copy(source, target(pl.ds(at, count)), sems.at[n]))
    for c in copies:
        c.start()
    return copies


def store_parts(me, source, outs, sems, rows, size):
    copies = []
    for i in range(size):
        if len(outs) == 1:
            target, at = outs[0].at[i], i * rows
        else:
            target = outs[i % 2].at[i // 2]
            at = pl.multiple_of(jnp.bitwise_xor(me, i) * rows, rows)
        copies.append(pltpu.make_async_copy(source(pl.ds(at, rows)), target, sems.at[i]))
    for c in copies:
        c.start()
    return copies


def pack_kernel(experts, q, k, v, router, gain_one, gain_two, out):
    rows = q.shape[0]
    pad = -(-experts // 8) * 8
    out[:, :QW] = q[...]
    out[:, QW : QW + KW] = k[...]
    out[:, QW + KW : QKV] = v[...]
    gains = [jnp.broadcast_to(g[...].astype(F32)[None, :], (8, rows)) for g in (gain_one, gain_two)]
    parts = [router[...].astype(F32)]
    if pad > experts:
        parts.append(jnp.zeros((pad - experts, rows), F32))
    parts += gains + [jnp.zeros((EXT - pad - 16, rows), F32)]
    out[:, QKV:] = jnp.concatenate(parts, axis=0).T.astype(BF)


def run_pack(q, k, v, router, gain_one, gain_two):
    rows, experts = router.shape
    return pl.pallas_call(
        functools.partial(pack_kernel, experts),
        name="pack",
        out_shape=sds((rows, QKV + EXT), BF),
        in_specs=[VMEM] * 6,
        out_specs=VMEM,
        compiler_params=params(),
        cost_estimate=cost(0.01),
    )(q, k, v, router.T, gain_one, gain_two)


def attention_kernel(size, rows, plan, me, tok, seg_row, seg_col, *rest):
    refs, rest = rest[:-7], rest[-7:]
    low_out, qkv_out, ctx_out, prob_out, ext_out, w, sems = rest
    copies = fetch(me[0], refs, plan, lambda s: w.at[s], sems, rows, size)
    seq = tok.shape[0]
    x = tok[...].astype(F32)
    factor = lax.rsqrt(jnp.mean(x * x, axis=-1, keepdims=True) + norm_eps)
    normed = x * factor
    same = seg_col[...] == seg_row[...]
    key_at = lax.broadcasted_iota(jnp.int32, (seq, seq), 0)
    query_at = lax.broadcasted_iota(jnp.int32, (seq, seq), 1)
    allowed = jnp.where(same & (key_at <= query_at), 0.0, masked_score)
    allowed = jnp.concatenate([allowed] * GROUPS, axis=1)
    for c in copies:
        c.wait()
    ext = w[:, QKV:].astype(F32).T[: ext_out.shape[0], :]
    ext_out[...] = ext
    experts_pad = ext_out.shape[0] - 16
    gain = ext[experts_pad : experts_pad + 1, :]
    low = (normed * gain).astype(BF)
    low_out[...] = low
    step = 512
    for j in range(QKV // step):
        at = slice(j * step, (j + 1) * step)
        part = dot(low, w[:, at])
        qkv_out[at, :] = part.T.astype(BF)
    for h in range(KV_HEADS):
        q = jnp.concatenate(
            [
                qkv_out[(GROUPS * h + g) * HEAD_DIM : (GROUPS * h + g + 1) * HEAD_DIM, :]
                for g in range(GROUPS)
            ],
            axis=1,
        )
        k = qkv_out[QW + h * HEAD_DIM : QW + (h + 1) * HEAD_DIM, :]
        v = qkv_out[QW + KW + h * HEAD_DIM : QW + KW + (h + 1) * HEAD_DIM, :]
        scores = dot(k, q, 0, 0) * HEAD_DIM ** (-0.5)
        scores = jnp.where(allowed < 0.0, masked_score, scores)
        top = jnp.max(scores, axis=0, keepdims=True)
        shifted = jnp.exp(scores - top)
        probs = (shifted * (1.0 / jnp.sum(shifted, axis=0, keepdims=True))).astype(BF)
        prob_out[h] = probs
        ctx = dot(v, probs).astype(BF)
        for g in range(GROUPS):
            at = (GROUPS * h + g) * HEAD_DIM
            ctx_out[at : at + HEAD_DIM, :] = ctx[:, g * seq : (g + 1) * seq]


def run_attention(me, tokens, seg_row, seg_col, pieces, size, ext_rows):
    seq, width = tokens.shape
    rows = width // size
    arrays, plan = pieces
    return pl.pallas_call(
        functools.partial(attention_kernel, size, rows, plan),
        name="attention",
        out_shape=[
            sds((seq, width), BF),
            sds((QKV, seq), BF),
            sds((QW, seq), BF),
            sds((KV_HEADS, seq, GROUPS * seq), BF),
            sds((ext_rows, width), F32),
        ],
        in_specs=[SMEM, VMEM, VMEM, VMEM] + [ANY] * len(arrays),
        out_specs=[VMEM] * 5,
        scratch_shapes=[
            pltpu.VMEM((width, QKV + EXT), BF),
            pltpu.SemaphoreType.DMA((len(plan),)),
        ],
        compiler_params=params(),
        cost_estimate=cost(0.01),
    )(me, tokens, seg_row, seg_col, *arrays)


def residual_kernel(size, rows, plan, me, tok, ctx, ext, place, *rest):
    refs, (res_out, low_out, w, sems) = rest[:-4], rest[-4:]
    copies = fetch(me[0], refs, plan, lambda s: w.at[s], sems, rows, size)
    experts_pad = ext.shape[0] - 16
    for c in copies:
        c.wait()
    res = tok[...].astype(F32) + dot(ctx[...], w[...], 0, 0)
    res_out[...] = res
    factor = lax.rsqrt(jnp.mean(res * res, axis=-1, keepdims=True) + norm_eps)
    seq = res.shape[0]
    low_out[:seq, :] = (res * factor * ext[experts_pad + 8 : experts_pad + 9, :]).astype(BF)
    low_out[seq:, :] = place[...]


def run_residual(me, tokens, ctx, ext, place, pieces, size):
    seq, width = tokens.shape
    rows = QW // size
    arrays, plan = pieces
    return pl.pallas_call(
        functools.partial(residual_kernel, size, rows, plan),
        name="residual",
        out_shape=[sds((seq, width), F32), sds((seq + EXTRA, width), BF)],
        in_specs=[SMEM, VMEM, VMEM, VMEM, VMEM] + [ANY] * len(arrays),
        out_specs=[VMEM] * 2,
        scratch_shapes=[pltpu.VMEM((QW, width), BF), pltpu.SemaphoreType.DMA((len(plan),))],
        compiler_params=params(),
        cost_estimate=cost(0.01),
    )(me, tokens, ctx, ext, place, *arrays)


def slot_of(block, seq, width):
    across = width // seq
    row, col = block // across * 8, block % across * seq
    return slice(row, row + 8), slice(col, col + seq)


def router_kernel(owners, per, z, ext, *rest):
    rows, rest = rest[:owners], rest[owners:]
    pos_out, p_out, own_out, all_p, all_pos = rest
    experts_pad = ext.shape[0] - 16
    seq, width = rows[0].shape[0] - EXTRA, rows[0].shape[1]
    router = ext[:experts_pad, :].astype(BF)
    at = z[0] * per
    for r in range(owners):
        logits = dot(router, rows[r][:seq, :], 1, 1)
        spots = rows[r][seq:, :].astype(F32)
        for b in range(experts_pad // 8):
            of, to = slot_of(b, seq, width)
            all_pos[b * 8 : (b + 1) * 8, :] = spots[of, to]
        where = all_pos[...]
        named = where >= 0.0
        logits = jnp.where(named, logits, masked_score)
        top = jnp.max(logits, axis=0, keepdims=True)
        shifted = jnp.where(named, jnp.exp(logits - top), 0.0)
        probs = shifted / jnp.sum(shifted, axis=0, keepdims=True)
        all_p[...] = probs
        if r == 0:
            own_out[...] = probs
        for l in range(per):
            p_out[l, r : r + 1, :] = all_p[pl.ds(at + l, 1), :]
            pos_out[l, r : r + 1, :] = all_pos[pl.ds(at + l, 1), :].astype(jnp.int32)


def run_router(z, ext, rows, per):
    owners = len(rows)
    seq = rows[0].shape[0] - EXTRA
    experts_pad = ext.shape[0] - 16
    return pl.pallas_call(
        functools.partial(router_kernel, owners, per),
        name="router",
        out_shape=[
            sds((per, owners, seq), jnp.int32),
            sds((per, owners, seq), F32),
            sds((experts_pad, seq), F32),
        ],
        in_specs=[SMEM, VMEM] + [VMEM] * owners,
        out_specs=[VMEM] * 3,
        scratch_shapes=[pltpu.VMEM((experts_pad, seq), F32)] * 2,
        compiler_params=params(),
        cost_estimate=cost(0.01),
    )(z, ext, *rows)


def pick_rows(owners, cap, number, z, pos, p, xs, cs, xv, cv, xr, cr, prow, sem_x, sem_c):
    seq = xv.shape[1]
    copies_x = [
        pltpu.make_async_copy(xs[r].at[pl.ds(0, seq)], xv.at[r], sem_x.at[r]) for r in range(owners)
    ]
    copies_c = []
    for r in range(owners):
        start = pl.multiple_of(owner_at(z[0], r, owners) * seq, seq)
        copies_c.append(pltpu.make_async_copy(cs.at[pl.ds(start, seq)], cv.at[r], sem_c.at[r]))
    for a, b in zip(copies_x, copies_c):
        a.start()
        b.start()

    def finish():
        slot = lax.broadcasted_iota(jnp.int32, (cap, seq), 0)
        for r in range(owners):
            copies_x[r].wait()
            copies_c[r].wait()
            hot = pos[number, r : r + 1, :] == slot
            low_hot = jnp.where(hot, 1.0, 0.0).astype(BF)
            at = pl.ds(r * cap, cap)
            xr[at, :] = dot(low_hot, xv[r]).astype(BF)
            cr[at, :] = dot(low_hot, cv[r]).astype(BF)
            prow[at, :] = jnp.sum(
                jnp.where(hot, p[number, r : r + 1, :], 0.0), axis=1, keepdims=True
            )

    return finish


def through_expert(owners, cap, number, pos, xr, cr, prow, w, hp, gg, ug, gate, gate_out):
    ff = w.shape[2]
    step = ff // HALVES
    gate[...] = jnp.zeros_like(gate)
    for j in range(HALVES):
        cols = slice(j * step, (j + 1) * step)
        gate_pre = dot(xr[...], w[0, :, cols])
        up_pre = dot(xr[...], w[1, :, cols])
        back = dot(cr[...], w[2, :, cols])
        probs = prow[...]
        s = jax.nn.sigmoid(gate_pre)
        silu = gate_pre * s
        hidden = silu * up_pre
        gate[...] += jnp.sum(hidden * back, axis=1, keepdims=True)
        hp[:, cols] = (hidden * probs).astype(BF)
        back = back * probs
        gg[:, cols] = (back * up_pre * (s + silu * (1.0 - s))).astype(BF)
        ug[:, cols] = (back * silu).astype(BF)
    seq = pos.shape[2]
    slot = lax.broadcasted_iota(jnp.int32, (cap, seq), 0)
    for r in range(owners):
        hot = pos[number, r : r + 1, :] == slot
        at = pl.ds(r * cap, cap)
        gate_out[r : r + 1, :] = jnp.sum(jnp.where(hot, gate[at, :], 0.0), axis=0, keepdims=True)


def load_weights(me, refs, plan, w, sems, slot_at, rows, size):
    shards = [ref.at[:, slot_at] if len(refs) == 1 else ref.at[slot_at] for ref in refs]
    return fetch(me, shards, plan, lambda s: w.at[:, s, :], sems, rows, size)


def weight_grads(xr, cr, hp, gg, ug, g, grads, sems, slot_at, rows, size):
    width = xr.shape[1]
    tile = width // HALVES
    for j in range(HALVES):
        cols = slice(j * tile, (j + 1) * tile)
        g[0, cols, :] = dot(xr[:, cols], gg[...], 0, 0).astype(BF)
        g[1, cols, :] = dot(xr[:, cols], ug[...], 0, 0).astype(BF)
        g[2, cols, :] = dot(cr[:, cols], hp[...], 0, 0).astype(BF)
    copies = [
        pltpu.make_async_copy(g.at[:, pl.ds(i * rows, rows), :], grads.at[i, slot_at], sems.at[i])
        for i in range(size)
    ]
    for c in copies:
        c.start()
    return copies


def rows_back(w, gg, ug, bv):
    tile = bv.shape[1] // HALVES
    for j in range(HALVES):
        cols = slice(j * tile, (j + 1) * tile)
        total = dot(gg[...], w[0, cols, :], 1, 1) + dot(ug[...], w[1, cols, :], 1, 1)
        bv[:, cols] = total.astype(BF)


def rows_out(w, hp, ov):
    tile = ov.shape[1] // HALVES
    for j in range(HALVES):
        cols = slice(j * tile, (j + 1) * tile)
        ov[:, cols] = dot(hp[...], w[cols, :], 1, 1).astype(BF)


def expert_kernel(
    size, rows, owners, cap, number, slot_at, weight_at, plan, count, me, z, pos, p, cs, *rest
):
    xs, refs, rest = rest[:owners], rest[owners : owners + count], rest[owners + count :]
    if slot_at > 0:
        rest = rest[1:]
    out_rows, back_rows, gate_out, grads = rest[:4]
    xv, cv, w, xr, cr, prow, hp, gg, ug, gate, ov, bv, g, sem_x, sem_c, sem_w, sem_o = rest[4:]
    finish = pick_rows(owners, cap, number, z, pos, p, xs, cs, xv, cv, xr, cr, prow, sem_x, sem_c)
    copies_w = load_weights(me[0], refs, plan, w, sem_w, weight_at, rows, size)
    finish()
    for c in copies_w:
        c.wait()
    through_expert(owners, cap, number, pos, xr, cr, prow, w, hp, gg, ug, gate, gate_out)
    copies = weight_grads(xr, cr, hp, gg, ug, g, grads, sem_w, slot_at, rows, size)
    rows_back(w, gg, ug, bv)
    copy_b = pltpu.make_async_copy(bv, back_rows, sem_o.at[0])
    copy_b.start()
    rows_out(w.at[2], hp, ov)
    copy_o = pltpu.make_async_copy(ov, out_rows, sem_o.at[1])
    copy_o.start()
    for c in copies + [copy_b, copy_o]:
        c.wait()


def grads_shape(size, count, rows, ff):
    return sds((size, count, 3, rows, ff), BF)


def run_expert(me, z, pos, p, xs, cs, pieces, weight_at, buffer, size, number, slot_at, count, cap):
    owners, seq = pos.shape[1:]
    width = xs[0].shape[1]
    refs, plan = pieces
    ff = refs[0].shape[-1]
    rows = width // size
    total = owners * cap
    given = [me, z, pos, p, cs, *xs, *refs] + ([] if buffer is None else [buffer])
    return pl.pallas_call(
        functools.partial(
            expert_kernel, size, rows, owners, cap, number, slot_at, weight_at, plan, len(refs)
        ),
        name="expert",
        out_shape=[
            sds((total, width), BF),
            sds((total, width), BF),
            sds((owners, seq), F32),
            grads_shape(size, count, rows, ff),
        ],
        in_specs=[SMEM, SMEM, VMEM, VMEM] + [ANY] * (len(given) - 4),
        out_specs=[ANY, ANY, VMEM, ANY],
        input_output_aliases={} if buffer is None else {len(given) - 1: 3},
        scratch_shapes=[
            pltpu.VMEM((owners, seq, width), BF),
            pltpu.VMEM((owners, seq, width), BF),
            pltpu.VMEM((3, width, ff), BF),
            pltpu.VMEM((total, width), BF),
            pltpu.VMEM((total, width), BF),
            pltpu.VMEM((total, 1), F32),
            pltpu.VMEM((total, ff), BF),
            pltpu.VMEM((total, ff), BF),
            pltpu.VMEM((total, ff), BF),
            pltpu.VMEM((total, 1), F32),
            pltpu.VMEM((total, width), BF),
            pltpu.VMEM((total, width), BF),
            pltpu.VMEM((3, width, ff), BF),
            pltpu.SemaphoreType.DMA((owners,)),
            pltpu.SemaphoreType.DMA((owners,)),
            pltpu.SemaphoreType.DMA((max(size, len(plan)),)),
            pltpu.SemaphoreType.DMA((2,)),
        ],
        compiler_params=params(),
        cost_estimate=cost(0.01),
    )(*given)


def combined_rows(per, cap, pos, r, rows):
    seq = pos.shape[2]
    slot = lax.broadcasted_iota(jnp.int32, (cap, seq), 0)
    hot = jnp.concatenate(
        [jnp.where(pos[l, pl.ds(r, 1), :] == slot, 1.0, 0.0).astype(BF) for l in range(per)], axis=0
    )
    stacked = jnp.concatenate([rows[l][...] for l in range(per)], axis=0)
    return dot(hot, stacked, 0, 0).astype(BF)


def combine_back_kernel(owners, per, cap, experts_pad, z, pos, *rest):
    rows, gates, rest = rest[:per], rest[per : 2 * per], rest[2 * per :]
    outs, block = rest[:owners], rest[owners]
    r = pl.program_id(0)
    seq, width = pos.shape[2], outs[0].shape[1]
    total = combined_rows(per, cap, pos, r, rows)
    block[...] = jnp.zeros_like(block)
    for l in range(per):
        block[pl.ds(z[0] * per + l, 1), :] = gates[l][pl.ds(r, 1), :]
    value = block[...]
    high = value.astype(BF)
    low = (value - high.astype(F32)).astype(BF)
    for o in range(owners):

        @pl.when(r == o)
        def _():
            outs[o][:seq, :] = total
            outs[o][seq:, :] = jnp.zeros((EXTRA, width), BF)
            both = jnp.concatenate([high, low], axis=0).astype(F32)
            for row in range(EXTRA // 8):
                across = width // seq
                blocks = [
                    both[(row * across + b) * 8 : (row * across + b + 1) * 8, :]
                    if row * across + b < 2 * experts_pad // 8
                    else jnp.zeros((8, seq), F32)
                    for b in range(across)
                ]
                outs[o][seq + row * 8 : seq + row * 8 + 8, :] = jnp.concatenate(
                    blocks, axis=1
                ).astype(BF)


def whole(shape):
    return pl.BlockSpec(shape, lambda r: (0,) * len(shape))


def run_combine_back(z, pos, rows, gates, cap, experts_pad):
    per, owners, seq = pos.shape
    width = rows[0].shape[1]
    shapes = [sds((seq + EXTRA, width), BF)] * owners
    return pl.pallas_call(
        functools.partial(combine_back_kernel, owners, per, cap, experts_pad),
        name="combine_back",
        grid=(owners,),
        out_shape=shapes,
        in_specs=[SMEM, whole(pos.shape)]
        + [pl.BlockSpec((cap, width), lambda r: (r, 0))] * per
        + [whole((owners, seq))] * per,
        out_specs=[whole(s.shape) for s in shapes],
        scratch_shapes=[pltpu.VMEM((experts_pad, seq), F32)],
        compiler_params=params(),
        cost_estimate=cost(0.01),
    )(z, pos, *rows, *gates)


def combine_out_kernel(per, cap, z, pos, *rest):
    rows, out = rest[:per], rest[per]
    out[...] = combined_rows(per, cap, pos, pl.program_id(0), rows)


def run_combine_out(z, pos, rows, cap):
    per, owners, seq = pos.shape
    width = rows[0].shape[1]
    grid_spec = pltpu.PrefetchScalarGridSpec(
        num_scalar_prefetch=1,
        grid=(owners,),
        in_specs=[pl.BlockSpec(pos.shape, lambda r, z: (0, 0, 0))]
        + [pl.BlockSpec((cap, width), lambda r, z: (r, 0))] * per,
        out_specs=pl.BlockSpec((seq, width), lambda r, z: (owner_at(z[0], r, owners), 0)),
    )
    return pl.pallas_call(
        functools.partial(combine_out_kernel, per, cap),
        name="combine_out",
        grid_spec=grid_spec,
        out_shape=sds((owners * seq, width), BF),
        compiler_params=params(),
        cost_estimate=cost(0.01),
    )(z, pos, *rows)


def second_kernel(
    size, rows, owners, per, plan, count, me, own_p, ext, low_two, res, cot, ctx, *rest
):
    backs, rest = rest[:owners], rest[owners:]
    outs_count = 1 if size != 8 else 2
    refs, rest = rest[:count], rest[count:]
    res_grad, ctx_grad, ext_grad = rest[:3]
    rest = rest[3:]
    grads, rest = rest[:outs_count], rest[outs_count:]
    w, g, gate, sems, sems_g = rest
    copies = fetch(me[0], refs, plan, lambda s: w.at[s], sems, rows, size)
    experts_pad = own_p.shape[0]
    seq, width = res.shape
    arrived = backs[0][seq:, :].astype(F32)
    for r in range(1, owners):
        arrived = arrived + backs[r][seq:, :].astype(F32)
    for b in range(experts_pad // 8):
        high_at = slot_of(b, seq, width)
        low_at = slot_of(b + experts_pad // 8, seq, width)
        gate[b * 8 : (b + 1) * 8, :] = arrived[high_at] + arrived[low_at]
    p = own_p[...]
    gate_grad = gate[...]
    weighted = jnp.sum(p * gate_grad, axis=0, keepdims=True)
    logit_grad = (p * (gate_grad - weighted)).astype(BF)
    router = ext[:experts_pad, :].astype(BF)
    ext_grad[:experts_pad, :] = dot(logit_grad, low_two[:seq, :])
    two = dot(logit_grad, router, 0, 0)
    for r in range(owners):
        two = two + backs[r][:seq, :].astype(F32)
    values = res[...]
    factor = lax.rsqrt(jnp.mean(values * values, axis=-1, keepdims=True) + norm_eps)
    normed = values * factor
    ext_grad[experts_pad:, :] = jnp.broadcast_to(
        jnp.sum(two * normed, axis=0, keepdims=True), (16, normed.shape[1])
    )
    scaled = two * ext[experts_pad + 8 : experts_pad + 9, :]
    inward = factor * (scaled - normed * jnp.mean(scaled * normed, axis=-1, keepdims=True))
    total = cot[...].astype(F32) + inward
    res_grad[...] = total
    low = total.astype(BF)
    step = QW // 4
    for j in range(4):
        at = slice(j * step, (j + 1) * step)
        g[at, :] = dot(ctx[at, :], low).astype(BF)
    copies_g = store_parts(me[0], lambda s: g.at[s], grads, sems_g, rows, size)
    for c in copies:
        c.wait()
    for j in range(4):
        at = slice(j * step, (j + 1) * step)
        ctx_grad[at, :] = dot(w[at, :], low, 1, 1).astype(BF)
    for c in copies_g:
        c.wait()


def run_second(me, own_p, ext, low_two, res, cot, ctx, backs, pieces, size, per):
    owners = len(backs)
    arrays, plan = pieces
    seq, width = res.shape
    rows = QW // size
    grads = part_shapes(size, (rows, width))
    experts_pad = own_p.shape[0]
    return pl.pallas_call(
        functools.partial(second_kernel, size, rows, owners, per, plan, len(arrays)),
        name="second_back",
        out_shape=[sds((seq, width), F32), sds((QW, seq), BF), sds((experts_pad + 16, width), F32)] + grads,
        in_specs=[SMEM] + [VMEM] * (6 + owners) + [ANY] * len(arrays),
        out_specs=[VMEM] * 3 + [ANY] * len(grads),
        scratch_shapes=[
            pltpu.VMEM((QW, width), BF),
            pltpu.VMEM((QW, width), BF),
            pltpu.VMEM((experts_pad, seq), F32),
            pltpu.SemaphoreType.DMA((len(plan),)),
            pltpu.SemaphoreType.DMA((size,)),
        ],
        compiler_params=params(),
        cost_estimate=cost(0.01),
    )(me, own_p, ext, low_two, res, cot, ctx, *backs, *arrays)


def heads_kernel(size, rows, me, ctx_grad, qkv, probs, low_one, *rest):
    outs_count = 1 if size != 8 else 2
    back_rows, rest = rest[0], rest[1:]
    grads, rest = rest[:outs_count], rest[outs_count:]
    g, back, sems_g = rest
    seq = low_one.shape[0]
    scale = HEAD_DIM ** (-0.5)
    for h in range(KV_HEADS):

        def heads(ref):
            return jnp.concatenate(
                [
                    ref[(GROUPS * h + i) * HEAD_DIM : (GROUPS * h + i + 1) * HEAD_DIM, :]
                    for i in range(GROUPS)
                ],
                axis=1,
            )

        upstream = heads(ctx_grad)
        q = heads(qkv)
        k = qkv[QW + h * HEAD_DIM : QW + (h + 1) * HEAD_DIM, :]
        v = qkv[QW + KW + h * HEAD_DIM : QW + KW + (h + 1) * HEAD_DIM, :]
        low_p = probs[h]
        weights = low_p.astype(F32)
        prob_grad = dot(v, upstream, 0, 0)
        inner = jnp.sum(prob_grad * weights, axis=0, keepdims=True)
        score_grad = (weights * (prob_grad - inner)).astype(BF)
        value_grad = dot(upstream, low_p, 1, 1)
        key_grad = dot(q, score_grad, 1, 1) * scale
        query_grad = dot(k, score_grad) * scale
        back[QW + h * HEAD_DIM : QW + (h + 1) * HEAD_DIM, :] = key_grad.astype(BF)
        back[QW + KW + h * HEAD_DIM : QW + KW + (h + 1) * HEAD_DIM, :] = value_grad.astype(BF)
        for i in range(GROUPS):
            at = (GROUPS * h + i) * HEAD_DIM
            back[at : at + HEAD_DIM, :] = query_grad[:, i * seq : (i + 1) * seq].astype(BF)
    step = 512
    for j in range(QKV // step):
        at = slice(j * step, (j + 1) * step)
        back_rows[:, at] = back[at, :].astype(F32).T.astype(BF)
    for j in range(QW // step):
        at = slice(j * step, (j + 1) * step)
        g[:, at] = dot(low_one[...], back_rows[:, at], 0, 0).astype(BF)
    copies_g = store_parts(me[0], lambda s: g.at[s], grads, sems_g, rows, size)
    for c in copies_g:
        c.wait()


def run_heads(me, ctx_grad, qkv, probs, low_one, size):
    seq, width = low_one.shape
    rows = width // size
    grads = part_shapes(size, (rows, QW))
    return pl.pallas_call(
        functools.partial(heads_kernel, size, rows),
        name="heads_back",
        out_shape=[sds((seq, QKV), BF)] + grads,
        in_specs=[SMEM] + [VMEM] * 4,
        out_specs=[VMEM] + [ANY] * len(grads),
        scratch_shapes=[
            pltpu.VMEM((width, QW), BF),
            pltpu.VMEM((QKV, seq), BF),
            pltpu.SemaphoreType.DMA((size,)),
        ],
        compiler_params=params(),
        cost_estimate=cost(0.01),
    )(me, ctx_grad, qkv, probs, low_one)


def first_kernel(
    size, rows, plan, count, me, back_rows, low_one, tok, ext, ext_grad, res_grad, *rest
):
    outs_count = 1 if size != 8 else 2
    refs, rest = rest[:count], rest[count:]
    tok_grad, rest = rest[0], rest[1:]
    grads, rest = rest[:outs_count], rest[outs_count:]
    w, g, sems, sems_g = rest
    copies = fetch(me[0], refs, plan, lambda s: w.at[s], sems, rows, size)
    step = 512
    for j in range(2 * KW // step):
        at = slice(j * step, (j + 1) * step)
        of = slice(QW + j * step, QW + (j + 1) * step)
        g[:, at] = dot(low_one[...], back_rows[:, of], 0, 0).astype(BF)
    for c in copies:
        c.wait()
    one = dot(back_rows[...], w[:, :QKV], 1, 1)
    x = tok[...].astype(F32)
    factor = lax.rsqrt(jnp.mean(x * x, axis=-1, keepdims=True) + norm_eps)
    normed = x * factor
    experts_pad = ext.shape[0] - 16
    gain = ext[experts_pad : experts_pad + 1, :]
    gain_grad = jnp.sum(one * normed, axis=0, keepdims=True)
    packed = jnp.concatenate(
        [
            ext_grad[:experts_pad, :],
            jnp.broadcast_to(gain_grad, (8, gain_grad.shape[1])),
            ext_grad[experts_pad + 8 :, :],
            jnp.zeros((EXT - experts_pad - 16, gain_grad.shape[1]), F32),
        ],
        axis=0,
    )
    g[:, 2 * KW :] = packed.T.astype(BF)
    copies_g = store_parts(me[0], lambda s: g.at[s], grads, sems_g, rows, size)
    scaled = one * gain
    inward = factor * (scaled - normed * jnp.mean(scaled * normed, axis=-1, keepdims=True))
    tok_grad[...] = res_grad[...] + inward
    for c in copies_g:
        c.wait()


def run_first(me, back_rows, low_one, tokens, ext, ext_grad, res_grad, pieces, size):
    arrays, plan = pieces
    seq, width = tokens.shape
    rows = width // size
    cols = 2 * KW + EXT
    grads = part_shapes(size, (rows, cols))
    return pl.pallas_call(
        functools.partial(first_kernel, size, rows, plan, len(arrays)),
        name="first_back",
        out_shape=[sds((seq, width), F32)] + grads,
        in_specs=[SMEM] + [VMEM] * 6 + [ANY] * len(arrays),
        out_specs=[VMEM] + [ANY] * len(grads),
        scratch_shapes=[
            pltpu.VMEM((width, QKV + EXT), BF),
            pltpu.VMEM((width, cols), BF),
            pltpu.SemaphoreType.DMA((len(plan),)),
            pltpu.SemaphoreType.DMA((size,)),
        ],
        compiler_params=params(),
        cost_estimate=cost(0.01),
    )(me, back_rows, low_one, tokens, ext, ext_grad, res_grad, *arrays)


def split_groups(per):
    cut = max(1, (2 * per) // 5)
    return [(0, cut), (cut, per)]


def weight_groups(per):
    return split_groups(per)


def body(
    tokens,
    segment_ids,
    expert_choices,
    attn_gain,
    query_weight,
    key_weight,
    value_weight,
    output_weight,
    ffn_gain,
    router_weight,
    expert_gate,
    expert_up,
    expert_down,
    cotangent,
):
    size = lax.axis_size("dp")
    owners = lax.axis_size("expert")
    me = lax.axis_index("dp").astype(jnp.int32).reshape(1)
    z = lax.axis_index("expert").astype(jnp.int32).reshape(1)
    seq, width = tokens.shape
    per = expert_gate.shape[0]
    experts = per * owners
    experts_pad = -(-experts // 8) * 8
    capacity = (seq * TOP * 9 + 8 * experts - 1) // (8 * experts)
    cap = -(-capacity // 16) * 16
    slim = query_weight.shape[0]

    packed = run_pack(query_weight, key_weight, value_weight, router_weight, attn_gain, ffn_gain)
    qkv_pieces = gather_shards(packed, 2, size, "qkv")
    early = output_weight
    if size == 8:
        early = after(early, *qkv_pieces[0][1:3])
    out_pieces = gather_shards(early, 1, size, "output")
    shards = jnp.stack([expert_gate, expert_up, jnp.swapaxes(expert_down, 1, 2)], axis=1)
    first, last = weight_groups(per)[0]
    part = shards[first:last]
    if size == 8:
        part = after(part, *out_pieces[0][1:3], *qkv_pieces[0][3:5])
    gathered = [gather_shards(part, 0, size, "experts0")]
    where_at = [
        (group, l - first)
        for group, (first, last) in enumerate(weight_groups(per))
        for l in range(first, last)
    ]

    ids = jnp.arange(experts_pad, dtype=jnp.int32)
    hot = jnp.any(expert_choices[:, None, :] == ids[None, :, None], axis=2)
    hot = hot.astype(BF).T
    at = jnp.arange(seq, dtype=jnp.int32)
    earlier = (at[:, None] < at[None, :]).astype(BF)
    place = jnp.dot(hot, earlier, preferred_element_type=F32)
    place = jnp.where(hot > 0, place, -1.0).astype(BF)
    across = width // seq
    place = jnp.pad(place, ((0, EXTRA * across - experts_pad), (0, 0)))
    place = place.reshape(EXTRA // 8, across, 8, seq).swapaxes(1, 2).reshape(EXTRA, width)
    cots = lax.all_gather(cotangent, "expert", axis=0, tiled=True)

    low_one, qkv, ctx, probs, extra = run_attention(
        me,
        tokens,
        segment_ids,
        segment_ids.reshape(seq, 1),
        qkv_pieces,
        size,
        experts_pad + 16,
    )
    res, low_two = run_residual(me, tokens, ctx, extra, place, out_pieces, size)
    xs = gather_owners(low_two, z[0], owners, gathered[0][0][1:3] if size == 8 else ())
    first, last = weight_groups(per)[1]
    part = shards[first:last]
    if size == 8:
        part = after(part, xs[2] if owners == 4 else low_two)
    gathered.append(gather_shards(part, 2, size, "experts1"))
    pos, p, own_p = run_router(z, extra, xs, per)

    out_rows, back_rows, gate_rows, expert_totals = [], [], [], []
    groups = split_groups(per)
    first, last = groups[0]
    buffer = None
    for l in range(first, last):
        group, at = where_at[l]
        if size == 8 and l == last - 1:
            p = after(p, *gathered[1][0][1:3])
        results = run_expert(
            me, z, pos, p, xs, cots, gathered[group], at, buffer, size, l, l - first, last - first, cap
        )
        out_rows.append(results[0])
        back_rows.append(results[1])
        gate_rows.append(results[2])
        buffer = results[3]
    total = lax.psum_scatter(buffer, "dp", scatter_dimension=0, tiled=False)
    expert_totals.append(total.astype(F32))
    first, last = groups[1]
    buffer = None
    for l in range(first, last):
        group, at = where_at[l]
        results = run_expert(
            me, z, pos, p, xs, cots, gathered[group], at, buffer, size, l, l - first, last - first, cap
        )
        out_rows.append(results[0])
        back_rows.append(results[1])
        gate_rows.append(results[2])
        buffer = results[3]
    total = lax.psum_scatter(buffer, "dp", scatter_dimension=0, tiled=False)
    expert_totals.append(total.astype(F32))
    backs = run_combine_back(z, pos, back_rows, gate_rows, cap, experts_pad)
    backs = return_owners(backs, owners)
    outs = run_combine_out(z, pos, out_rows, cap)
    ctx = after(ctx, outs)
    results = run_second(
        me, own_p, extra, low_two, res, cotangent, ctx, backs, out_pieces, size, per
    )
    res_grad, ctx_grad, ext_grad = results[:3]
    out_grads = results[3:]
    outs = exchange(after(outs, ctx_grad))
    mixed = res
    for r in range(owners):
        mixed = mixed + outs[r * seq : (r + 1) * seq].astype(F32)
    mixed = mixed.astype(BF)
    results = run_heads(me, ctx_grad, qkv, probs, low_one, size)
    back_heads, query_grads = results[0], results[1:]
    if size == 8:
        o_sent, o_kept = pair_sum(out_grads, 1)
        back_heads = after(back_heads, o_sent)
    results = run_first(
        me, back_heads, low_one, tokens, extra, ext_grad, res_grad, qkv_pieces, size
    )
    grad_tokens, rest_grads = results[0], results[1:]
    stacked = jnp.concatenate(expert_totals, axis=0)
    expert_outputs = (stacked[:, 0], stacked[:, 1], jnp.swapaxes(stacked[:, 2], 1, 2))
    if size == 8:
        q_sent, q_kept = pair_sum(query_grads, 0)
        r_sent, r_kept = pair_sum(rest_grads, 1, q_sent)
        o_sent, o_kept = link_sum(o_sent, o_kept, 1, r_sent, *expert_outputs)
        q_sent, q_kept = link_sum(q_sent, q_kept, 0, o_sent)
        r_sent, r_kept = link_sum(r_sent, r_kept, 1, q_sent)
        out_total = last_sum(o_sent, o_kept, 1, r_sent, mixed)
        query_total = last_sum(q_sent, q_kept, 0, out_total)
        rest_total = last_sum(r_sent, r_kept, 1, query_total)
        out_total = spread(owner_sum(out_total)).astype(F32)
        both = after(jnp.concatenate([query_total, rest_total], axis=1), out_total)
        both = spread(owner_sum(both)).astype(F32)
        query_total, rest_total = both[:, :QW], both[:, QW:]
    else:
        out_total, query_total, rest_total = map(plain_sum, (out_grads, query_grads, rest_grads))

    return (
        mixed,
        grad_tokens,
        rest_total[:, 2 * KW + experts_pad],
        query_total,
        rest_total[:, :KW],
        rest_total[:, KW : 2 * KW],
        out_total,
        rest_total[:, 2 * KW + experts_pad + 8],
        rest_total[:, 2 * KW : 2 * KW + experts],
        *expert_outputs,
    )


def solution(mesh):
    return jax.shard_map(
        body,
        mesh=mesh,
        in_specs=(
            P(("dp", "expert"), None),
            P(("dp", "expert"), None),
            P(("dp", "expert"), None),
            P("dp"),
            P("dp", None),
            P("dp", None),
            P("dp", None),
            P("dp", None),
            P("dp"),
            P("dp", None),
            P("expert", "dp", None),
            P("expert", "dp", None),
            P("expert", None, "dp"),
            P(("dp", "expert"), None),
        ),
        out_specs=(
            P(("dp", "expert"), None),
            P(("dp", "expert"), None),
            P("dp"),
            P("dp", None),
            P("dp", None),
            P("dp", None),
            P("dp", None),
            P("dp"),
            P("dp", None),
            P("expert", "dp", None),
            P("expert", "dp", None),
            P("expert", None, "dp"),
        ),
        check_vma=False,
    )
```

```python
import functools

import jax
import jax.numpy as jnp
from jax import lax
from jax.experimental import pallas as pl
from jax.experimental.pallas import tpu as pltpu
from jax.sharding import PartitionSpec as P

HEADS = 24
KV_HEADS = 8
HEAD_DIM = 64
TOP = 8
GROUPS = HEADS // KV_HEADS
QW = HEADS * HEAD_DIM
KW = KV_HEADS * HEAD_DIM
QKV = QW + 2 * KW
EXT = 128
HALVES = 2
EXTRA = 16
COST_SCALE = 1.0

norm_eps = 1e-06
masked_score = -1e30
BF = jnp.bfloat16
F32 = jnp.float32
ANY = pl.BlockSpec(memory_space=pl.ANY)
VMEM = pl.BlockSpec(memory_space=pltpu.VMEM)
SMEM = pl.BlockSpec(memory_space=pltpu.SMEM)
VMEM_LIMIT = 56 * 1024 * 1024


def dot(a, b, ca=1, cb=0):
    return lax.dot_general(a, b, (((ca,), (cb,)), ((), ())), preferred_element_type=F32)


def params():
    return pltpu.CompilerParams(vmem_limit_bytes=VMEM_LIMIT)


def cost(us):
    return pl.CostEstimate(
        flops=int(us * 1.1e9), bytes_accessed=int(us * 3.6e6 * COST_SCALE), transcendentals=0
    )


def sds(shape, dtype):
    return jax.ShapeDtypeStruct(shape, dtype)


def swap(value, bit, size):
    return lax.ppermute(value, "dp", [(i, i ^ bit) for i in range(size)])


def wait(order, *values):
    return lax.optimization_barrier((order,) + values)


def hold(order, value):
    return lax.optimization_barrier((order, value))[1]


def plain_shards(shard, size):
    rows = shard.shape[-2]
    arrays = [lax.all_gather(shard, "dp", axis=0, tiled=False)]
    return arrays, [(i, 0, rows) for i in range(size)]


def add(a, b):
    return (a.astype(F32) + b.astype(F32)).astype(BF)


def owner_at(z, r, owners):
    return jnp.bitwise_xor(z, r) if owners == 4 else lax.rem(z - r + owners, owners)


def along(value, pairs):
    return lax.ppermute(value, "expert", pairs)


def cross(value, bit):
    return along(value, [(i, i ^ bit) for i in range(4)])


def plain_owners(value, owners):
    turns = [[(i, (i + r) % owners) for i in range(owners)] for r in range(1, owners)]
    return [value] + [along(value, pairs) for pairs in turns]


def plain_return(parts, owners):
    turns = [[(i, (i - r) % owners) for i in range(owners)] for r in range(1, owners)]
    return [parts[0]] + [along(v, pairs) for v, pairs in zip(parts[1:], turns)]


def exchange(value):
    return lax.all_to_all(value, "expert", split_axis=0, concat_axis=0, tiled=True)


def part_shapes(size, shape):
    if size != 8:
        return [sds((size,) + shape, BF)]
    return [sds(shape, BF)] * 4 + [sds((4,) + shape, BF)]


def fetch(me, refs, plan, target, sems, rows, size):
    copies = []
    for n, (i, start, count) in enumerate(plan):
        source = refs[0].at[i] if len(refs) == 1 else refs[n]
        at = (jnp.bitwise_xor(me, i) if size == 8 else i) * rows + start
        if size == 8:
            at = pl.multiple_of(at, rows // 2)
        copies.append(pltpu.make_async_copy(source, target(pl.ds(at, count)), sems.at[n]))
    for c in copies:
        c.start()
    return copies


def pair_refs(own, other, size):
    if size != 8:
        return [own]
    return [(other if i % 2 else own).at[i // 2] for i in range(size)]


def store_parts(me, source, outs, sems, rows, size):
    copies = []
    for i in range(size):
        if len(outs) == 1:
            target, at = outs[0].at[i], i * rows
        else:
            target = outs[i]
            at = pl.multiple_of(jnp.bitwise_xor(me, i) * rows, rows)
        copies.append(pltpu.make_async_copy(source(pl.ds(at, rows)), target, sems.at[i]))
    for c in copies:
        c.start()
    return copies


def pack_kernel(experts, q, k, v, router, gain_one, gain_two, out):
    rows = q.shape[0]
    pad = -(-experts // 8) * 8
    out[:, :QW] = q[...]
    out[:, QW : QW + KW] = k[...]
    out[:, QW + KW : QKV] = v[...]
    gains = [jnp.broadcast_to(g[...].astype(F32)[None, :], (8, rows)) for g in (gain_one, gain_two)]
    parts = [router[...].astype(F32)]
    if pad > experts:
        parts.append(jnp.zeros((pad - experts, rows), F32))
    parts += gains + [jnp.zeros((EXT - pad - 16, rows), F32)]
    out[:, QKV:] = jnp.concatenate(parts, axis=0).T.astype(BF)


def run_pack(q, k, v, router, gain_one, gain_two):
    rows, experts = router.shape
    return pl.pallas_call(
        functools.partial(pack_kernel, experts),
        name="pack",
        out_shape=sds((rows, QKV + EXT), BF),
        in_specs=[VMEM] * 6,
        out_specs=VMEM,
        compiler_params=params(),
        cost_estimate=cost(0.01),
    )(q, k, v, router.T, gain_one, gain_two)


def attention_kernel(size, rows, plan, me, tok, seg_row, seg_col, *rest):
    refs, rest = rest[:-7], rest[-7:]
    low_out, qkv_out, ctx_out, prob_out, ext_out, w, sems = rest
    copies = fetch(me[0], refs, plan, lambda s: w.at[s], sems, rows, size)
    seq = tok.shape[0]
    x = tok[...].astype(F32)
    factor = lax.rsqrt(jnp.mean(x * x, axis=-1, keepdims=True) + norm_eps)
    normed = x * factor
    same = seg_col[...] == seg_row[...]
    key_at = lax.broadcasted_iota(jnp.int32, (seq, seq), 0)
    query_at = lax.broadcasted_iota(jnp.int32, (seq, seq), 1)
    allowed = jnp.where(same & (key_at <= query_at), 0.0, masked_score)
    allowed = jnp.concatenate([allowed] * GROUPS, axis=1)
    for c in copies:
        c.wait()
    ext = w[:, QKV:].astype(F32).T[: ext_out.shape[0], :]
    ext_out[...] = ext
    experts_pad = ext_out.shape[0] - 16
    gain = ext[experts_pad : experts_pad + 1, :]
    low = (normed * gain).astype(BF)
    step = 512
    for j in range(low.shape[1] // step):
        at = slice(j * step, (j + 1) * step)
        low_out[at, :] = low[:, at].astype(F32).T.astype(BF)
    for j in range(QKV // step):
        at = slice(j * step, (j + 1) * step)
        part = dot(low, w[:, at])
        qkv_out[at, :] = part.T.astype(BF)
    for h in range(KV_HEADS):
        q = jnp.concatenate(
            [
                qkv_out[(GROUPS * h + g) * HEAD_DIM : (GROUPS * h + g + 1) * HEAD_DIM, :]
                for g in range(GROUPS)
            ],
            axis=1,
        )
        k = qkv_out[QW + h * HEAD_DIM : QW + (h + 1) * HEAD_DIM, :]
        v = qkv_out[QW + KW + h * HEAD_DIM : QW + KW + (h + 1) * HEAD_DIM, :]
        scores = dot(k, q, 0, 0) * HEAD_DIM ** (-0.5)
        scores = jnp.where(allowed < 0.0, masked_score, scores)
        top = jnp.max(scores, axis=0, keepdims=True)
        shifted = jnp.exp(scores - top)
        probs = (shifted * (1.0 / jnp.sum(shifted, axis=0, keepdims=True))).astype(BF)
        prob_out[h] = probs
        ctx = dot(v, probs).astype(BF)
        for g in range(GROUPS):
            at = (GROUPS * h + g) * HEAD_DIM
            ctx_out[at : at + HEAD_DIM, :] = ctx[:, g * seq : (g + 1) * seq]


def run_attention(me, tokens, seg_row, seg_col, pieces, size, ext_rows):
    seq, width = tokens.shape
    rows = width // size
    arrays, plan = pieces
    return pl.pallas_call(
        functools.partial(attention_kernel, size, rows, plan),
        name="attention",
        out_shape=[
            sds((width, seq), BF),
            sds((QKV, seq), BF),
            sds((QW, seq), BF),
            sds((KV_HEADS, seq, GROUPS * seq), BF),
            sds((ext_rows, width), F32),
        ],
        in_specs=[SMEM, VMEM, VMEM, VMEM] + [ANY] * len(arrays),
        out_specs=[VMEM] * 5,
        scratch_shapes=[
            pltpu.VMEM((width, QKV + EXT), BF),
            pltpu.SemaphoreType.DMA((len(plan),)),
        ],
        compiler_params=params(),
        cost_estimate=cost(0.01),
    )(me, tokens, seg_row, seg_col, *arrays)


def residual_kernel(size, rows, plan, me, tok, ctx, ext, place, *rest):
    refs, (res_out, low_out, w, sems) = rest[:-4], rest[-4:]
    copies = fetch(me[0], refs, plan, lambda s: w.at[s], sems, rows, size)
    experts_pad = ext.shape[0] - 16
    for c in copies:
        c.wait()
    res = tok[...].astype(F32) + dot(ctx[...], w[...], 0, 0)
    res_out[...] = res
    factor = lax.rsqrt(jnp.mean(res * res, axis=-1, keepdims=True) + norm_eps)
    seq = res.shape[0]
    low_out[:seq, :] = (res * factor * ext[experts_pad + 8 : experts_pad + 9, :]).astype(BF)
    low_out[seq:, :] = place[...]


def run_residual(me, tokens, ctx, ext, place, pieces, size):
    seq, width = tokens.shape
    rows = QW // size
    arrays, plan = pieces
    return pl.pallas_call(
        functools.partial(residual_kernel, size, rows, plan),
        name="residual",
        out_shape=[sds((seq, width), F32), sds((seq + EXTRA, width), BF)],
        in_specs=[SMEM, VMEM, VMEM, VMEM, VMEM] + [ANY] * len(arrays),
        out_specs=[VMEM] * 2,
        scratch_shapes=[pltpu.VMEM((QW, width), BF), pltpu.SemaphoreType.DMA((len(plan),))],
        compiler_params=params(),
        cost_estimate=cost(0.01),
    )(me, tokens, ctx, ext, place, *arrays)


def slot_of(block, seq, width):
    across = width // seq
    row, col = block // across * 8, block % across * seq
    return slice(row, row + 8), slice(col, col + seq)


def router_kernel(owners, per, z, ext, *rest):
    rows, rest = rest[:owners], rest[owners:]
    pos_out, p_out, own_out, all_p, all_pos = rest
    experts_pad = ext.shape[0] - 16
    seq, width = rows[0].shape[0] - EXTRA, rows[0].shape[1]
    router = ext[:experts_pad, :].astype(BF)
    at = z[0] * per
    for r in range(owners):
        logits = dot(router, rows[r][:seq, :], 1, 1)
        spots = rows[r][seq:, :].astype(F32)
        for b in range(experts_pad // 8):
            of, to = slot_of(b, seq, width)
            all_pos[b * 8 : (b + 1) * 8, :] = spots[of, to]
        where = all_pos[...]
        named = where >= 0.0
        logits = jnp.where(named, logits, masked_score)
        top = jnp.max(logits, axis=0, keepdims=True)
        shifted = jnp.where(named, jnp.exp(logits - top), 0.0)
        probs = shifted / jnp.sum(shifted, axis=0, keepdims=True)
        all_p[...] = probs
        if r == 0:
            own_out[...] = probs
        for l in range(per):
            p_out[l, r : r + 1, :] = all_p[pl.ds(at + l, 1), :]
            pos_out[l, r : r + 1, :] = all_pos[pl.ds(at + l, 1), :].astype(jnp.int32)


def run_router(z, ext, rows, per):
    owners = len(rows)
    seq = rows[0].shape[0] - EXTRA
    experts_pad = ext.shape[0] - 16
    return pl.pallas_call(
        functools.partial(router_kernel, owners, per),
        name="router",
        out_shape=[
            sds((per, owners, seq), jnp.int32),
            sds((per, owners, seq), F32),
            sds((experts_pad, seq), F32),
        ],
        in_specs=[SMEM, VMEM] + [VMEM] * owners,
        out_specs=[VMEM] * 3,
        scratch_shapes=[pltpu.VMEM((experts_pad, seq), F32)] * 2,
        compiler_params=params(),
        cost_estimate=cost(0.01),
    )(z, ext, *rows)


def load_rows(owners, z, xs, cs, xv, cv, sem_x, sem_c):
    seq = xv.shape[1]
    copies = []
    for r in range(owners):
        start = pl.multiple_of(owner_at(z[0], r, owners) * seq, seq)
        copies.append(pltpu.make_async_copy(xs[r].at[pl.ds(0, seq)], xv.at[r], sem_x.at[r]))
        copies.append(pltpu.make_async_copy(cs.at[pl.ds(start, seq)], cv.at[r], sem_c.at[r]))
    for c in copies:
        c.start()

    def wait():
        for c in copies:
            c.wait()

    return wait


def pick_rows(owners, cap, number, pos, p, xv, cv, xr, cr, prow):
    seq = xv.shape[1]
    slot = lax.broadcasted_iota(jnp.int32, (cap, seq), 0)
    for r in range(owners):
        hot = pos[number, r : r + 1, :] == slot
        low_hot = jnp.where(hot, 1.0, 0.0).astype(BF)
        at = pl.ds(r * cap, cap)
        xr[at, :] = dot(low_hot, xv[r]).astype(BF)
        cr[at, :] = dot(low_hot, cv[r]).astype(BF)
        prow[at, :] = jnp.sum(jnp.where(hot, p[number, r : r + 1, :], 0.0), axis=1, keepdims=True)


def through_expert(owners, cap, number, pos, xr, cr, prow, w, hp, gg, ug, gate, gate_out):
    ff = w.shape[2]
    step = ff // HALVES
    gate[...] = jnp.zeros_like(gate)
    for j in range(HALVES):
        cols = slice(j * step, (j + 1) * step)
        gate_pre = dot(xr[...], w[0, :, cols])
        up_pre = dot(xr[...], w[1, :, cols])
        back = dot(cr[...], w[2, :, cols])
        probs = prow[...]
        s = jax.nn.sigmoid(gate_pre)
        silu = gate_pre * s
        hidden = silu * up_pre
        gate[...] += jnp.sum(hidden * back, axis=1, keepdims=True)
        hp[:, cols] = (hidden * probs).astype(BF)
        back = back * probs
        gg[:, cols] = (back * up_pre * (s + silu * (1.0 - s))).astype(BF)
        ug[:, cols] = (back * silu).astype(BF)
    seq = pos.shape[2]
    slot = lax.broadcasted_iota(jnp.int32, (cap, seq), 0)
    for r in range(owners):
        hot = pos[number, r : r + 1, :] == slot
        at = pl.ds(r * cap, cap)
        gate_out[r : r + 1, :] = jnp.sum(jnp.where(hot, gate[at, :], 0.0), axis=0, keepdims=True)


def load_weights(me, refs, plan, w, sems, slot_at, rows, size):
    shards = [ref.at[:, slot_at] if len(refs) == 1 else ref.at[slot_at] for ref in refs]
    return fetch(me, shards, plan, lambda s: w.at[:, s, :], sems, rows, size)


def weight_grads(xr, cr, hp, gg, ug, g, grads, sems, slot_at, rows, size):
    width = xr.shape[1]
    tile = width // HALVES
    for j in range(HALVES):
        cols = slice(j * tile, (j + 1) * tile)
        g[0, cols, :] = dot(xr[:, cols], gg[...], 0, 0).astype(BF)
        g[1, cols, :] = dot(xr[:, cols], ug[...], 0, 0).astype(BF)
        g[2, cols, :] = dot(cr[:, cols], hp[...], 0, 0).astype(BF)
    copies = [
        pltpu.make_async_copy(g.at[:, pl.ds(i * rows, rows), :], grads.at[i, slot_at], sems.at[i])
        for i in range(size)
    ]
    for c in copies:
        c.start()
    return copies


def rows_back(w, gg, ug, bv):
    tile = bv.shape[1] // HALVES
    for j in range(HALVES):
        cols = slice(j * tile, (j + 1) * tile)
        total = dot(gg[...], w[0, cols, :], 1, 1) + dot(ug[...], w[1, cols, :], 1, 1)
        bv[:, cols] = total.astype(BF)


def rows_out(w, hp, ov):
    tile = ov.shape[1] // HALVES
    for j in range(HALVES):
        cols = slice(j * tile, (j + 1) * tile)
        ov[:, cols] = dot(hp[...], w[cols, :], 1, 1).astype(BF)


def experts_kernel(size, rows, owners, cap, first, many, plan, count, me, z, pos, p, cs, *rest):
    xs, refs, rest = rest[:owners], rest[owners : owners + count], rest[owners + count :]
    if first > 0:
        rest = rest[1:]
    out_rows, back_rows, gate_out, grads = rest[:4]
    xv, cv, w, xr, cr, prow, hp, gg, ug, gate, ov, bv, g, sem_x, sem_c, sem_w, sem_g, sem_o = rest[4:]
    wait_rows = load_rows(owners, z, xs, cs, xv, cv, sem_x, sem_c)

    def load(i):
        return load_weights(me[0], refs, plan, w.at[i % 2], sem_w.at[i % 2], i, rows, size)

    coming = load(0)
    leaving = []
    for i in range(many):
        here = i % 2
        number = first + i
        if i == 0:
            wait_rows()
        pick_rows(owners, cap, number, pos, p, xv, cv, xr, cr, prow)
        for c in coming:
            c.wait()
        if i + 1 < many:
            coming = load(i + 1)
        if len(leaving) > 1:
            for c in leaving[i - 2]:
                c.wait()
        through_expert(
            owners, cap, number, pos, xr, cr, prow, w.at[here], hp, gg, ug, gate, gate_out.at[i]
        )
        copies = weight_grads(
            xr, cr, hp, gg, ug, g.at[here], grads, sem_g.at[here], number, rows, size
        )
        rows_back(w.at[here], gg, ug, bv.at[here])
        copies.append(pltpu.make_async_copy(bv.at[here], back_rows.at[i], sem_o.at[here, 0]))
        copies[-1].start()
        rows_out(w.at[here, 2], hp, ov.at[here])
        copies.append(pltpu.make_async_copy(ov.at[here], out_rows.at[i], sem_o.at[here, 1]))
        copies[-1].start()
        leaving.append(copies)
    for copies in leaving[-2:]:
        for c in copies:
            c.wait()


def run_experts(me, z, pos, p, xs, cs, pieces, buffer, size, first, many, cap):
    per, owners, seq = pos.shape
    width = xs[0].shape[1]
    refs, plan = pieces
    ff = refs[0].shape[-1]
    rows = width // size
    total = owners * cap
    given = [me, z, pos, p, cs, *xs, *refs] + ([] if buffer is None else [buffer])
    return pl.pallas_call(
        functools.partial(
            experts_kernel, size, rows, owners, cap, first, many, plan, len(refs)
        ),
        name="experts",
        out_shape=[
            sds((many, total, width), BF),
            sds((many, total, width), BF),
            sds((many, owners, seq), F32),
            sds((size, per, 3, rows, ff), BF),
        ],
        in_specs=[SMEM, SMEM, VMEM, VMEM] + [ANY] * (len(given) - 4),
        out_specs=[ANY, ANY, VMEM, ANY],
        input_output_aliases={} if buffer is None else {len(given) - 1: 3},
        scratch_shapes=[
            pltpu.VMEM((owners, seq, width), BF),
            pltpu.VMEM((owners, seq, width), BF),
            pltpu.VMEM((2, 3, width, ff), BF),
            pltpu.VMEM((total, width), BF),
            pltpu.VMEM((total, width), BF),
            pltpu.VMEM((total, 1), F32),
            pltpu.VMEM((total, ff), BF),
            pltpu.VMEM((total, ff), BF),
            pltpu.VMEM((total, ff), BF),
            pltpu.VMEM((total, 1), F32),
            pltpu.VMEM((2, total, width), BF),
            pltpu.VMEM((2, total, width), BF),
            pltpu.VMEM((2, 3, width, ff), BF),
            pltpu.SemaphoreType.DMA((owners,)),
            pltpu.SemaphoreType.DMA((owners,)),
            pltpu.SemaphoreType.DMA((2, len(plan))),
            pltpu.SemaphoreType.DMA((2, size)),
            pltpu.SemaphoreType.DMA((2, 2)),
        ],
        compiler_params=params(),
        cost_estimate=cost(0.01),
    )(*given)


def combined_rows(per, cap, pos, r, rows):
    seq = pos.shape[2]
    slot = lax.broadcasted_iota(jnp.int32, (cap, seq), 0)
    hot = jnp.concatenate(
        [jnp.where(pos[l, pl.ds(r, 1), :] == slot, 1.0, 0.0).astype(BF) for l in range(per)], axis=0
    )
    total, at = 0.0, 0
    for group in rows:
        count = group.shape[0] * cap
        total = total + dot(hot[at : at + count], group[...].reshape(count, -1), 0, 0)
        at += count
    return total.astype(BF)


def combine_back_kernel(start, owners, per, cap, experts_pad, groups, z, pos, *rest):
    rows, gates, rest = rest[:groups], rest[groups : 2 * groups], rest[2 * groups :]
    outs, block = rest[:owners], rest[owners]
    step = pl.program_id(0)
    r = step + start
    seq, width = pos.shape[2], outs[0].shape[1]
    total = combined_rows(per, cap, pos, r, rows)
    block[...] = jnp.zeros_like(block)
    gates = [group.at[l] for group in gates for l in range(group.shape[0])]
    for l in range(per):
        block[pl.ds(z[0] * per + l, 1), :] = gates[l][pl.ds(r, 1), :]
    value = block[...]
    high = value.astype(BF)
    low = (value - high.astype(F32)).astype(BF)
    for o in range(owners):

        @pl.when(step == o)
        def _():
            outs[o][:seq, :] = total
            outs[o][seq:, :] = jnp.zeros((EXTRA, width), BF)
            both = jnp.concatenate([high, low], axis=0).astype(F32)
            for row in range(EXTRA // 8):
                across = width // seq
                blocks = [
                    both[(row * across + b) * 8 : (row * across + b + 1) * 8, :]
                    if row * across + b < 2 * experts_pad // 8
                    else jnp.zeros((8, seq), F32)
                    for b in range(across)
                ]
                outs[o][seq + row * 8 : seq + row * 8 + 8, :] = jnp.concatenate(
                    blocks, axis=1
                ).astype(BF)


def whole(shape):
    return pl.BlockSpec(shape, lambda r: (0,) * len(shape))


def run_combine_back(z, pos, rows, gates, cap, experts_pad, start, owners):
    per, _, seq = pos.shape
    width = rows[0].shape[2]
    shapes = [sds((seq + EXTRA, width), BF)] * owners
    return pl.pallas_call(
        functools.partial(combine_back_kernel, start, owners, per, cap, experts_pad, len(rows)),
        name="combine_back",
        grid=(owners,),
        out_shape=shapes,
        in_specs=[SMEM, whole(pos.shape)]
        + [pl.BlockSpec((a.shape[0], cap, width), lambda r: (0, r + start, 0)) for a in rows]
        + [whole(a.shape) for a in gates],
        out_specs=[whole(s.shape) for s in shapes],
        scratch_shapes=[pltpu.VMEM((experts_pad, seq), F32)],
        compiler_params=params(),
        cost_estimate=cost(0.01),
    )(z, pos, *rows, *gates)


def combine_out_kernel(owners, per, cap, pos, *rest):
    rows, outs = rest[:-owners], rest[-owners:]
    r = pl.program_id(0)
    total = combined_rows(per, cap, pos, r, rows)
    for o in range(owners):

        @pl.when(r == o)
        def _():
            outs[o][...] = total


def run_combine_out(pos, rows, cap):
    per, owners, seq = pos.shape
    width = rows[0].shape[2]
    return pl.pallas_call(
        functools.partial(combine_out_kernel, owners, per, cap),
        name="combine_out",
        grid=(owners,),
        out_shape=[sds((seq, width), BF)] * owners,
        in_specs=[whole(pos.shape)]
        + [pl.BlockSpec((a.shape[0], cap, width), lambda r: (0, r, 0)) for a in rows],
        out_specs=[whole((seq, width))] * owners,
        compiler_params=params(),
        cost_estimate=cost(0.01),
    )(pos, *rows)


def join_kernel(owners, own, *rest):
    more, (parts, out) = rest[:-2], rest[-2:]
    rows, cols = own.shape
    total = own[...].astype(F32)
    for piece in more:
        total = total + piece[...].astype(F32)
    total = total.astype(BF)
    low = parts.shape[0] // owners
    summed = 0.0
    for r in range(owners):
        summed = summed + parts[r * low : (r + 1) * low, :].astype(F32)
    summed = summed.astype(BF)
    wide = summed.shape[1] // owners
    for r in range(owners):
        out[r * rows : (r + 1) * rows, :cols] = total
        for k in range(owners):
            at = r * rows + k * low
            out[at : at + low, cols:] = summed[:, k * wide : (k + 1) * wide]


def run_join(pieces, parts, owners):
    rows, cols = pieces[0].shape
    return pl.pallas_call(
        functools.partial(join_kernel, owners),
        name="join",
        out_shape=sds((owners * rows, cols + parts.shape[1] // owners), BF),
        in_specs=[VMEM] * (len(pieces) + 1),
        out_specs=VMEM,
        compiler_params=params(),
        cost_estimate=cost(0.01),
    )(*pieces, parts)


def finish_kernel(owners, total, query, key, value, out, router, gain_one, gain_two):
    rows = query.shape[0]
    wide, narrow = QW // owners, KW // owners
    one = wide + 2 * narrow
    low, out_wide = rows // owners, out.shape[1] // owners
    ext_sum = 0.0
    for j in range(owners):
        block = total[j * rows : (j + 1) * rows, :].astype(F32)
        query[:, j * wide : (j + 1) * wide] = block[:, :wide]
        key[:, j * narrow : (j + 1) * narrow] = block[:, wide : wide + narrow]
        value[:, j * narrow : (j + 1) * narrow] = block[:, wide + narrow : one]
        ext_sum = ext_sum + block[:, one : one + EXT]
        for k in range(owners):
            out[j * low : (j + 1) * low, k * out_wide : (k + 1) * out_wide] = block[
                k * low : (k + 1) * low, one + EXT :
            ]
    ext_sum = ext_sum.T
    experts = router.shape[0]
    pad = -(-experts // 8) * 8
    router[...] = ext_sum[:experts, :]
    gain_one[...] = ext_sum[pad, :]
    gain_two[...] = ext_sum[pad + 8, :]


def run_finish(total, owners, experts):
    rows = total.shape[0] // owners
    width = (total.shape[1] - EXT - (QW + 2 * KW) // owners) * owners
    return pl.pallas_call(
        functools.partial(finish_kernel, owners),
        name="finish",
        out_shape=[
            sds((rows, QW), F32),
            sds((rows, KW), F32),
            sds((rows, KW), F32),
            sds((rows, width), F32),
            sds((experts, rows), F32),
            sds((rows,), F32),
            sds((rows,), F32),
        ],
        in_specs=[VMEM],
        out_specs=[VMEM] * 7,
        compiler_params=params(),
        cost_estimate=cost(0.01),
    )(total)


def second_kernel(
    size, rows, owners, per, plan, count, me, own_p, ext, low_two, res, cot, ctx, *rest
):
    backs, rest = rest[:owners], rest[owners:]
    refs, rest = rest[:count], rest[count:]
    res_grad, ctx_grad, ext_grad, own, other, w, g, gate, sems, sems_g = rest
    copies = fetch(me[0], refs, plan, lambda s: w.at[s], sems, rows, size)
    experts_pad = own_p.shape[0]
    seq, width = res.shape
    arrived = backs[0][seq:, :].astype(F32)
    for r in range(1, owners):
        arrived = arrived + backs[r][seq:, :].astype(F32)
    for b in range(experts_pad // 8):
        high_at = slot_of(b, seq, width)
        low_at = slot_of(b + experts_pad // 8, seq, width)
        gate[b * 8 : (b + 1) * 8, :] = arrived[high_at] + arrived[low_at]
    p = own_p[...]
    gate_grad = gate[...]
    weighted = jnp.sum(p * gate_grad, axis=0, keepdims=True)
    logit_grad = (p * (gate_grad - weighted)).astype(BF)
    router = ext[:experts_pad, :].astype(BF)
    ext_grad[:experts_pad, :] = dot(logit_grad, low_two[:seq, :])
    two = dot(logit_grad, router, 0, 0)
    for r in range(owners):
        two = two + backs[r][:seq, :].astype(F32)
    values = res[...]
    factor = lax.rsqrt(jnp.mean(values * values, axis=-1, keepdims=True) + norm_eps)
    normed = values * factor
    ext_grad[experts_pad:, :] = jnp.broadcast_to(
        jnp.sum(two * normed, axis=0, keepdims=True), (16, normed.shape[1])
    )
    scaled = two * ext[experts_pad + 8 : experts_pad + 9, :]
    inward = factor * (scaled - normed * jnp.mean(scaled * normed, axis=-1, keepdims=True))
    total = cot[...].astype(F32) + inward
    res_grad[...] = total
    low = total.astype(BF)
    step = QW // 4
    for j in range(4):
        at = slice(j * step, (j + 1) * step)
        g[at, :] = dot(ctx[at, :], low).astype(BF)
    copies_g = store_parts(me[0], lambda s: g.at[s], pair_refs(own, other, size), sems_g, rows, size)
    for c in copies:
        c.wait()
    for j in range(4):
        at = slice(j * step, (j + 1) * step)
        ctx_grad[at, :] = dot(w[at, :], low, 1, 1).astype(BF)
    for c in copies_g:
        c.wait()


def run_second(me, own_p, ext, low_two, res, cot, ctx, backs, pieces, size, per):
    owners = len(backs)
    arrays, plan = pieces
    seq, width = res.shape
    rows = QW // size
    experts_pad = own_p.shape[0]
    return pl.pallas_call(
        functools.partial(second_kernel, size, rows, owners, per, plan, len(arrays)),
        name="second_back",
        out_shape=[
            sds((seq, width), F32),
            sds((QW, seq), BF),
            sds((experts_pad + 16, width), F32),
            sds((size if size != 8 else 4, rows, width), BF),
            sds((4, rows, width), BF),
        ],
        in_specs=[SMEM] + [VMEM] * (6 + owners) + [ANY] * len(arrays),
        out_specs=[VMEM] * 3 + [ANY] * 2,
        scratch_shapes=[
            pltpu.VMEM((QW, width), BF),
            pltpu.VMEM((QW, width), BF),
            pltpu.VMEM((experts_pad, seq), F32),
            pltpu.SemaphoreType.DMA((len(plan),)),
            pltpu.SemaphoreType.DMA((size,)),
        ],
        compiler_params=params(),
        cost_estimate=cost(0.01),
    )(me, own_p, ext, low_two, res, cot, ctx, *backs, *arrays)


def heads_kernel(ctx_grad, qkv, probs, back, blocks):
    seq = qkv.shape[1]
    scale = HEAD_DIM ** (-0.5)
    for h in range(KV_HEADS):

        def heads(ref):
            return jnp.concatenate(
                [
                    ref[(GROUPS * h + i) * HEAD_DIM : (GROUPS * h + i + 1) * HEAD_DIM, :]
                    for i in range(GROUPS)
                ],
                axis=1,
            )

        upstream = heads(ctx_grad)
        q = heads(qkv)
        k = qkv[QW + h * HEAD_DIM : QW + (h + 1) * HEAD_DIM, :]
        v = qkv[QW + KW + h * HEAD_DIM : QW + KW + (h + 1) * HEAD_DIM, :]
        low_p = probs[h]
        weights = low_p.astype(F32)
        prob_grad = dot(v, upstream, 0, 0)
        inner = jnp.sum(prob_grad * weights, axis=0, keepdims=True)
        score_grad = (weights * (prob_grad - inner)).astype(BF)
        value_grad = dot(upstream, low_p, 1, 1)
        key_grad = dot(q, score_grad, 1, 1) * scale
        query_grad = dot(k, score_grad) * scale
        back[QW + h * HEAD_DIM : QW + (h + 1) * HEAD_DIM, :] = key_grad.astype(BF)
        back[QW + KW + h * HEAD_DIM : QW + KW + (h + 1) * HEAD_DIM, :] = value_grad.astype(BF)
        for i in range(GROUPS):
            at = (GROUPS * h + i) * HEAD_DIM
            back[at : at + HEAD_DIM, :] = query_grad[:, i * seq : (i + 1) * seq].astype(BF)
    owners = blocks.shape[0] // seq
    wide, slim = QW // owners, KW // owners
    for j in range(owners):
        block = jnp.concatenate(
            [
                back[j * wide : (j + 1) * wide, :],
                back[QW + j * slim : QW + (j + 1) * slim, :],
                back[QW + KW + j * slim : QW + KW + (j + 1) * slim, :],
            ],
            axis=0,
        )
        blocks[j * seq : (j + 1) * seq, :] = block.astype(F32).T.astype(BF)


def run_heads(ctx_grad, qkv, probs, owners):
    seq = qkv.shape[1]
    return pl.pallas_call(
        heads_kernel,
        name="heads_back",
        out_shape=[sds((QKV, seq), BF), sds((owners * seq, QKV // owners), BF)],
        in_specs=[VMEM] * 3,
        out_specs=[VMEM] * 2,
        compiler_params=params(),
        cost_estimate=cost(0.01),
    )(ctx_grad, qkv, probs)


def first_kernel(size, rows, plan, me, back, tok, ext, ext_grad, res_grad, *rest):
    refs, (tok_grad, ext_cols, w, sems) = rest[:-4], rest[-4:]
    copies = fetch(me[0], refs, plan, lambda s: w.at[s], sems, rows, size)
    for c in copies:
        c.wait()
    one = dot(back[...], w[:, :QKV], 0, 1)
    x = tok[...].astype(F32)
    factor = lax.rsqrt(jnp.mean(x * x, axis=-1, keepdims=True) + norm_eps)
    normed = x * factor
    experts_pad = ext.shape[0] - 16
    gain = ext[experts_pad : experts_pad + 1, :]
    gain_grad = jnp.sum(one * normed, axis=0, keepdims=True)
    packed = jnp.concatenate(
        [
            ext_grad[:experts_pad, :],
            jnp.broadcast_to(gain_grad, (8, gain_grad.shape[1])),
            ext_grad[experts_pad + 8 :, :],
            jnp.zeros((EXT - experts_pad - 16, gain_grad.shape[1]), F32),
        ],
        axis=0,
    )
    ext_cols[...] = packed.T.astype(BF)
    scaled = one * gain
    inward = factor * (scaled - normed * jnp.mean(scaled * normed, axis=-1, keepdims=True))
    tok_grad[...] = res_grad[...] + inward


def run_first(me, back, tokens, ext, ext_grad, res_grad, pieces, size):
    arrays, plan = pieces
    seq, width = tokens.shape
    rows = width // size
    return pl.pallas_call(
        functools.partial(first_kernel, size, rows, plan),
        name="first_back",
        out_shape=[sds((seq, width), F32), sds((width, EXT), BF)],
        in_specs=[SMEM] + [VMEM] * 5 + [ANY] * len(arrays),
        out_specs=[VMEM] * 2,
        scratch_shapes=[
            pltpu.VMEM((width, QKV + EXT), BF),
            pltpu.SemaphoreType.DMA((len(plan),)),
        ],
        compiler_params=params(),
        cost_estimate=cost(60),
    )(me, back, tokens, ext, ext_grad, res_grad, *arrays)


def project_kernel(size, rows, me, low_all, back_all, ext_cols, *rest):
    grads, (g, sems_g) = rest[:-2], rest[-2:]
    owners, _, seq = low_all.shape
    cols = back_all.shape[1]
    g[:, cols:] = ext_cols[...]
    total = 0.0
    for r in range(owners):
        total = total + dot(low_all[r], back_all[r * seq : (r + 1) * seq, :])
    g[:, :cols] = total.astype(BF)
    if size == 8:
        grads = [grads[4].at[i // 2] if i % 2 else grads[i // 2] for i in range(size)]
    copies_g = store_parts(me[0], lambda s: g.at[s], grads, sems_g, rows, size)
    for c in copies_g:
        c.wait()


def run_project(me, low_all, back_all, ext_cols, size):
    width, cols = low_all.shape[1], back_all.shape[1] + EXT
    rows = width // size
    grads = part_shapes(size, (rows, cols))
    return pl.pallas_call(
        functools.partial(project_kernel, size, rows),
        name="project_back",
        out_shape=grads,
        in_specs=[SMEM] + [VMEM] * 3,
        out_specs=[ANY] * len(grads),
        scratch_shapes=[pltpu.VMEM((width, cols), BF), pltpu.SemaphoreType.DMA((size,))],
        compiler_params=params(),
        cost_estimate=cost(60),
    )(me, low_all, back_all, ext_cols)


def split_groups(per):
    cut = max(1, (2 * per) // 5)
    return [(0, cut), (cut, per)]


def body(
    tokens,
    segment_ids,
    expert_choices,
    attn_gain,
    query_weight,
    key_weight,
    value_weight,
    output_weight,
    ffn_gain,
    router_weight,
    expert_gate,
    expert_up,
    expert_down,
    cotangent,
):
    size = lax.axis_size("dp")
    owners = lax.axis_size("expert")
    paired = size == 8 and owners == 4
    me = lax.axis_index("dp").astype(jnp.int32).reshape(1)
    z = lax.axis_index("expert").astype(jnp.int32).reshape(1)
    seq, width = tokens.shape
    per = expert_gate.shape[0]
    experts = per * owners
    experts_pad = -(-experts // 8) * 8
    capacity = (seq * TOP * 9 + 8 * experts - 1) // (8 * experts)
    cap = -(-capacity // 16) * 16
    slim = query_weight.shape[0]
    segments = segment_ids.reshape(seq, 1)
    (a_first, a_last), (b_first, b_last) = split_groups(per)

    cots = lax.all_gather(cotangent, "expert", axis=0, tiled=True)
    packed = run_pack(query_weight, key_weight, value_weight, router_weight, attn_gain, ffn_gain)
    shards = jnp.stack([expert_gate, expert_up, jnp.swapaxes(expert_down, 1, 2)], axis=1)
    a_shard, b_shard = shards[a_first:a_last], shards[b_first:b_last]

    ids = jnp.arange(experts_pad, dtype=jnp.int32)
    hot = jnp.any(expert_choices[:, None, :] == ids[None, :, None], axis=2)
    hot = hot.astype(BF).T
    at = jnp.arange(seq, dtype=jnp.int32)
    earlier = (at[:, None] < at[None, :]).astype(BF)
    place = jnp.dot(hot, earlier, preferred_element_type=F32)
    place = jnp.where(hot > 0, place, -1.0).astype(BF)
    across = width // seq
    place = jnp.pad(place, ((0, EXTRA * across - experts_pad), (0, 0)))
    place = place.reshape(EXTRA // 8, across, 8, seq).swapaxes(1, 2).reshape(EXTRA, width)

    if paired:
        half = slim // 2
        full = [(0, 0, slim), (2, 0, slim), (4, 0, slim), (6, 0, slim)]
        full += [(m + 1, first, rows) for m, first, rows in full]
        split = [(0, 0, slim), (2, 0, slim), (4, 0, slim), (6, 0, half), (6, half, half)]
        split += [(m + 1, first, rows) for m, first, rows in split]
        order = segment_ids
        qx, qy, q1 = (swap(packed, bit, size) for bit in (2, 4, 1))
        order, qx, qy, q1 = wait(order, qx, qy, q1)
        qa, qb = swap(qx[:half], 4, size), swap(qy[half:], 2, size)
        q3 = swap(qx, 1, size)
        o_shard = hold(order, output_weight)
        ox, oy = swap(o_shard, 2, size), swap(o_shard, 4, size)
        order, qa, qb, q3 = wait(order, qa, qb, q3)
        q5, q6, q7 = swap(hold(order, qy), 1, size), swap(qa, 1, size), swap(qb, 1, size)
        order, q5, q6, q7, ox, oy = wait(order, q5, q6, q7, ox, oy)
        qkv_pieces = ([packed, qx, qy, qa, qb, q1, q3, q5, q6, q7], split)
        oc, o3, o5 = swap(oy, 2, size), swap(ox, 1, size), swap(oy, 1, size)
        ay, o1 = swap(hold(order, a_shard), 4, size), swap(hold(order, output_weight), 1, size)
        low_one, qkv, ctx, probs, extra = run_attention(
            me, hold(order, tokens), segment_ids, segments, qkv_pieces, size, experts_pad + 16
        )
        order, ctx, oc, o3, o5, o1 = wait(order, ctx, oc, o3, o5, o1)
        o7, ax = swap(oc, 1, size), swap(hold(order, a_shard), 2, size)
        order, o7, cots = wait(order, o7, cots)
        out_pieces = ([output_weight, ox, oy, oc, o1, o3, o5, o7], full)
        res, low_two = run_residual(
            me, hold(order, tokens), ctx, extra, place, out_pieces, size
        )
        order, low_two, ay = wait(order, low_two, ay)
        far, near = cross(low_two, 2), cross(low_two, 1)
        held = hold(order, b_shard)
        by, bx = swap(held, 4, size), swap(held, 2, size)
        order, ax = wait(order, ax)
        ac = swap(ax, 4, size)
        order, far, near = wait(order, far, near)
        middle = along(hold(order, low_two), [(1, 2), (2, 1)])
        passed = along(far, [(2, 3), (1, 0)])
        order, middle, passed, by, bx = wait(order, middle, passed, by, bx)
        inner = (z[0] == 1) | (z[0] == 2)
        xs = [low_two, near, far, jnp.where(inner, middle, passed)]
        low_all = lax.all_gather(hold(order, low_one), "expert", axis=0, tiled=True)
        ba, bb = swap(bx[..., :half, :], 4, size), swap(by[..., half:, :], 2, size)
        a1, a3, a5 = (swap(hold(order, v), 1, size) for v in (a_shard, ax, ay))
        pos, p, own_p = run_router(z, hold(order, extra), xs, per)
        order, p, ac, a1, a3, a5 = wait(order, p, ac, a1, a3, a5)
        a7, b3, b5 = swap(ac, 1, size), swap(hold(order, bx), 1, size), swap(hold(order, by), 1, size)
        order, a7 = wait(order, a7)
        b1 = swap(hold(order, b_shard), 1, size)
        a_pieces = ([a_shard, ax, ay, ac, a1, a3, a5, a7], full)
    else:
        qkv_pieces = plain_shards(packed, size)
        out_pieces = plain_shards(output_weight, size)
        a_pieces, b_pieces = plain_shards(a_shard, size), plain_shards(b_shard, size)
        low_one, qkv, ctx, probs, extra = run_attention(
            me, tokens, segment_ids, segments, qkv_pieces, size, experts_pad + 16
        )
        res, low_two = run_residual(me, tokens, ctx, extra, place, out_pieces, size)
        xs = plain_owners(low_two, owners)
        low_all = lax.all_gather(low_one, "expert", axis=0, tiled=True)
        pos, p, own_p = run_router(z, extra, xs, per)
        order = p
    low_all = low_all.reshape(owners, width, seq)

    a_rows = run_experts(
        me, z, pos, hold(order, p), xs, cots, a_pieces, None, size, a_first, a_last - a_first, cap
    )
    if paired:
        order, a_gate, ba, bb, b1, b3, b5 = wait(order, a_rows[2], ba, bb, b1, b3, b5)
        b6, b7 = swap(ba, 1, size), swap(bb, 1, size)
        order, b6, b7 = wait(order, b6, b7)
        b_pieces = ([b_shard, bx, by, ba, bb, b1, b3, b5, b6, b7], split)
    b_rows = run_experts(
        me, z, pos, hold(order, p), xs, cots, b_pieces, a_rows[3], size, b_first, b_last - b_first, cap
    )
    expert_total = lax.psum_scatter(b_rows[3], "dp", scatter_dimension=0, tiled=False)
    expert_total = expert_total.astype(F32)
    expert_outputs = (
        expert_total[:, 0],
        expert_total[:, 1],
        jnp.swapaxes(expert_total[:, 2], 1, 2),
    )
    back_rows = ([a_rows[1], b_rows[1]], [a_rows[2], b_rows[2]], cap, experts_pad)
    last_part = run_combine_back(z, pos, *back_rows, owners - 1, 1)[0]
    if paired:
        order, last_part = wait(order, last_part)
        passed, middle = along(last_part, [(3, 2), (0, 1)]), along(last_part, [(1, 2), (2, 1)])
    else:
        order = last_part
    backs = run_combine_back(z, hold(order, pos), *back_rows, 0, owners - 1)
    backs = [*backs, last_part]
    out_rows = [a_rows[0], b_rows[0]]
    if paired:
        outs = run_combine_out(hold(order, pos), out_rows, cap)
        order, passed, middle, *outs = wait(order, passed, middle, *outs)
        far, near = cross(add(backs[2], passed), 2), cross(hold(order, backs[1]), 1)
        order, far, near = wait(order, far, near)
        backs = [backs[0], near, far, middle]
        last_out = hold(order, outs[3])
        passed, middle = along(last_out, [(3, 2), (0, 1)]), along(last_out, [(1, 2), (2, 1)])
        near_out = cross(hold(order, outs[1]), 1)
    else:
        outs = run_combine_out(pos, out_rows, cap)
        backs = plain_return(backs, owners)
        outs = plain_return(outs, owners)
        order = backs[0]
    res_grad, ctx_grad, ext_grad, o_own, o_other = run_second(
        me, own_p, hold(order, extra), low_two, res, cotangent, ctx, backs, out_pieces, size, per
    )
    back, blocks = run_heads(ctx_grad, qkv, probs, owners)
    if paired:
        order, blocks, back, passed, middle, near_out = wait(
            order, blocks, back, passed, middle, near_out
        )
    back_all = exchange(blocks)
    if paired:
        o_other = swap(hold(order, o_other), 1, size)
        order, o_other = wait(order, o_other)
        mid = width // 2
        o_up, o_left = add(o_own[2:, :, :mid], o_other[2:, :, :mid]), add(
            o_own[1::2, :, mid:], o_other[1::2, :, mid:]
        )
        relay = add(outs[2], passed)
        order, o_up, o_left, relay = wait(order, o_up, o_left, relay)
        o_up, o_left = swap(o_up, 4, size), swap(o_left, 2, size)
    grad_tokens, ext_cols = run_first(
        me, hold(order, back), tokens, extra, ext_grad, res_grad, qkv_pieces, size
    )
    if paired:
        order, ext_cols, back_all, o_up, o_left = wait(order, ext_cols, back_all, o_up, o_left)
        lower = seq // 2
        relay = hold(order, relay)
        far_a = cross(relay[:lower], 2)

        def three(*values):
            return sum(v.astype(F32) for v in values)

        o_second = three(o_own[1, :, :mid], o_other[1, :, :mid], o_up[1]).astype(BF)
        o_third = three(o_own[2, :, mid:], o_other[2, :, mid:], o_left[1]).astype(BF)
        o_first = three(o_own[0, :, :mid], o_other[0, :, :mid], o_up[0])
        o_last = three(o_own[0, :, mid:], o_other[0, :, mid:], o_left[0])
        o_second, o_third = swap(o_second, 2, size), swap(o_third, 4, size)
    parts = run_project(me, low_all, back_all, ext_cols, size)
    if paired:
        order, far_a, o_second, o_third, *parts = wait(order, far_a, o_second, o_third, *parts)
        near = swap(parts[4], 1, size)
        far_b = cross(hold(order, relay)[lower:], 2)
        o_total = jnp.concatenate(
            [three(o_first, o_second).astype(BF), three(o_last, o_third).astype(BF)], axis=1
        )
        o_parts = exchange(o_total)
        order, near = wait(order, near)
        pair = [add(parts[m], near[m]) for m in (1, 2, 3)]
        order, *pair = wait(order, *pair)
        links = [swap(pair[m - 1], 2 * m, size) for m in (1, 2, 3)]
        order, o_parts, far_b, *links = wait(order, o_parts, far_b, *links)
        far_out = jnp.concatenate([far_a, far_b], axis=0)
        outs = [outs[0], near_out, far_out, middle]
        total = exchange(run_join([parts[0], near[0], *links], o_parts, owners))
    else:
        total = lax.psum_scatter(parts[0], "dp", scatter_dimension=0, tiled=False)
        total = exchange(jnp.concatenate([total] * owners, axis=0))
    mixed = res
    for part in outs:
        mixed = mixed + part.astype(F32)
    mixed = mixed.astype(BF)
    if paired:
        total, mixed, *expert_outputs = lax.optimization_barrier((total, mixed, *expert_outputs))
        results = run_finish(total, owners, experts)
        query_total, key_total, value_total, out_total, router_total, gain_one, gain_two = results
        router_total = router_total.T
    else:
        o_total = lax.psum_scatter(o_own, "dp", scatter_dimension=0, tiled=False)
        out_total = lax.psum(o_total, "expert").astype(F32)
        total = total.reshape(owners, slim, -1).astype(F32)
        wide, narrow = QW // owners, KW // owners

        def side_by_side(first, last):
            return jnp.concatenate([total[j, :, first:last] for j in range(owners)], axis=1)

        query_total = side_by_side(0, wide)
        key_total = side_by_side(wide, wide + narrow)
        value_total = side_by_side(wide + narrow, wide + 2 * narrow)
        ext_total = jnp.sum(total[:, :, wide + 2 * narrow :], axis=0)
        router_total = ext_total[:, :experts]
        gain_one, gain_two = ext_total[:, experts_pad], ext_total[:, experts_pad + 8]
    return (
        mixed,
        grad_tokens,
        gain_one,
        query_total,
        key_total,
        value_total,
        out_total,
        gain_two,
        router_total,
        *expert_outputs,
    )


def solution(mesh):
    return jax.shard_map(
        body,
        mesh=mesh,
        in_specs=(
            P(("dp", "expert"), None),
            P(("dp", "expert"), None),
            P(("dp", "expert"), None),
            P("dp"),
            P("dp", None),
            P("dp", None),
            P("dp", None),
            P("dp", None),
            P("dp"),
            P("dp", None),
            P("expert", "dp", None),
            P("expert", "dp", None),
            P("expert", None, "dp"),
            P(("dp", "expert"), None),
        ),
        out_specs=(
            P(("dp", "expert"), None),
            P(("dp", "expert"), None),
            P("dp"),
            P("dp", None),
            P("dp", None),
            P("dp", None),
            P("dp", None),
            P("dp"),
            P("dp", None),
            P("expert", "dp", None),
            P("expert", "dp", None),
            P("expert", None, "dp"),
        ),
        check_vma=False,
    )
```

```python
import functools

import jax
import jax.numpy as jnp
from jax import lax
from jax.experimental import pallas as pl
from jax.experimental.pallas import tpu as pltpu
from jax.sharding import PartitionSpec as P

HEADS = 24
KV_HEADS = 8
HEAD_DIM = 64
TOP = 8
GROUPS = HEADS // KV_HEADS
QW = HEADS * HEAD_DIM
KW = KV_HEADS * HEAD_DIM
QKV = QW + 2 * KW
EXT = 128
HALVES = 2
EXTRA = 16
COST_SCALE = 1.0

norm_eps = 1e-06
masked_score = -1e30
BF = jnp.bfloat16
F32 = jnp.float32
ANY = pl.BlockSpec(memory_space=pl.ANY)
VMEM = pl.BlockSpec(memory_space=pltpu.VMEM)
SMEM = pl.BlockSpec(memory_space=pltpu.SMEM)
VMEM_LIMIT = 56 * 1024 * 1024


def dot(a, b, ca=1, cb=0):
    return lax.dot_general(a, b, (((ca,), (cb,)), ((), ())), preferred_element_type=F32)


def params():
    return pltpu.CompilerParams(vmem_limit_bytes=VMEM_LIMIT)


def cost(us):
    return pl.CostEstimate(
        flops=int(us * 1.1e9), bytes_accessed=int(us * 3.6e6 * COST_SCALE), transcendentals=0
    )


def sds(shape, dtype):
    return jax.ShapeDtypeStruct(shape, dtype)


def swap(value, bit, size):
    return lax.ppermute(value, "dp", [(i, i ^ bit) for i in range(size)])


def wait(order, *values):
    return lax.optimization_barrier((order,) + values)


def hold(order, value):
    return lax.optimization_barrier((order, value))[1]


def plain_shards(shard, size):
    rows = shard.shape[-2]
    arrays = [lax.all_gather(shard, "dp", axis=0, tiled=False)]
    return arrays, [(i, 0, rows) for i in range(size)]


def add(a, b):
    return (a.astype(F32) + b.astype(F32)).astype(BF)


def owner_at(z, r, owners):
    return jnp.bitwise_xor(z, r) if owners == 4 else lax.rem(z - r + owners, owners)


def along(value, pairs):
    return lax.ppermute(value, "expert", pairs)


def cross(value, bit):
    return along(value, [(i, i ^ bit) for i in range(4)])


def plain_owners(value, owners):
    turns = [[(i, (i + r) % owners) for i in range(owners)] for r in range(1, owners)]
    return [value] + [along(value, pairs) for pairs in turns]


def plain_return(parts, owners):
    turns = [[(i, (i - r) % owners) for i in range(owners)] for r in range(1, owners)]
    return [parts[0]] + [along(v, pairs) for v, pairs in zip(parts[1:], turns)]


def exchange(value):
    return lax.all_to_all(value, "expert", split_axis=0, concat_axis=0, tiled=True)


def part_shapes(size, shape):
    if size != 8:
        return [sds((size,) + shape, BF)]
    return [sds(shape, BF)] * 4 + [sds((4,) + shape, BF)]


def fetch(me, refs, plan, target, sems, rows, size):
    copies = []
    for n, (i, start, count) in enumerate(plan):
        source = refs[0].at[i] if len(refs) == 1 else refs[n]
        at = (jnp.bitwise_xor(me, i) if size == 8 else i) * rows + start
        if size == 8:
            at = pl.multiple_of(at, rows // 2)
        copies.append(pltpu.make_async_copy(source, target(pl.ds(at, count)), sems.at[n]))
    for c in copies:
        c.start()
    return copies


def pair_refs(own, other, size):
    if size != 8:
        return [own]
    return [(other if i % 2 else own).at[i // 2] for i in range(size)]


def store_parts(me, source, outs, sems, rows, size):
    copies = []
    for i in range(size):
        if len(outs) == 1:
            target, at = outs[0].at[i], i * rows
        else:
            target = outs[i]
            at = pl.multiple_of(jnp.bitwise_xor(me, i) * rows, rows)
        copies.append(pltpu.make_async_copy(source(pl.ds(at, rows)), target, sems.at[i]))
    for c in copies:
        c.start()
    return copies


def pack_kernel(experts, q, k, v, router, gain_one, gain_two, out):
    rows = q.shape[0]
    pad = -(-experts // 8) * 8
    out[:, :QW] = q[...]
    out[:, QW : QW + KW] = k[...]
    out[:, QW + KW : QKV] = v[...]
    gains = [jnp.broadcast_to(g[...].astype(F32)[None, :], (8, rows)) for g in (gain_one, gain_two)]
    parts = [router[...].astype(F32)]
    if pad > experts:
        parts.append(jnp.zeros((pad - experts, rows), F32))
    parts += gains + [jnp.zeros((EXT - pad - 16, rows), F32)]
    out[:, QKV:] = jnp.concatenate(parts, axis=0).T.astype(BF)


def run_pack(q, k, v, router, gain_one, gain_two):
    rows, experts = router.shape
    return pl.pallas_call(
        functools.partial(pack_kernel, experts),
        name="pack",
        out_shape=sds((rows, QKV + EXT), BF),
        in_specs=[VMEM] * 6,
        out_specs=VMEM,
        compiler_params=params(),
        cost_estimate=cost(0.01),
    )(q, k, v, router.T, gain_one, gain_two)


def attention_kernel(size, rows, plan, me, tok, seg_row, seg_col, *rest):
    refs, rest = rest[:-7], rest[-7:]
    low_out, qkv_out, ctx_out, prob_out, ext_out, w, sems = rest
    copies = fetch(me[0], refs, plan, lambda s: w.at[s], sems, rows, size)
    seq = tok.shape[0]
    x = tok[...].astype(F32)
    factor = lax.rsqrt(jnp.mean(x * x, axis=-1, keepdims=True) + norm_eps)
    normed = x * factor
    same = seg_col[...] == seg_row[...]
    key_at = lax.broadcasted_iota(jnp.int32, (seq, seq), 0)
    query_at = lax.broadcasted_iota(jnp.int32, (seq, seq), 1)
    allowed = jnp.where(same & (key_at <= query_at), 0.0, masked_score)
    allowed = jnp.concatenate([allowed] * GROUPS, axis=1)
    for c in copies:
        c.wait()
    ext = w[:, QKV:].astype(F32).T[: ext_out.shape[0], :]
    ext_out[...] = ext
    experts_pad = ext_out.shape[0] - 16
    gain = ext[experts_pad : experts_pad + 1, :]
    low = (normed * gain).astype(BF)
    step = 512
    for j in range(low.shape[1] // step):
        at = slice(j * step, (j + 1) * step)
        low_out[at, :] = low[:, at].astype(F32).T.astype(BF)
    for j in range(QKV // step):
        at = slice(j * step, (j + 1) * step)
        part = dot(low, w[:, at])
        qkv_out[at, :] = part.T.astype(BF)
    for h in range(KV_HEADS):
        q = jnp.concatenate(
            [
                qkv_out[(GROUPS * h + g) * HEAD_DIM : (GROUPS * h + g + 1) * HEAD_DIM, :]
                for g in range(GROUPS)
            ],
            axis=1,
        )
        k = qkv_out[QW + h * HEAD_DIM : QW + (h + 1) * HEAD_DIM, :]
        v = qkv_out[QW + KW + h * HEAD_DIM : QW + KW + (h + 1) * HEAD_DIM, :]
        scores = dot(k, q, 0, 0) * HEAD_DIM ** (-0.5)
        scores = jnp.where(allowed < 0.0, masked_score, scores)
        top = jnp.max(scores, axis=0, keepdims=True)
        shifted = jnp.exp(scores - top)
        probs = (shifted * (1.0 / jnp.sum(shifted, axis=0, keepdims=True))).astype(BF)
        prob_out[h] = probs
        ctx = dot(v, probs).astype(BF)
        for g in range(GROUPS):
            at = (GROUPS * h + g) * HEAD_DIM
            ctx_out[at : at + HEAD_DIM, :] = ctx[:, g * seq : (g + 1) * seq]


def run_attention(me, tokens, seg_row, seg_col, pieces, size, ext_rows):
    seq, width = tokens.shape
    rows = width // size
    arrays, plan = pieces
    return pl.pallas_call(
        functools.partial(attention_kernel, size, rows, plan),
        name="attention",
        out_shape=[
            sds((width, seq), BF),
            sds((QKV, seq), BF),
            sds((QW, seq), BF),
            sds((KV_HEADS, seq, GROUPS * seq), BF),
            sds((ext_rows, width), F32),
        ],
        in_specs=[SMEM, VMEM, VMEM, VMEM] + [ANY] * len(arrays),
        out_specs=[VMEM] * 5,
        scratch_shapes=[
            pltpu.VMEM((width, QKV + EXT), BF),
            pltpu.SemaphoreType.DMA((len(plan),)),
        ],
        compiler_params=params(),
        cost_estimate=cost(0.01),
    )(me, tokens, seg_row, seg_col, *arrays)


def residual_kernel(size, rows, plan, me, tok, ctx, ext, place, *rest):
    refs, (res_out, low_out, w, sems) = rest[:-4], rest[-4:]
    copies = fetch(me[0], refs, plan, lambda s: w.at[s], sems, rows, size)
    experts_pad = ext.shape[0] - 16
    for c in copies:
        c.wait()
    res = tok[...].astype(F32) + dot(ctx[...], w[...], 0, 0)
    res_out[...] = res
    factor = lax.rsqrt(jnp.mean(res * res, axis=-1, keepdims=True) + norm_eps)
    seq = res.shape[0]
    low_out[:seq, :] = (res * factor * ext[experts_pad + 8 : experts_pad + 9, :]).astype(BF)
    low_out[seq:, :] = place[...]


def run_residual(me, tokens, ctx, ext, place, pieces, size):
    seq, width = tokens.shape
    rows = QW // size
    arrays, plan = pieces
    return pl.pallas_call(
        functools.partial(residual_kernel, size, rows, plan),
        name="residual",
        out_shape=[sds((seq, width), F32), sds((seq + EXTRA, width), BF)],
        in_specs=[SMEM, VMEM, VMEM, VMEM, VMEM] + [ANY] * len(arrays),
        out_specs=[VMEM] * 2,
        scratch_shapes=[pltpu.VMEM((QW, width), BF), pltpu.SemaphoreType.DMA((len(plan),))],
        compiler_params=params(),
        cost_estimate=cost(0.01),
    )(me, tokens, ctx, ext, place, *arrays)


def slot_of(block, seq, width):
    across = width // seq
    row, col = block // across * 8, block % across * seq
    return slice(row, row + 8), slice(col, col + seq)


def router_kernel(owners, per, z, ext, *rest):
    given, rest = rest[:-6], rest[-6:]
    pos_out, p_out, own_out, last_out, all_p, all_pos = rest
    if len(given) > owners:
        inner = (z[0] == 1) | (z[0] == 2)

        @pl.when(inner)
        def _():
            last_out[...] = given[owners - 1][...]

        @pl.when(jnp.logical_not(inner))
        def _():
            last_out[...] = given[owners][...]
    else:
        last_out[...] = given[owners - 1][...]
    rows = list(given[: owners - 1]) + [last_out]
    experts_pad = ext.shape[0] - 16
    seq, width = rows[0].shape[0] - EXTRA, rows[0].shape[1]
    router = ext[:experts_pad, :].astype(BF)
    at = z[0] * per
    for r in range(owners):
        logits = dot(router, rows[r][:seq, :], 1, 1)
        spots = rows[r][seq:, :].astype(F32)
        for b in range(experts_pad // 8):
            of, to = slot_of(b, seq, width)
            all_pos[b * 8 : (b + 1) * 8, :] = spots[of, to]
        where = all_pos[...]
        named = where >= 0.0
        logits = jnp.where(named, logits, masked_score)
        top = jnp.max(logits, axis=0, keepdims=True)
        shifted = jnp.where(named, jnp.exp(logits - top), 0.0)
        probs = shifted / jnp.sum(shifted, axis=0, keepdims=True)
        all_p[...] = probs
        if r == 0:
            own_out[...] = probs
        for l in range(per):
            p_out[l, r : r + 1, :] = all_p[pl.ds(at + l, 1), :]
            pos_out[l, r : r + 1, :] = all_pos[pl.ds(at + l, 1), :].astype(jnp.int32)


def run_router(z, ext, rows, per, owners):
    seq = rows[0].shape[0] - EXTRA
    experts_pad = ext.shape[0] - 16
    return pl.pallas_call(
        functools.partial(router_kernel, owners, per),
        name="router",
        out_shape=[
            sds((per, owners, seq), jnp.int32),
            sds((per, owners, seq), F32),
            sds((experts_pad, seq), F32),
            sds(rows[0].shape, BF),
        ],
        in_specs=[SMEM, VMEM] + [VMEM] * len(rows),
        out_specs=[VMEM] * 4,
        scratch_shapes=[pltpu.VMEM((experts_pad, seq), F32)] * 2,
        compiler_params=params(),
        cost_estimate=cost(0.01),
    )(z, ext, *rows)


def load_rows(owners, z, xs, cs, xv, cv, sem_x, sem_c):
    seq = xv.shape[1]
    copies = []
    for r in range(owners):
        start = pl.multiple_of(owner_at(z[0], r, owners) * seq, seq)
        copies.append(pltpu.make_async_copy(xs[r].at[pl.ds(0, seq)], xv.at[r], sem_x.at[r]))
        copies.append(pltpu.make_async_copy(cs.at[pl.ds(start, seq)], cv.at[r], sem_c.at[r]))
    for c in copies:
        c.start()

    def wait(r):
        copies[2 * r].wait()
        copies[2 * r + 1].wait()

    return wait


def pick_rows(owners, cap, number, pos, p, xv, cv, xr, cr, prow, wait_rows):
    seq = xv.shape[1]
    slot = lax.broadcasted_iota(jnp.int32, (cap, seq), 0)
    for r in range(owners):
        hot = pos[number, r : r + 1, :] == slot
        low_hot = jnp.where(hot, 1.0, 0.0).astype(BF)
        at = pl.ds(r * cap, cap)
        if wait_rows is not None:
            wait_rows(r)
        xr[at, :] = dot(low_hot, xv[r]).astype(BF)
        cr[at, :] = dot(low_hot, cv[r]).astype(BF)
        prow[at, :] = jnp.sum(jnp.where(hot, p[number, r : r + 1, :], 0.0), axis=1, keepdims=True)


def through_expert(owners, cap, number, pos, xr, cr, prow, w, hp, gg, ug, gate, gate_out):
    ff = w.shape[2]
    step = ff // HALVES
    gate[...] = jnp.zeros_like(gate)
    for j in range(HALVES):
        cols = slice(j * step, (j + 1) * step)
        gate_pre = dot(xr[...], w[0, :, cols])
        up_pre = dot(xr[...], w[1, :, cols])
        back = dot(cr[...], w[2, :, cols])
        probs = prow[...]
        s = jax.nn.sigmoid(gate_pre)
        silu = gate_pre * s
        hidden = silu * up_pre
        gate[...] += jnp.sum(hidden * back, axis=1, keepdims=True)
        hp[:, cols] = (hidden * probs).astype(BF)
        back = back * probs
        gg[:, cols] = (back * up_pre * (s + silu * (1.0 - s))).astype(BF)
        ug[:, cols] = (back * silu).astype(BF)
    seq = pos.shape[2]
    slot = lax.broadcasted_iota(jnp.int32, (cap, seq), 0)
    for r in range(owners):
        hot = pos[number, r : r + 1, :] == slot
        at = pl.ds(r * cap, cap)
        gate_out[r : r + 1, :] = jnp.sum(jnp.where(hot, gate[at, :], 0.0), axis=0, keepdims=True)


def load_weights(me, refs, plan, w, sems, slot_at, rows, size):
    shards = [ref.at[:, slot_at] if len(refs) == 1 else ref.at[slot_at] for ref in refs]
    return fetch(me, shards, plan, lambda s: w.at[:, s, :], sems, rows, size)


def weight_grads(xr, cr, hp, gg, ug, g, grads, sems, slot_at, rows, size):
    width = xr.shape[1]
    tile = width // HALVES
    for j in range(HALVES):
        cols = slice(j * tile, (j + 1) * tile)
        g[0, cols, :] = dot(xr[:, cols], gg[...], 0, 0).astype(BF)
        g[1, cols, :] = dot(xr[:, cols], ug[...], 0, 0).astype(BF)
        g[2, cols, :] = dot(cr[:, cols], hp[...], 0, 0).astype(BF)
    copies = [
        pltpu.make_async_copy(g.at[:, pl.ds(i * rows, rows), :], grads.at[i, slot_at], sems.at[i])
        for i in range(size)
    ]
    for c in copies:
        c.start()
    return copies


def rows_back(w, gg, ug, bv):
    tile = bv.shape[1] // HALVES
    for j in range(HALVES):
        cols = slice(j * tile, (j + 1) * tile)
        total = dot(gg[...], w[0, cols, :], 1, 1) + dot(ug[...], w[1, cols, :], 1, 1)
        bv[:, cols] = total.astype(BF)


def rows_out(w, hp, ov):
    tile = ov.shape[1] // HALVES
    for j in range(HALVES):
        cols = slice(j * tile, (j + 1) * tile)
        ov[:, cols] = dot(hp[...], w[cols, :], 1, 1).astype(BF)


def experts_kernel(size, rows, owners, cap, first, many, plan, count, me, z, pos, p, cs, *rest):
    xs, refs, rest = rest[:owners], rest[owners : owners + count], rest[owners + count :]
    if first > 0:
        rest = rest[1:]
    out_rows, back_rows, gate_out, grads = rest[:4]
    xv, cv, w, xr, cr, prow, hp, gg, ug, gate, ov, bv, g, sem_x, sem_c, sem_w, sem_g, sem_o = rest[4:]
    wait_rows = load_rows(owners, z, xs, cs, xv, cv, sem_x, sem_c)

    def load(i):
        return load_weights(me[0], refs, plan, w.at[i % 2], sem_w.at[i % 2], i, rows, size)

    coming = load(0)
    leaving = []
    for i in range(many):
        here = i % 2
        number = first + i
        pick_rows(
            owners, cap, number, pos, p, xv, cv, xr, cr, prow, wait_rows if i == 0 else None
        )
        for c in coming:
            c.wait()
        if i + 1 < many:
            coming = load(i + 1)
        if len(leaving) > 1:
            for c in leaving[i - 2]:
                c.wait()
        through_expert(
            owners, cap, number, pos, xr, cr, prow, w.at[here], hp, gg, ug, gate, gate_out.at[i]
        )
        copies = weight_grads(
            xr, cr, hp, gg, ug, g.at[here], grads, sem_g.at[here], number, rows, size
        )
        rows_back(w.at[here], gg, ug, bv.at[here])
        copies.append(pltpu.make_async_copy(bv.at[here], back_rows.at[i], sem_o.at[here, 0]))
        copies[-1].start()
        rows_out(w.at[here, 2], hp, ov.at[here])
        copies.append(pltpu.make_async_copy(ov.at[here], out_rows.at[i], sem_o.at[here, 1]))
        copies[-1].start()
        leaving.append(copies)
    for copies in leaving[-2:]:
        for c in copies:
            c.wait()


def run_experts(me, z, pos, p, xs, cs, pieces, buffer, size, first, many, cap):
    per, owners, seq = pos.shape
    width = xs[0].shape[1]
    refs, plan = pieces
    ff = refs[0].shape[-1]
    rows = width // size
    total = owners * cap
    given = [me, z, pos, p, cs, *xs, *refs] + ([] if buffer is None else [buffer])
    return pl.pallas_call(
        functools.partial(
            experts_kernel, size, rows, owners, cap, first, many, plan, len(refs)
        ),
        name="experts",
        out_shape=[
            sds((many, total, width), BF),
            sds((many, total, width), BF),
            sds((many, owners, seq), F32),
            sds((size, per, 3, rows, ff), BF),
        ],
        in_specs=[SMEM, SMEM, VMEM, VMEM] + [ANY] * (len(given) - 4),
        out_specs=[ANY, ANY, VMEM, ANY],
        input_output_aliases={} if buffer is None else {len(given) - 1: 3},
        scratch_shapes=[
            pltpu.VMEM((owners, seq, width), BF),
            pltpu.VMEM((owners, seq, width), BF),
            pltpu.VMEM((2, 3, width, ff), BF),
            pltpu.VMEM((total, width), BF),
            pltpu.VMEM((total, width), BF),
            pltpu.VMEM((total, 1), F32),
            pltpu.VMEM((total, ff), BF),
            pltpu.VMEM((total, ff), BF),
            pltpu.VMEM((total, ff), BF),
            pltpu.VMEM((total, 1), F32),
            pltpu.VMEM((2, total, width), BF),
            pltpu.VMEM((2, total, width), BF),
            pltpu.VMEM((2, 3, width, ff), BF),
            pltpu.SemaphoreType.DMA((owners,)),
            pltpu.SemaphoreType.DMA((owners,)),
            pltpu.SemaphoreType.DMA((2, len(plan))),
            pltpu.SemaphoreType.DMA((2, size)),
            pltpu.SemaphoreType.DMA((2, 2)),
        ],
        compiler_params=params(),
        cost_estimate=cost(0.01),
    )(*given)


def combined_rows(per, cap, pos, r, rows):
    seq = pos.shape[2]
    slot = lax.broadcasted_iota(jnp.int32, (cap, seq), 0)
    hot = jnp.concatenate(
        [jnp.where(pos[l, pl.ds(r, 1), :] == slot, 1.0, 0.0).astype(BF) for l in range(per)], axis=0
    )
    total, at = 0.0, 0
    for group in rows:
        count = group.shape[0] * cap
        total = total + dot(hot[at : at + count], group[...].reshape(count, -1), 0, 0)
        at += count
    return total.astype(BF)


def combine_back_kernel(start, owners, per, cap, experts_pad, groups, z, pos, *rest):
    rows, gates, rest = rest[:groups], rest[groups : 2 * groups], rest[2 * groups :]
    outs, block = rest[:owners], rest[owners]
    step = pl.program_id(0)
    r = step + start
    seq, width = pos.shape[2], outs[0].shape[1]
    total = combined_rows(per, cap, pos, r, rows)
    block[...] = jnp.zeros_like(block)
    gates = [group.at[l] for group in gates for l in range(group.shape[0])]
    for l in range(per):
        block[pl.ds(z[0] * per + l, 1), :] = gates[l][pl.ds(r, 1), :]
    value = block[...]
    high = value.astype(BF)
    low = (value - high.astype(F32)).astype(BF)
    for o in range(owners):

        @pl.when(step == o)
        def _():
            outs[o][:seq, :] = total
            outs[o][seq:, :] = jnp.zeros((EXTRA, width), BF)
            both = jnp.concatenate([high, low], axis=0).astype(F32)
            for row in range(EXTRA // 8):
                across = width // seq
                blocks = [
                    both[(row * across + b) * 8 : (row * across + b + 1) * 8, :]
                    if row * across + b < 2 * experts_pad // 8
                    else jnp.zeros((8, seq), F32)
                    for b in range(across)
                ]
                outs[o][seq + row * 8 : seq + row * 8 + 8, :] = jnp.concatenate(
                    blocks, axis=1
                ).astype(BF)


def whole(shape):
    return pl.BlockSpec(shape, lambda r: (0,) * len(shape))


def run_combine_back(z, pos, rows, gates, cap, experts_pad, start, owners):
    per, _, seq = pos.shape
    width = rows[0].shape[2]
    shapes = [sds((seq + EXTRA, width), BF)] * owners
    return pl.pallas_call(
        functools.partial(combine_back_kernel, start, owners, per, cap, experts_pad, len(rows)),
        name="combine_back",
        grid=(owners,),
        out_shape=shapes,
        in_specs=[SMEM, whole(pos.shape)]
        + [pl.BlockSpec((a.shape[0], cap, width), lambda r: (0, r + start, 0)) for a in rows]
        + [whole(a.shape) for a in gates],
        out_specs=[whole(s.shape) for s in shapes],
        scratch_shapes=[pltpu.VMEM((experts_pad, seq), F32)],
        compiler_params=params(),
        cost_estimate=cost(0.01),
    )(z, pos, *rows, *gates)


def combine_out_kernel(owners, per, cap, pos, *rest):
    rows, outs = rest[:-owners], rest[-owners:]
    r = pl.program_id(0)
    total = combined_rows(per, cap, pos, r, rows)
    for o in range(owners):

        @pl.when(r == o)
        def _():
            outs[o][...] = total


def run_combine_out(pos, rows, cap):
    per, owners, seq = pos.shape
    width = rows[0].shape[2]
    return pl.pallas_call(
        functools.partial(combine_out_kernel, owners, per, cap),
        name="combine_out",
        grid=(owners,),
        out_shape=[sds((seq, width), BF)] * owners,
        in_specs=[whole(pos.shape)]
        + [pl.BlockSpec((a.shape[0], cap, width), lambda r: (0, r, 0)) for a in rows],
        out_specs=[whole((seq, width))] * owners,
        compiler_params=params(),
        cost_estimate=cost(0.01),
    )(pos, *rows)


def join_kernel(owners, own, *rest):
    more, (parts, out) = rest[:-2], rest[-2:]
    rows, cols = own.shape
    total = own[...].astype(F32)
    for piece in more:
        total = total + piece[...].astype(F32)
    total = total.astype(BF)
    low = parts.shape[0] // owners
    summed = 0.0
    for r in range(owners):
        summed = summed + parts[r * low : (r + 1) * low, :].astype(F32)
    summed = summed.astype(BF)
    wide = summed.shape[1] // owners
    out[:, :cols] = total
    for k in range(owners):
        out[k * low : (k + 1) * low, cols:] = summed[:, k * wide : (k + 1) * wide]


def run_join(pieces, parts, owners):
    rows, cols = pieces[0].shape
    return pl.pallas_call(
        functools.partial(join_kernel, owners),
        name="join",
        out_shape=sds((rows, cols + parts.shape[1] // owners), BF),
        in_specs=[VMEM] * (len(pieces) + 1),
        out_specs=VMEM,
        compiler_params=params(),
        cost_estimate=cost(0.01),
    )(*pieces, parts)


def finish_kernel(owners, z, *rest):
    given, (query, key, value, out, router, gain_one, gain_two, last) = rest[:-8], rest[-8:]
    rows = query.shape[0]
    wide, narrow = QW // owners, KW // owners
    one = wide + 2 * narrow
    low, out_wide = rows // owners, out.shape[1] // owners
    inner = (z[0] == 1) | (z[0] == 2)

    @pl.when(inner)
    def _():
        last[...] = given[3][...]

    @pl.when(jnp.logical_not(inner))
    def _():
        last[...] = given[4][...]

    ext_sum = 0.0
    for r, ref in enumerate((given[0], given[1], given[2], last)):
        j = jnp.bitwise_xor(z[0], r)
        block = ref[...].astype(F32)
        query[:, pl.ds(pl.multiple_of(j * wide, wide), wide)] = block[:, :wide]
        slim = pl.ds(pl.multiple_of(j * narrow, narrow), narrow)
        key[:, slim] = block[:, wide : wide + narrow]
        value[:, slim] = block[:, wide + narrow : one]
        ext_sum = ext_sum + block[:, one : one + EXT]
        to = pl.ds(pl.multiple_of(j * low, low), low)
        for k in range(owners):
            out[to, k * out_wide : (k + 1) * out_wide] = block[
                k * low : (k + 1) * low, one + EXT :
            ]
    ext_sum = ext_sum.T
    experts = router.shape[0]
    pad = -(-experts // 8) * 8
    router[...] = ext_sum[:experts, :]
    gain_one[...] = ext_sum[pad, :]
    gain_two[...] = ext_sum[pad + 8, :]


def run_finish(z, given, owners, experts):
    rows, cols = given[0].shape
    width = (cols - EXT - (QW + 2 * KW) // owners) * owners
    return pl.pallas_call(
        functools.partial(finish_kernel, owners),
        name="finish",
        out_shape=[
            sds((rows, QW), F32),
            sds((rows, KW), F32),
            sds((rows, KW), F32),
            sds((rows, width), F32),
            sds((experts, rows), F32),
            sds((rows,), F32),
            sds((rows,), F32),
        ],
        in_specs=[SMEM] + [VMEM] * len(given),
        out_specs=[VMEM] * 7,
        scratch_shapes=[pltpu.VMEM((rows, cols), BF)],
        compiler_params=params(),
        cost_estimate=cost(0.01),
    )(z, *given)


def second_kernel(
    size, rows, owners, per, plan, count, me, own_p, ext, low_two, res, cot, ctx, *rest
):
    backs, rest = rest[:owners], rest[owners:]
    refs, rest = rest[:count], rest[count:]
    res_grad, ctx_grad, ext_grad, own, other, w, g, gate, sems, sems_g = rest
    copies = fetch(me[0], refs, plan, lambda s: w.at[s], sems, rows, size)
    experts_pad = own_p.shape[0]
    seq, width = res.shape
    arrived = backs[0][seq:, :].astype(F32)
    for r in range(1, owners):
        arrived = arrived + backs[r][seq:, :].astype(F32)
    for b in range(experts_pad // 8):
        high_at = slot_of(b, seq, width)
        low_at = slot_of(b + experts_pad // 8, seq, width)
        gate[b * 8 : (b + 1) * 8, :] = arrived[high_at] + arrived[low_at]
    p = own_p[...]
    gate_grad = gate[...]
    weighted = jnp.sum(p * gate_grad, axis=0, keepdims=True)
    logit_grad = (p * (gate_grad - weighted)).astype(BF)
    router = ext[:experts_pad, :].astype(BF)
    ext_grad[:experts_pad, :] = dot(logit_grad, low_two[:seq, :])
    two = dot(logit_grad, router, 0, 0)
    for r in range(owners):
        two = two + backs[r][:seq, :].astype(F32)
    values = res[...]
    factor = lax.rsqrt(jnp.mean(values * values, axis=-1, keepdims=True) + norm_eps)
    normed = values * factor
    ext_grad[experts_pad:, :] = jnp.broadcast_to(
        jnp.sum(two * normed, axis=0, keepdims=True), (16, normed.shape[1])
    )
    scaled = two * ext[experts_pad + 8 : experts_pad + 9, :]
    inward = factor * (scaled - normed * jnp.mean(scaled * normed, axis=-1, keepdims=True))
    total = cot[...].astype(F32) + inward
    res_grad[...] = total
    low = total.astype(BF)
    step = QW // 4
    for j in range(4):
        at = slice(j * step, (j + 1) * step)
        g[at, :] = dot(ctx[at, :], low).astype(BF)
    copies_g = store_parts(me[0], lambda s: g.at[s], pair_refs(own, other, size), sems_g, rows, size)
    for c in copies:
        c.wait()
    for j in range(4):
        at = slice(j * step, (j + 1) * step)
        ctx_grad[at, :] = dot(w[at, :], low, 1, 1).astype(BF)
    for c in copies_g:
        c.wait()


def run_second(me, own_p, ext, low_two, res, cot, ctx, backs, pieces, size, per):
    owners = len(backs)
    arrays, plan = pieces
    seq, width = res.shape
    rows = QW // size
    experts_pad = own_p.shape[0]
    return pl.pallas_call(
        functools.partial(second_kernel, size, rows, owners, per, plan, len(arrays)),
        name="second_back",
        out_shape=[
            sds((seq, width), F32),
            sds((QW, seq), BF),
            sds((experts_pad + 16, width), F32),
            sds((size if size != 8 else 4, rows, width), BF),
            sds((4, rows, width), BF),
        ],
        in_specs=[SMEM] + [VMEM] * (6 + owners) + [ANY] * len(arrays),
        out_specs=[VMEM] * 3 + [ANY] * 2,
        scratch_shapes=[
            pltpu.VMEM((QW, width), BF),
            pltpu.VMEM((QW, width), BF),
            pltpu.VMEM((experts_pad, seq), F32),
            pltpu.SemaphoreType.DMA((len(plan),)),
            pltpu.SemaphoreType.DMA((size,)),
        ],
        compiler_params=params(),
        cost_estimate=cost(0.01),
    )(me, own_p, ext, low_two, res, cot, ctx, *backs, *arrays)


def heads_kernel(ctx_grad, qkv, probs, back, blocks):
    seq = qkv.shape[1]
    scale = HEAD_DIM ** (-0.5)
    for h in range(KV_HEADS):

        def heads(ref):
            return jnp.concatenate(
                [
                    ref[(GROUPS * h + i) * HEAD_DIM : (GROUPS * h + i + 1) * HEAD_DIM, :]
                    for i in range(GROUPS)
                ],
                axis=1,
            )

        upstream = heads(ctx_grad)
        q = heads(qkv)
        k = qkv[QW + h * HEAD_DIM : QW + (h + 1) * HEAD_DIM, :]
        v = qkv[QW + KW + h * HEAD_DIM : QW + KW + (h + 1) * HEAD_DIM, :]
        low_p = probs[h]
        weights = low_p.astype(F32)
        prob_grad = dot(v, upstream, 0, 0)
        inner = jnp.sum(prob_grad * weights, axis=0, keepdims=True)
        score_grad = (weights * (prob_grad - inner)).astype(BF)
        value_grad = dot(upstream, low_p, 1, 1)
        key_grad = dot(q, score_grad, 1, 1) * scale
        query_grad = dot(k, score_grad) * scale
        back[QW + h * HEAD_DIM : QW + (h + 1) * HEAD_DIM, :] = key_grad.astype(BF)
        back[QW + KW + h * HEAD_DIM : QW + KW + (h + 1) * HEAD_DIM, :] = value_grad.astype(BF)
        for i in range(GROUPS):
            at = (GROUPS * h + i) * HEAD_DIM
            back[at : at + HEAD_DIM, :] = query_grad[:, i * seq : (i + 1) * seq].astype(BF)
    owners = blocks.shape[0] // seq
    wide, slim = QW // owners, KW // owners
    for j in range(owners):
        block = jnp.concatenate(
            [
                back[j * wide : (j + 1) * wide, :],
                back[QW + j * slim : QW + (j + 1) * slim, :],
                back[QW + KW + j * slim : QW + KW + (j + 1) * slim, :],
            ],
            axis=0,
        )
        blocks[j * seq : (j + 1) * seq, :] = block.astype(F32).T.astype(BF)


def run_heads(ctx_grad, qkv, probs, owners):
    seq = qkv.shape[1]
    return pl.pallas_call(
        heads_kernel,
        name="heads_back",
        out_shape=[sds((QKV, seq), BF), sds((owners * seq, QKV // owners), BF)],
        in_specs=[VMEM] * 3,
        out_specs=[VMEM] * 2,
        compiler_params=params(),
        cost_estimate=cost(0.01),
    )(ctx_grad, qkv, probs)


def first_kernel(size, rows, plan, me, back, tok, ext, ext_grad, res_grad, *rest):
    refs, (tok_grad, ext_cols, w, sems) = rest[:-4], rest[-4:]
    copies = fetch(me[0], refs, plan, lambda s: w.at[s], sems, rows, size)
    for c in copies:
        c.wait()
    one = dot(back[...], w[:, :QKV], 0, 1)
    x = tok[...].astype(F32)
    factor = lax.rsqrt(jnp.mean(x * x, axis=-1, keepdims=True) + norm_eps)
    normed = x * factor
    experts_pad = ext.shape[0] - 16
    gain = ext[experts_pad : experts_pad + 1, :]
    gain_grad = jnp.sum(one * normed, axis=0, keepdims=True)
    packed = jnp.concatenate(
        [
            ext_grad[:experts_pad, :],
            jnp.broadcast_to(gain_grad, (8, gain_grad.shape[1])),
            ext_grad[experts_pad + 8 :, :],
            jnp.zeros((EXT - experts_pad - 16, gain_grad.shape[1]), F32),
        ],
        axis=0,
    )
    ext_cols[...] = packed.T.astype(BF)
    scaled = one * gain
    inward = factor * (scaled - normed * jnp.mean(scaled * normed, axis=-1, keepdims=True))
    tok_grad[...] = res_grad[...] + inward


def run_first(me, back, tokens, ext, ext_grad, res_grad, pieces, size):
    arrays, plan = pieces
    seq, width = tokens.shape
    rows = width // size
    return pl.pallas_call(
        functools.partial(first_kernel, size, rows, plan),
        name="first_back",
        out_shape=[sds((seq, width), F32), sds((width, EXT), BF)],
        in_specs=[SMEM] + [VMEM] * 5 + [ANY] * len(arrays),
        out_specs=[VMEM] * 2,
        scratch_shapes=[
            pltpu.VMEM((width, QKV + EXT), BF),
            pltpu.SemaphoreType.DMA((len(plan),)),
        ],
        compiler_params=params(),
        cost_estimate=cost(60),
    )(me, back, tokens, ext, ext_grad, res_grad, *arrays)


def project_kernel(size, rows, me, low_all, back_all, ext_cols, *rest):
    grads, (g, sems_g) = rest[:-2], rest[-2:]
    owners, _, seq = low_all.shape
    cols = back_all.shape[1]
    g[:, cols:] = ext_cols[...]
    total = 0.0
    for r in range(owners):
        total = total + dot(low_all[r], back_all[r * seq : (r + 1) * seq, :])
    g[:, :cols] = total.astype(BF)
    if size == 8:
        grads = [grads[4].at[i // 2] if i % 2 else grads[i // 2] for i in range(size)]
    copies_g = store_parts(me[0], lambda s: g.at[s], grads, sems_g, rows, size)
    for c in copies_g:
        c.wait()


def run_project(me, low_all, back_all, ext_cols, size):
    width, cols = low_all.shape[1], back_all.shape[1] + EXT
    rows = width // size
    grads = part_shapes(size, (rows, cols))
    return pl.pallas_call(
        functools.partial(project_kernel, size, rows),
        name="project_back",
        out_shape=grads,
        in_specs=[SMEM] + [VMEM] * 3,
        out_specs=[ANY] * len(grads),
        scratch_shapes=[pltpu.VMEM((width, cols), BF), pltpu.SemaphoreType.DMA((size,))],
        compiler_params=params(),
        cost_estimate=cost(60),
    )(me, low_all, back_all, ext_cols)


def split_groups(per):
    cut = max(1, (2 * per) // 5)
    return [(0, cut), (cut, per)]


def body(
    tokens,
    segment_ids,
    expert_choices,
    attn_gain,
    query_weight,
    key_weight,
    value_weight,
    output_weight,
    ffn_gain,
    router_weight,
    expert_gate,
    expert_up,
    expert_down,
    cotangent,
):
    size = lax.axis_size("dp")
    owners = lax.axis_size("expert")
    paired = size == 8 and owners == 4
    me = lax.axis_index("dp").astype(jnp.int32).reshape(1)
    z = lax.axis_index("expert").astype(jnp.int32).reshape(1)
    seq, width = tokens.shape
    per = expert_gate.shape[0]
    experts = per * owners
    experts_pad = -(-experts // 8) * 8
    capacity = (seq * TOP * 9 + 8 * experts - 1) // (8 * experts)
    cap = -(-capacity // 16) * 16
    slim = query_weight.shape[0]
    segments = segment_ids.reshape(seq, 1)
    (a_first, a_last), (b_first, b_last) = split_groups(per)

    cots = lax.all_gather(cotangent, "expert", axis=0, tiled=True)
    packed = run_pack(query_weight, key_weight, value_weight, router_weight, attn_gain, ffn_gain)
    shards = jnp.stack([expert_gate, expert_up, jnp.swapaxes(expert_down, 1, 2)], axis=1)
    a_shard, b_shard = shards[a_first:a_last], shards[b_first:b_last]

    ids = jnp.arange(experts_pad, dtype=jnp.int32)
    hot = jnp.any(expert_choices[:, None, :] == ids[None, :, None], axis=2)
    hot = hot.astype(BF).T
    at = jnp.arange(seq, dtype=jnp.int32)
    earlier = (at[:, None] < at[None, :]).astype(BF)
    place = jnp.dot(hot, earlier, preferred_element_type=F32)
    place = jnp.where(hot > 0, place, -1.0).astype(BF)
    across = width // seq
    place = jnp.pad(place, ((0, EXTRA * across - experts_pad), (0, 0)))
    place = place.reshape(EXTRA // 8, across, 8, seq).swapaxes(1, 2).reshape(EXTRA, width)

    if paired:
        half = slim // 2
        full = [(0, 0, slim), (2, 0, slim), (4, 0, slim), (6, 0, slim)]
        full += [(m + 1, first, rows) for m, first, rows in full]
        split = [(0, 0, slim), (2, 0, slim), (4, 0, slim), (6, 0, half), (6, half, half)]
        split += [(m + 1, first, rows) for m, first, rows in split]
        order = segment_ids
        qx, qy, q1 = (swap(packed, bit, size) for bit in (2, 4, 1))
        order, qx, qy, q1 = wait(order, qx, qy, q1)
        qa, qb = swap(qx[:half], 4, size), swap(qy[half:], 2, size)
        q3 = swap(qx, 1, size)
        o_shard = hold(order, output_weight)
        ox, oy = swap(o_shard, 2, size), swap(o_shard, 4, size)
        order, qa, qb, q3 = wait(order, qa, qb, q3)
        q5, q6, q7 = swap(hold(order, qy), 1, size), swap(qa, 1, size), swap(qb, 1, size)
        order, q5, q6, q7, ox, oy = wait(order, q5, q6, q7, ox, oy)
        qkv_pieces = ([packed, qx, qy, qa, qb, q1, q3, q5, q6, q7], split)
        oc, o3, o5 = swap(oy, 2, size), swap(ox, 1, size), swap(oy, 1, size)
        ay, o1 = swap(hold(order, a_shard), 4, size), swap(hold(order, output_weight), 1, size)
        low_one, qkv, ctx, probs, extra = run_attention(
            me, hold(order, tokens), segment_ids, segments, qkv_pieces, size, experts_pad + 16
        )
        order, ctx, oc, o3, o5, o1 = wait(order, ctx, oc, o3, o5, o1)
        o7, ax = swap(oc, 1, size), swap(hold(order, a_shard), 2, size)
        order, o7, cots = wait(order, o7, cots)
        out_pieces = ([output_weight, ox, oy, oc, o1, o3, o5, o7], full)
        res, low_two = run_residual(
            me, hold(order, tokens), ctx, extra, place, out_pieces, size
        )
        order, low_two, ay = wait(order, low_two, ay)
        far, near = cross(low_two, 2), cross(low_two, 1)
        held = hold(order, b_shard)
        by, bx = swap(held, 4, size), swap(held, 2, size)
        order, ax = wait(order, ax)
        ac = swap(ax, 4, size)
        order, far, near = wait(order, far, near)
        middle = along(hold(order, low_two), [(1, 2), (2, 1)])
        passed = along(far, [(2, 3), (1, 0)])
        order, middle, passed, by, bx = wait(order, middle, passed, by, bx)
        xs = [low_two, near, far, middle, passed]
        low_all = lax.all_gather(hold(order, low_one), "expert", axis=0, tiled=True)
        ba, bb = swap(bx[..., :half, :], 4, size), swap(by[..., half:, :], 2, size)
        a1, a3, a5 = (swap(hold(order, v), 1, size) for v in (a_shard, ax, ay))
        pos, p, own_p, xs[3] = run_router(z, hold(order, extra), xs, per, owners)
        xs = xs[:owners]
        order, p, ac, a1, a3, a5 = wait(order, p, ac, a1, a3, a5)
        a7, b3, b5 = swap(ac, 1, size), swap(hold(order, bx), 1, size), swap(hold(order, by), 1, size)
        order, a7 = wait(order, a7)
        b1 = swap(hold(order, b_shard), 1, size)
        a_pieces = ([a_shard, ax, ay, ac, a1, a3, a5, a7], full)
    else:
        qkv_pieces = plain_shards(packed, size)
        out_pieces = plain_shards(output_weight, size)
        a_pieces, b_pieces = plain_shards(a_shard, size), plain_shards(b_shard, size)
        low_one, qkv, ctx, probs, extra = run_attention(
            me, tokens, segment_ids, segments, qkv_pieces, size, experts_pad + 16
        )
        res, low_two = run_residual(me, tokens, ctx, extra, place, out_pieces, size)
        xs = plain_owners(low_two, owners)
        low_all = lax.all_gather(low_one, "expert", axis=0, tiled=True)
        pos, p, own_p, _ = run_router(z, extra, xs, per, owners)
        order = p
    low_all = low_all.reshape(owners, width, seq)

    a_rows = run_experts(
        me, z, pos, hold(order, p), xs, cots, a_pieces, None, size, a_first, a_last - a_first, cap
    )
    if paired:
        order, a_gate, ba, bb, b1, b3, b5 = wait(order, a_rows[2], ba, bb, b1, b3, b5)
        b6, b7 = swap(ba, 1, size), swap(bb, 1, size)
        order, b6, b7 = wait(order, b6, b7)
        b_pieces = ([b_shard, bx, by, ba, bb, b1, b3, b5, b6, b7], split)
    b_rows = run_experts(
        me, z, pos, hold(order, p), xs, cots, b_pieces, a_rows[3], size, b_first, b_last - b_first, cap
    )
    expert_total = lax.psum_scatter(b_rows[3], "dp", scatter_dimension=0, tiled=False)
    expert_total = expert_total.astype(F32)
    expert_outputs = (
        expert_total[:, 0],
        expert_total[:, 1],
        jnp.swapaxes(expert_total[:, 2], 1, 2),
    )
    back_rows = ([a_rows[1], b_rows[1]], [a_rows[2], b_rows[2]], cap, experts_pad)
    last_part = run_combine_back(z, pos, *back_rows, owners - 1, 1)[0]
    if paired:
        order, last_part = wait(order, last_part)
        passed, middle = along(last_part, [(3, 2), (0, 1)]), along(last_part, [(1, 2), (2, 1)])
    else:
        order = last_part
    backs = run_combine_back(z, hold(order, pos), *back_rows, 0, owners - 1)
    backs = [*backs, last_part]
    out_rows = [a_rows[0], b_rows[0]]
    if paired:
        outs = run_combine_out(hold(order, pos), out_rows, cap)
        order, passed, middle, *outs = wait(order, passed, middle, *outs)
        far, near = cross(add(backs[2], passed), 2), cross(hold(order, backs[1]), 1)
        order, far, near = wait(order, far, near)
        backs = [backs[0], near, far, middle]
        last_out = hold(order, outs[3])
        passed, middle = along(last_out, [(3, 2), (0, 1)]), along(last_out, [(1, 2), (2, 1)])
    else:
        outs = run_combine_out(pos, out_rows, cap)
        backs = plain_return(backs, owners)
        outs = plain_return(outs, owners)
        order = backs[0]
    res_grad, ctx_grad, ext_grad, o_own, o_other = run_second(
        me, own_p, hold(order, extra), low_two, res, cotangent, ctx, backs, out_pieces, size, per
    )
    back, blocks = run_heads(ctx_grad, qkv, probs, owners)
    if paired:
        order, blocks, back, passed, middle = wait(order, blocks, back, passed, middle)
    back_all = exchange(blocks)
    if paired:
        o_other = swap(hold(order, o_other), 1, size)
        order, o_other = wait(order, o_other)
        mid = width // 2
        o_up, o_left = add(o_own[2:, :, :mid], o_other[2:, :, :mid]), add(
            o_own[1::2, :, mid:], o_other[1::2, :, mid:]
        )
        relay = add(outs[2], passed)
        order, o_up, o_left, relay = wait(order, o_up, o_left, relay)
        o_up, o_left = swap(o_up, 4, size), swap(o_left, 2, size)
    grad_tokens, ext_cols = run_first(
        me, hold(order, back), tokens, extra, ext_grad, res_grad, qkv_pieces, size
    )
    if paired:
        order, ext_cols, o_up, o_left = wait(order, ext_cols, o_up, o_left)

        def three(*values):
            return sum(v.astype(F32) for v in values)

        o_second = three(o_own[1, :, :mid], o_other[1, :, :mid], o_up[1]).astype(BF)
        o_third = three(o_own[2, :, mid:], o_other[2, :, mid:], o_left[1]).astype(BF)
        o_first = three(o_own[0, :, :mid], o_other[0, :, :mid], o_up[0])
        o_last = three(o_own[0, :, mid:], o_other[0, :, mid:], o_left[0])
        order, back_all, o_second, o_third, o_first, o_last = wait(
            order, back_all, o_second, o_third, o_first, o_last
        )
        o_second, o_third = swap(o_second, 2, size), swap(o_third, 4, size)
        far_out, near_out = cross(hold(order, relay), 2), cross(hold(order, outs[1]), 1)
    parts = run_project(me, low_all, back_all, ext_cols, size)
    if paired:
        near = swap(parts[4], 1, size)
        order, near = wait(order, near)
        pair = [add(parts[m], near[m]) for m in (1, 2, 3)]
        order, o_second, o_third, *pair = wait(order, o_second, o_third, *pair)
        links = [swap(pair[m - 1], 2 * m, size) for m in (1, 2, 3)]
        o_total = jnp.concatenate(
            [three(o_first, o_second).astype(BF), three(o_last, o_third).astype(BF)], axis=1
        )
        o_parts = exchange(o_total)
        order, far_out, near_out = wait(order, far_out, near_out)
        order, o_parts, *links = wait(order, o_parts, *links)
        outs = [outs[0], near_out, far_out, middle]
        total = run_join([parts[0], near[0], *links], o_parts, owners)
        far, near = cross(total, 2), cross(total, 1)
        order, far, near = wait(order, far, near)
        middle_total = along(hold(order, total), [(1, 2), (2, 1)])
        passed_total = along(far, [(2, 3), (1, 0)])
        total = [total, near, far, middle_total, passed_total]
    else:
        total = lax.psum_scatter(parts[0], "dp", scatter_dimension=0, tiled=False)
        total = exchange(jnp.concatenate([total] * owners, axis=0))
    mixed = res
    for part in outs:
        mixed = mixed + part.astype(F32)
    mixed = mixed.astype(BF)
    if paired:
        last, mixed, *expert_outputs = wait(total[4], mixed, *expert_outputs)
        results = run_finish(z, [*total[:4], last], owners, experts)
        query_total, key_total, value_total, out_total, router_total, gain_one, gain_two = results
        router_total = router_total.T
    else:
        o_total = lax.psum_scatter(o_own, "dp", scatter_dimension=0, tiled=False)
        out_total = lax.psum(o_total, "expert").astype(F32)
        total = total.reshape(owners, slim, -1).astype(F32)
        wide, narrow = QW // owners, KW // owners

        def side_by_side(first, last):
            return jnp.concatenate([total[j, :, first:last] for j in range(owners)], axis=1)

        query_total = side_by_side(0, wide)
        key_total = side_by_side(wide, wide + narrow)
        value_total = side_by_side(wide + narrow, wide + 2 * narrow)
        ext_total = jnp.sum(total[:, :, wide + 2 * narrow :], axis=0)
        router_total = ext_total[:, :experts]
        gain_one, gain_two = ext_total[:, experts_pad], ext_total[:, experts_pad + 8]
    return (
        mixed,
        grad_tokens,
        gain_one,
        query_total,
        key_total,
        value_total,
        out_total,
        gain_two,
        router_total,
        *expert_outputs,
    )


def solution(mesh):
    return jax.shard_map(
        body,
        mesh=mesh,
        in_specs=(
            P(("dp", "expert"), None),
            P(("dp", "expert"), None),
            P(("dp", "expert"), None),
            P("dp"),
            P("dp", None),
            P("dp", None),
            P("dp", None),
            P("dp", None),
            P("dp"),
            P("dp", None),
            P("expert", "dp", None),
            P("expert", "dp", None),
            P("expert", None, "dp"),
            P(("dp", "expert"), None),
        ),
        out_specs=(
            P(("dp", "expert"), None),
            P(("dp", "expert"), None),
            P("dp"),
            P("dp", None),
            P("dp", None),
            P("dp", None),
            P("dp", None),
            P("dp"),
            P("dp", None),
            P("expert", "dp", None),
            P("expert", "dp", None),
            P("expert", None, "dp"),
        ),
        check_vma=False,
    )
```

```python
import functools

import jax
import jax.numpy as jnp
from jax import lax
from jax.experimental import pallas as pl
from jax.experimental.pallas import tpu as pltpu
from jax.sharding import PartitionSpec as P

HEADS = 24
KV_HEADS = 8
HEAD_DIM = 64
TOP = 8
GROUPS = HEADS // KV_HEADS
QW = HEADS * HEAD_DIM
KW = KV_HEADS * HEAD_DIM
QKV = QW + 2 * KW
EXT = 128
HALVES = 2
EXTRA = 16
COST_SCALE = 1.0

norm_eps = 1e-06
masked_score = -1e30
BF = jnp.bfloat16
F32 = jnp.float32
ANY = pl.BlockSpec(memory_space=pl.ANY)
VMEM = pl.BlockSpec(memory_space=pltpu.VMEM)
SMEM = pl.BlockSpec(memory_space=pltpu.SMEM)
VMEM_LIMIT = 56 * 1024 * 1024


def dot(a, b, ca=1, cb=0):
    return lax.dot_general(a, b, (((ca,), (cb,)), ((), ())), preferred_element_type=F32)


def params():
    return pltpu.CompilerParams(vmem_limit_bytes=VMEM_LIMIT)


def cost(us):
    return pl.CostEstimate(
        flops=int(us * 1.1e9), bytes_accessed=int(us * 3.6e6 * COST_SCALE), transcendentals=0
    )


def sds(shape, dtype):
    return jax.ShapeDtypeStruct(shape, dtype)


def swap(value, bit, size):
    return lax.ppermute(value, "dp", [(i, i ^ bit) for i in range(size)])


def wait(order, *values):
    return lax.optimization_barrier((order,) + values)


def hold(order, value):
    return lax.optimization_barrier((order, value))[1]


def plain_shards(shard, size):
    rows = shard.shape[-2]
    arrays = [lax.all_gather(shard, "dp", axis=0, tiled=False)]
    return arrays, [(i, 0, rows) for i in range(size)]


def add(a, b):
    return (a.astype(F32) + b.astype(F32)).astype(BF)


def owner_at(z, r, owners):
    return jnp.bitwise_xor(z, r) if owners == 4 else lax.rem(z - r + owners, owners)


def along(value, pairs):
    return lax.ppermute(value, "expert", pairs)


def cross(value, bit):
    return along(value, [(i, i ^ bit) for i in range(4)])


def plain_owners(value, owners):
    turns = [[(i, (i + r) % owners) for i in range(owners)] for r in range(1, owners)]
    return [value] + [along(value, pairs) for pairs in turns]


def plain_return(parts, owners):
    turns = [[(i, (i - r) % owners) for i in range(owners)] for r in range(1, owners)]
    return [parts[0]] + [along(v, pairs) for v, pairs in zip(parts[1:], turns)]


def exchange(value):
    return lax.all_to_all(value, "expert", split_axis=0, concat_axis=0, tiled=True)


def part_shapes(size, shape):
    if size != 8:
        return [sds((size,) + shape, BF)]
    return [sds(shape, BF)] * 4 + [sds((4,) + shape, BF)]


def fetch(me, refs, plan, target, sems, rows, size):
    copies = []
    for n, (i, start, count) in enumerate(plan):
        source = refs[0].at[i] if len(refs) == 1 else refs[n]
        at = (jnp.bitwise_xor(me, i) if size == 8 else i) * rows + start
        if size == 8:
            at = pl.multiple_of(at, rows // 2)
        copies.append(pltpu.make_async_copy(source, target(pl.ds(at, count)), sems.at[n]))
    for c in copies:
        c.start()
    return copies


def pair_refs(own, other, size):
    if size != 8:
        return [own]
    return [(other if i % 2 else own).at[i // 2] for i in range(size)]


def store_parts(me, source, outs, sems, rows, size):
    copies = []
    for i in range(size):
        if len(outs) == 1:
            target, at = outs[0].at[i], i * rows
        else:
            target = outs[i]
            at = pl.multiple_of(jnp.bitwise_xor(me, i) * rows, rows)
        copies.append(pltpu.make_async_copy(source(pl.ds(at, rows)), target, sems.at[i]))
    for c in copies:
        c.start()
    return copies


def pack_kernel(experts, q, k, v, router, gain_one, gain_two, out):
    rows = q.shape[0]
    pad = -(-experts // 8) * 8
    out[:, :QW] = q[...]
    out[:, QW : QW + KW] = k[...]
    out[:, QW + KW : QKV] = v[...]
    gains = [jnp.broadcast_to(g[...].astype(F32)[None, :], (8, rows)) for g in (gain_one, gain_two)]
    parts = [router[...].astype(F32)]
    if pad > experts:
        parts.append(jnp.zeros((pad - experts, rows), F32))
    parts += gains + [jnp.zeros((EXT - pad - 16, rows), F32)]
    out[:, QKV:] = jnp.concatenate(parts, axis=0).T.astype(BF)


def run_pack(q, k, v, router, gain_one, gain_two):
    rows, experts = router.shape
    return pl.pallas_call(
        functools.partial(pack_kernel, experts),
        name="pack",
        out_shape=sds((rows, QKV + EXT), BF),
        in_specs=[VMEM] * 6,
        out_specs=VMEM,
        compiler_params=params(),
        cost_estimate=cost(0.01),
    )(q, k, v, router.T, gain_one, gain_two)


def attention_kernel(size, rows, plan, me, tok, seg_row, seg_col, *rest):
    refs, rest = rest[:-7], rest[-7:]
    low_out, qkv_out, ctx_out, prob_out, ext_out, w, sems = rest
    copies = fetch(me[0], refs, plan, lambda s: w.at[s], sems, rows, size)
    seq = tok.shape[0]
    x = tok[...].astype(F32)
    factor = lax.rsqrt(jnp.mean(x * x, axis=-1, keepdims=True) + norm_eps)
    normed = x * factor
    same = seg_col[...] == seg_row[...]
    key_at = lax.broadcasted_iota(jnp.int32, (seq, seq), 0)
    query_at = lax.broadcasted_iota(jnp.int32, (seq, seq), 1)
    allowed = jnp.where(same & (key_at <= query_at), 0.0, masked_score)
    allowed = jnp.concatenate([allowed] * GROUPS, axis=1)
    for c in copies:
        c.wait()
    ext = w[:, QKV:].astype(F32).T[: ext_out.shape[0], :]
    ext_out[...] = ext
    experts_pad = ext_out.shape[0] - 16
    gain = ext[experts_pad : experts_pad + 1, :]
    low = (normed * gain).astype(BF)
    step = 512
    for j in range(low.shape[1] // step):
        at = slice(j * step, (j + 1) * step)
        low_out[at, :] = low[:, at].astype(F32).T.astype(BF)
    for j in range(QKV // step):
        at = slice(j * step, (j + 1) * step)
        part = dot(low, w[:, at])
        qkv_out[at, :] = part.T.astype(BF)
    for h in range(KV_HEADS):
        q = jnp.concatenate(
            [
                qkv_out[(GROUPS * h + g) * HEAD_DIM : (GROUPS * h + g + 1) * HEAD_DIM, :]
                for g in range(GROUPS)
            ],
            axis=1,
        )
        k = qkv_out[QW + h * HEAD_DIM : QW + (h + 1) * HEAD_DIM, :]
        v = qkv_out[QW + KW + h * HEAD_DIM : QW + KW + (h + 1) * HEAD_DIM, :]
        scores = dot(k, q, 0, 0) * HEAD_DIM ** (-0.5)
        scores = jnp.where(allowed < 0.0, masked_score, scores)
        top = jnp.max(scores, axis=0, keepdims=True)
        shifted = jnp.exp(scores - top)
        probs = (shifted * (1.0 / jnp.sum(shifted, axis=0, keepdims=True))).astype(BF)
        prob_out[h] = probs
        ctx = dot(v, probs).astype(BF)
        for g in range(GROUPS):
            at = (GROUPS * h + g) * HEAD_DIM
            ctx_out[at : at + HEAD_DIM, :] = ctx[:, g * seq : (g + 1) * seq]


def run_attention(me, tokens, seg_row, seg_col, pieces, size, ext_rows):
    seq, width = tokens.shape
    rows = width // size
    arrays, plan = pieces
    return pl.pallas_call(
        functools.partial(attention_kernel, size, rows, plan),
        name="attention",
        out_shape=[
            sds((width, seq), BF),
            sds((QKV, seq), BF),
            sds((QW, seq), BF),
            sds((KV_HEADS, seq, GROUPS * seq), BF),
            sds((ext_rows, width), F32),
        ],
        in_specs=[SMEM, VMEM, VMEM, VMEM] + [ANY] * len(arrays),
        out_specs=[VMEM] * 5,
        scratch_shapes=[
            pltpu.VMEM((width, QKV + EXT), BF),
            pltpu.SemaphoreType.DMA((len(plan),)),
        ],
        compiler_params=params(),
        cost_estimate=cost(0.01),
    )(me, tokens, seg_row, seg_col, *arrays)


def residual_kernel(size, rows, plan, me, tok, ctx, ext, place, *rest):
    refs, (res_out, low_out, w, sems) = rest[:-4], rest[-4:]
    copies = fetch(me[0], refs, plan, lambda s: w.at[s], sems, rows, size)
    experts_pad = ext.shape[0] - 16
    for c in copies:
        c.wait()
    res = tok[...].astype(F32) + dot(ctx[...], w[...], 0, 0)
    res_out[...] = res
    factor = lax.rsqrt(jnp.mean(res * res, axis=-1, keepdims=True) + norm_eps)
    seq = res.shape[0]
    low_out[:seq, :] = (res * factor * ext[experts_pad + 8 : experts_pad + 9, :]).astype(BF)
    low_out[seq:, :] = place[...]


def run_residual(me, tokens, ctx, ext, place, pieces, size):
    seq, width = tokens.shape
    rows = QW // size
    arrays, plan = pieces
    return pl.pallas_call(
        functools.partial(residual_kernel, size, rows, plan),
        name="residual",
        out_shape=[sds((seq, width), F32), sds((seq + EXTRA, width), BF)],
        in_specs=[SMEM, VMEM, VMEM, VMEM, VMEM] + [ANY] * len(arrays),
        out_specs=[VMEM] * 2,
        scratch_shapes=[pltpu.VMEM((QW, width), BF), pltpu.SemaphoreType.DMA((len(plan),))],
        compiler_params=params(),
        cost_estimate=cost(0.01),
    )(me, tokens, ctx, ext, place, *arrays)


def slot_of(block, seq, width):
    across = width // seq
    row, col = block // across * 8, block % across * seq
    return slice(row, row + 8), slice(col, col + seq)


def router_kernel(owners, per, z, ext, *rest):
    given, rest = rest[:-6], rest[-6:]
    pos_out, p_out, own_out, last_out, all_p, all_pos = rest
    if len(given) > owners:
        inner = (z[0] == 1) | (z[0] == 2)

        @pl.when(inner)
        def _():
            last_out[...] = given[owners - 1][...]

        @pl.when(jnp.logical_not(inner))
        def _():
            last_out[...] = given[owners][...]
    else:
        last_out[...] = given[owners - 1][...]
    rows = list(given[: owners - 1]) + [last_out]
    experts_pad = ext.shape[0] - 16
    seq, width = rows[0].shape[0] - EXTRA, rows[0].shape[1]
    router = ext[:experts_pad, :].astype(BF)
    at = z[0] * per
    for r in range(owners):
        logits = dot(router, rows[r][:seq, :], 1, 1)
        spots = rows[r][seq:, :].astype(F32)
        for b in range(experts_pad // 8):
            of, to = slot_of(b, seq, width)
            all_pos[b * 8 : (b + 1) * 8, :] = spots[of, to]
        where = all_pos[...]
        named = where >= 0.0
        logits = jnp.where(named, logits, masked_score)
        top = jnp.max(logits, axis=0, keepdims=True)
        shifted = jnp.where(named, jnp.exp(logits - top), 0.0)
        probs = shifted / jnp.sum(shifted, axis=0, keepdims=True)
        all_p[...] = probs
        if r == 0:
            own_out[...] = probs
        for l in range(per):
            p_out[l, r : r + 1, :] = all_p[pl.ds(at + l, 1), :]
            pos_out[l, r : r + 1, :] = all_pos[pl.ds(at + l, 1), :].astype(jnp.int32)


def run_router(z, ext, rows, per, owners):
    seq = rows[0].shape[0] - EXTRA
    experts_pad = ext.shape[0] - 16
    return pl.pallas_call(
        functools.partial(router_kernel, owners, per),
        name="router",
        out_shape=[
            sds((per, owners, seq), jnp.int32),
            sds((per, owners, seq), F32),
            sds((experts_pad, seq), F32),
            sds(rows[0].shape, BF),
        ],
        in_specs=[SMEM, VMEM] + [VMEM] * len(rows),
        out_specs=[VMEM] * 4,
        scratch_shapes=[pltpu.VMEM((experts_pad, seq), F32)] * 2,
        compiler_params=params(),
        cost_estimate=cost(0.01),
    )(z, ext, *rows)


def load_rows(owners, z, xs, cs, xv, cv, sem_x, sem_c):
    seq = xv.shape[1]
    copies = []
    for r in range(owners):
        start = pl.multiple_of(owner_at(z[0], r, owners) * seq, seq)
        copies.append(pltpu.make_async_copy(xs[r].at[pl.ds(0, seq)], xv.at[r], sem_x.at[r]))
        copies.append(pltpu.make_async_copy(cs.at[pl.ds(start, seq)], cv.at[r], sem_c.at[r]))
    for c in copies:
        c.start()

    def wait(r):
        copies[2 * r].wait()
        copies[2 * r + 1].wait()

    return wait


def pick_rows(owners, cap, number, pos, p, xv, cv, xr, cr, prow, wait_rows):
    seq = xv.shape[1]
    slot = lax.broadcasted_iota(jnp.int32, (cap, seq), 0)
    for r in range(owners):
        hot = pos[number, r : r + 1, :] == slot
        low_hot = jnp.where(hot, 1.0, 0.0).astype(BF)
        at = pl.ds(r * cap, cap)
        if wait_rows is not None:
            wait_rows(r)
        xr[at, :] = dot(low_hot, xv[r]).astype(BF)
        cr[at, :] = dot(low_hot, cv[r]).astype(BF)
        prow[at, :] = jnp.sum(jnp.where(hot, p[number, r : r + 1, :], 0.0), axis=1, keepdims=True)


def through_expert(owners, cap, number, pos, xr, cr, prow, w, hp, gg, ug, gate, gate_out):
    ff = w.shape[2]
    step = ff // HALVES
    gate[...] = jnp.zeros_like(gate)
    for j in range(HALVES):
        cols = slice(j * step, (j + 1) * step)
        gate_pre = dot(xr[...], w[0, :, cols])
        up_pre = dot(xr[...], w[1, :, cols])
        back = dot(cr[...], w[2, :, cols])
        probs = prow[...]
        s = jax.nn.sigmoid(gate_pre)
        silu = gate_pre * s
        hidden = silu * up_pre
        gate[...] += jnp.sum(hidden * back, axis=1, keepdims=True)
        hp[:, cols] = (hidden * probs).astype(BF)
        back = back * probs
        gg[:, cols] = (back * up_pre * (s + silu * (1.0 - s))).astype(BF)
        ug[:, cols] = (back * silu).astype(BF)
    seq = pos.shape[2]
    slot = lax.broadcasted_iota(jnp.int32, (cap, seq), 0)
    for r in range(owners):
        hot = pos[number, r : r + 1, :] == slot
        at = pl.ds(r * cap, cap)
        gate_out[r : r + 1, :] = jnp.sum(jnp.where(hot, gate[at, :], 0.0), axis=0, keepdims=True)


def load_weights(me, refs, plan, w, sems, slot_at, rows, size):
    shards = [ref.at[:, slot_at] if len(refs) == 1 else ref.at[slot_at] for ref in refs]
    return fetch(me, shards, plan, lambda s: w.at[:, s, :], sems, rows, size)


def weight_grads(xr, cr, hp, gg, ug, g, grads, sems, slot_at, rows, size):
    width = xr.shape[1]
    tile = width // HALVES
    for j in range(HALVES):
        cols = slice(j * tile, (j + 1) * tile)
        g[0, cols, :] = dot(xr[:, cols], gg[...], 0, 0).astype(BF)
        g[1, cols, :] = dot(xr[:, cols], ug[...], 0, 0).astype(BF)
        g[2, cols, :] = dot(cr[:, cols], hp[...], 0, 0).astype(BF)
    copies = [
        pltpu.make_async_copy(g.at[:, pl.ds(i * rows, rows), :], grads.at[i, slot_at], sems.at[i])
        for i in range(size)
    ]
    for c in copies:
        c.start()
    return copies


def rows_back(w, gg, ug, bv):
    tile = bv.shape[1] // HALVES
    for j in range(HALVES):
        cols = slice(j * tile, (j + 1) * tile)
        total = dot(gg[...], w[0, cols, :], 1, 1) + dot(ug[...], w[1, cols, :], 1, 1)
        bv[:, cols] = total.astype(BF)


def rows_out(w, hp, ov):
    tile = ov.shape[1] // HALVES
    for j in range(HALVES):
        cols = slice(j * tile, (j + 1) * tile)
        ov[:, cols] = dot(hp[...], w[cols, :], 1, 1).astype(BF)


def experts_kernel(size, rows, owners, cap, first, many, plan, count, me, z, pos, p, cs, *rest):
    xs, refs, rest = rest[:owners], rest[owners : owners + count], rest[owners + count :]
    if first > 0:
        rest = rest[1:]
    out_rows, back_rows, gate_out, grads = rest[:4]
    xv, cv, w, xr, cr, prow, hp, gg, ug, gate, ov, bv, g, sem_x, sem_c, sem_w, sem_g, sem_o = rest[4:]
    wait_rows = load_rows(owners, z, xs, cs, xv, cv, sem_x, sem_c)

    def load(i):
        return load_weights(me[0], refs, plan, w.at[i % 2], sem_w.at[i % 2], i, rows, size)

    coming = load(0)
    leaving = []
    for i in range(many):
        here = i % 2
        number = first + i
        pick_rows(
            owners, cap, number, pos, p, xv, cv, xr, cr, prow, wait_rows if i == 0 else None
        )
        for c in coming:
            c.wait()
        if i + 1 < many:
            coming = load(i + 1)
        if len(leaving) > 1:
            for c in leaving[i - 2]:
                c.wait()
        through_expert(
            owners, cap, number, pos, xr, cr, prow, w.at[here], hp, gg, ug, gate, gate_out.at[i]
        )
        copies = weight_grads(
            xr, cr, hp, gg, ug, g.at[here], grads, sem_g.at[here], number, rows, size
        )
        rows_back(w.at[here], gg, ug, bv.at[here])
        copies.append(pltpu.make_async_copy(bv.at[here], back_rows.at[i], sem_o.at[here, 0]))
        copies[-1].start()
        rows_out(w.at[here, 2], hp, ov.at[here])
        copies.append(pltpu.make_async_copy(ov.at[here], out_rows.at[i], sem_o.at[here, 1]))
        copies[-1].start()
        leaving.append(copies)
    for copies in leaving[-2:]:
        for c in copies:
            c.wait()


def run_experts(me, z, pos, p, xs, cs, pieces, buffer, size, first, many, cap):
    per, owners, seq = pos.shape
    width = xs[0].shape[1]
    refs, plan = pieces
    ff = refs[0].shape[-1]
    rows = width // size
    total = owners * cap
    given = [me, z, pos, p, cs, *xs, *refs] + ([] if buffer is None else [buffer])
    return pl.pallas_call(
        functools.partial(
            experts_kernel, size, rows, owners, cap, first, many, plan, len(refs)
        ),
        name="experts",
        out_shape=[
            sds((many, total, width), BF),
            sds((many, total, width), BF),
            sds((many, owners, seq), F32),
            sds((size, per, 3, rows, ff), BF),
        ],
        in_specs=[SMEM, SMEM, VMEM, VMEM] + [ANY] * (len(given) - 4),
        out_specs=[ANY, ANY, VMEM, ANY],
        input_output_aliases={} if buffer is None else {len(given) - 1: 3},
        scratch_shapes=[
            pltpu.VMEM((owners, seq, width), BF),
            pltpu.VMEM((owners, seq, width), BF),
            pltpu.VMEM((2, 3, width, ff), BF),
            pltpu.VMEM((total, width), BF),
            pltpu.VMEM((total, width), BF),
            pltpu.VMEM((total, 1), F32),
            pltpu.VMEM((total, ff), BF),
            pltpu.VMEM((total, ff), BF),
            pltpu.VMEM((total, ff), BF),
            pltpu.VMEM((total, 1), F32),
            pltpu.VMEM((2, total, width), BF),
            pltpu.VMEM((2, total, width), BF),
            pltpu.VMEM((2, 3, width, ff), BF),
            pltpu.SemaphoreType.DMA((owners,)),
            pltpu.SemaphoreType.DMA((owners,)),
            pltpu.SemaphoreType.DMA((2, len(plan))),
            pltpu.SemaphoreType.DMA((2, size)),
            pltpu.SemaphoreType.DMA((2, 2)),
        ],
        compiler_params=params(),
        cost_estimate=cost(0.01),
    )(*given)


def combined_rows(per, cap, pos, r, rows):
    seq = pos.shape[2]
    slot = lax.broadcasted_iota(jnp.int32, (cap, seq), 0)
    hot = jnp.concatenate(
        [jnp.where(pos[l, pl.ds(r, 1), :] == slot, 1.0, 0.0).astype(BF) for l in range(per)], axis=0
    )
    total, at = 0.0, 0
    for group in rows:
        count = group.shape[0] * cap
        total = total + dot(hot[at : at + count], group[...].reshape(count, -1), 0, 0)
        at += count
    return total.astype(BF)


def combine_back_kernel(start, owners, per, cap, experts_pad, groups, z, pos, *rest):
    rows, gates, rest = rest[:groups], rest[groups : 2 * groups], rest[2 * groups :]
    outs, block = rest[:owners], rest[owners]
    step = pl.program_id(0)
    r = step + start
    seq, width = pos.shape[2], outs[0].shape[1]
    total = combined_rows(per, cap, pos, r, rows)
    block[...] = jnp.zeros_like(block)
    gates = [group.at[l] for group in gates for l in range(group.shape[0])]
    for l in range(per):
        block[pl.ds(z[0] * per + l, 1), :] = gates[l][pl.ds(r, 1), :]
    value = block[...]
    high = value.astype(BF)
    low = (value - high.astype(F32)).astype(BF)
    for o in range(owners):

        @pl.when(step == o)
        def _():
            outs[o][:seq, :] = total
            outs[o][seq:, :] = jnp.zeros((EXTRA, width), BF)
            both = jnp.concatenate([high, low], axis=0).astype(F32)
            for row in range(EXTRA // 8):
                across = width // seq
                blocks = [
                    both[(row * across + b) * 8 : (row * across + b + 1) * 8, :]
                    if row * across + b < 2 * experts_pad // 8
                    else jnp.zeros((8, seq), F32)
                    for b in range(across)
                ]
                outs[o][seq + row * 8 : seq + row * 8 + 8, :] = jnp.concatenate(
                    blocks, axis=1
                ).astype(BF)


def whole(shape):
    return pl.BlockSpec(shape, lambda r: (0,) * len(shape))


def run_combine_back(z, pos, rows, gates, cap, experts_pad, start, owners):
    per, _, seq = pos.shape
    width = rows[0].shape[2]
    shapes = [sds((seq + EXTRA, width), BF)] * owners
    return pl.pallas_call(
        functools.partial(combine_back_kernel, start, owners, per, cap, experts_pad, len(rows)),
        name="combine_back",
        grid=(owners,),
        out_shape=shapes,
        in_specs=[SMEM, whole(pos.shape)]
        + [pl.BlockSpec((a.shape[0], cap, width), lambda r: (0, r + start, 0)) for a in rows]
        + [whole(a.shape) for a in gates],
        out_specs=[whole(s.shape) for s in shapes],
        scratch_shapes=[pltpu.VMEM((experts_pad, seq), F32)],
        compiler_params=params(),
        cost_estimate=cost(0.01),
    )(z, pos, *rows, *gates)


def combine_out_kernel(owners, per, cap, pos, *rest):
    rows, outs = rest[:-owners], rest[-owners:]
    r = pl.program_id(0)
    total = combined_rows(per, cap, pos, r, rows)
    for o in range(owners):

        @pl.when(r == o)
        def _():
            outs[o][...] = total


def run_combine_out(pos, rows, cap):
    per, owners, seq = pos.shape
    width = rows[0].shape[2]
    return pl.pallas_call(
        functools.partial(combine_out_kernel, owners, per, cap),
        name="combine_out",
        grid=(owners,),
        out_shape=[sds((seq, width), BF)] * owners,
        in_specs=[whole(pos.shape)]
        + [pl.BlockSpec((a.shape[0], cap, width), lambda r: (0, r, 0)) for a in rows],
        out_specs=[whole((seq, width))] * owners,
        compiler_params=params(),
        cost_estimate=cost(0.01),
    )(pos, *rows)


def join_kernel(owners, own, *rest):
    more, (parts, out) = rest[:-2], rest[-2:]
    rows, cols = own.shape
    total = own[...].astype(F32)
    for piece in more:
        total = total + piece[...].astype(F32)
    total = total.astype(BF)
    low = parts.shape[0] // owners
    summed = 0.0
    for r in range(owners):
        summed = summed + parts[r * low : (r + 1) * low, :].astype(F32)
    summed = summed.astype(BF)
    wide = summed.shape[1] // owners
    out[:, :cols] = total
    for k in range(owners):
        out[k * low : (k + 1) * low, cols:] = summed[:, k * wide : (k + 1) * wide]


def run_join(pieces, parts, owners):
    rows, cols = pieces[0].shape
    return pl.pallas_call(
        functools.partial(join_kernel, owners),
        name="join",
        out_shape=sds((rows, cols + parts.shape[1] // owners), BF),
        in_specs=[VMEM] * (len(pieces) + 1),
        out_specs=VMEM,
        compiler_params=params(),
        cost_estimate=cost(0.01),
    )(*pieces, parts)


def finish_kernel(owners, z, *rest):
    given, (query, key, value, out, router, gain_one, gain_two, last) = rest[:-8], rest[-8:]
    rows = query.shape[0]
    wide, narrow = QW // owners, KW // owners
    one = wide + 2 * narrow
    low, out_wide = rows // owners, out.shape[1] // owners
    inner = (z[0] == 1) | (z[0] == 2)

    @pl.when(inner)
    def _():
        last[...] = given[3][...]

    @pl.when(jnp.logical_not(inner))
    def _():
        last[...] = given[4][...]

    ext_sum = 0.0
    for r, ref in enumerate((given[0], given[1], given[2], last)):
        j = jnp.bitwise_xor(z[0], r)
        block = ref[...].astype(F32)
        query[:, pl.ds(pl.multiple_of(j * wide, wide), wide)] = block[:, :wide]
        slim = pl.ds(pl.multiple_of(j * narrow, narrow), narrow)
        key[:, slim] = block[:, wide : wide + narrow]
        value[:, slim] = block[:, wide + narrow : one]
        ext_sum = ext_sum + block[:, one : one + EXT]
        to = pl.ds(pl.multiple_of(j * low, low), low)
        for k in range(owners):
            out[to, k * out_wide : (k + 1) * out_wide] = block[
                k * low : (k + 1) * low, one + EXT :
            ]
    ext_sum = ext_sum.T
    experts = router.shape[0]
    pad = -(-experts // 8) * 8
    router[...] = ext_sum[:experts, :]
    gain_one[...] = ext_sum[pad, :]
    gain_two[...] = ext_sum[pad + 8, :]


def run_finish(z, given, owners, experts):
    rows, cols = given[0].shape
    width = (cols - EXT - (QW + 2 * KW) // owners) * owners
    return pl.pallas_call(
        functools.partial(finish_kernel, owners),
        name="finish",
        out_shape=[
            sds((rows, QW), F32),
            sds((rows, KW), F32),
            sds((rows, KW), F32),
            sds((rows, width), F32),
            sds((experts, rows), F32),
            sds((rows,), F32),
            sds((rows,), F32),
        ],
        in_specs=[SMEM] + [VMEM] * len(given),
        out_specs=[VMEM] * 7,
        scratch_shapes=[pltpu.VMEM((rows, cols), BF)],
        compiler_params=params(),
        cost_estimate=cost(0.01),
    )(z, *given)


def second_kernel(
    size, rows, owners, per, plan, count, me, own_p, ext, low_two, res, cot, ctx, *rest
):
    backs, rest = rest[:owners], rest[owners:]
    refs, rest = rest[:count], rest[count:]
    res_grad, ctx_grad, ext_grad, own, other, w, g, gate, sems, sems_g = rest
    copies = fetch(me[0], refs, plan, lambda s: w.at[s], sems, rows, size)
    experts_pad = own_p.shape[0]
    seq, width = res.shape
    arrived = backs[0][seq:, :].astype(F32)
    for r in range(1, owners):
        arrived = arrived + backs[r][seq:, :].astype(F32)
    for b in range(experts_pad // 8):
        high_at = slot_of(b, seq, width)
        low_at = slot_of(b + experts_pad // 8, seq, width)
        gate[b * 8 : (b + 1) * 8, :] = arrived[high_at] + arrived[low_at]
    p = own_p[...]
    gate_grad = gate[...]
    weighted = jnp.sum(p * gate_grad, axis=0, keepdims=True)
    logit_grad = (p * (gate_grad - weighted)).astype(BF)
    router = ext[:experts_pad, :].astype(BF)
    ext_grad[:experts_pad, :] = dot(logit_grad, low_two[:seq, :])
    two = dot(logit_grad, router, 0, 0)
    for r in range(owners):
        two = two + backs[r][:seq, :].astype(F32)
    values = res[...]
    factor = lax.rsqrt(jnp.mean(values * values, axis=-1, keepdims=True) + norm_eps)
    normed = values * factor
    ext_grad[experts_pad:, :] = jnp.broadcast_to(
        jnp.sum(two * normed, axis=0, keepdims=True), (16, normed.shape[1])
    )
    scaled = two * ext[experts_pad + 8 : experts_pad + 9, :]
    inward = factor * (scaled - normed * jnp.mean(scaled * normed, axis=-1, keepdims=True))
    total = cot[...].astype(F32) + inward
    res_grad[...] = total
    low = total.astype(BF)
    step = QW // 4
    for j in range(4):
        at = slice(j * step, (j + 1) * step)
        g[at, :] = dot(ctx[at, :], low).astype(BF)
    copies_g = store_parts(me[0], lambda s: g.at[s], pair_refs(own, other, size), sems_g, rows, size)
    for c in copies:
        c.wait()
    for j in range(4):
        at = slice(j * step, (j + 1) * step)
        ctx_grad[at, :] = dot(w[at, :], low, 1, 1).astype(BF)
    for c in copies_g:
        c.wait()


def run_second(me, own_p, ext, low_two, res, cot, ctx, backs, pieces, size, per):
    owners = len(backs)
    arrays, plan = pieces
    seq, width = res.shape
    rows = QW // size
    experts_pad = own_p.shape[0]
    return pl.pallas_call(
        functools.partial(second_kernel, size, rows, owners, per, plan, len(arrays)),
        name="second_back",
        out_shape=[
            sds((seq, width), F32),
            sds((QW, seq), BF),
            sds((experts_pad + 16, width), F32),
            sds((size if size != 8 else 4, rows, width), BF),
            sds((4, rows, width), BF),
        ],
        in_specs=[SMEM] + [VMEM] * (6 + owners) + [ANY] * len(arrays),
        out_specs=[VMEM] * 3 + [ANY] * 2,
        scratch_shapes=[
            pltpu.VMEM((QW, width), BF),
            pltpu.VMEM((QW, width), BF),
            pltpu.VMEM((experts_pad, seq), F32),
            pltpu.SemaphoreType.DMA((len(plan),)),
            pltpu.SemaphoreType.DMA((size,)),
        ],
        compiler_params=params(),
        cost_estimate=cost(0.01),
    )(me, own_p, ext, low_two, res, cot, ctx, *backs, *arrays)


def heads_kernel(ctx_grad, qkv, probs, back, blocks):
    seq = qkv.shape[1]
    scale = HEAD_DIM ** (-0.5)
    for h in range(KV_HEADS):

        def heads(ref):
            return jnp.concatenate(
                [
                    ref[(GROUPS * h + i) * HEAD_DIM : (GROUPS * h + i + 1) * HEAD_DIM, :]
                    for i in range(GROUPS)
                ],
                axis=1,
            )

        upstream = heads(ctx_grad)
        q = heads(qkv)
        k = qkv[QW + h * HEAD_DIM : QW + (h + 1) * HEAD_DIM, :]
        v = qkv[QW + KW + h * HEAD_DIM : QW + KW + (h + 1) * HEAD_DIM, :]
        low_p = probs[h]
        weights = low_p.astype(F32)
        prob_grad = dot(v, upstream, 0, 0)
        inner = jnp.sum(prob_grad * weights, axis=0, keepdims=True)
        score_grad = (weights * (prob_grad - inner)).astype(BF)
        value_grad = dot(upstream, low_p, 1, 1)
        key_grad = dot(q, score_grad, 1, 1) * scale
        query_grad = dot(k, score_grad) * scale
        back[QW + h * HEAD_DIM : QW + (h + 1) * HEAD_DIM, :] = key_grad.astype(BF)
        back[QW + KW + h * HEAD_DIM : QW + KW + (h + 1) * HEAD_DIM, :] = value_grad.astype(BF)
        for i in range(GROUPS):
            at = (GROUPS * h + i) * HEAD_DIM
            back[at : at + HEAD_DIM, :] = query_grad[:, i * seq : (i + 1) * seq].astype(BF)
    owners = blocks.shape[0] // seq
    wide, slim = QW // owners, KW // owners
    for j in range(owners):
        block = jnp.concatenate(
            [
                back[j * wide : (j + 1) * wide, :],
                back[QW + j * slim : QW + (j + 1) * slim, :],
                back[QW + KW + j * slim : QW + KW + (j + 1) * slim, :],
            ],
            axis=0,
        )
        blocks[j * seq : (j + 1) * seq, :] = block.astype(F32).T.astype(BF)


def run_heads(ctx_grad, qkv, probs, owners):
    seq = qkv.shape[1]
    return pl.pallas_call(
        heads_kernel,
        name="heads_back",
        out_shape=[sds((QKV, seq), BF), sds((owners * seq, QKV // owners), BF)],
        in_specs=[VMEM] * 3,
        out_specs=[VMEM] * 2,
        compiler_params=params(),
        cost_estimate=cost(0.01),
    )(ctx_grad, qkv, probs)


def first_kernel(size, rows, plan, me, back, tok, ext, ext_grad, res_grad, *rest):
    refs, (tok_grad, ext_cols, w, sems) = rest[:-4], rest[-4:]
    copies = fetch(me[0], refs, plan, lambda s: w.at[s], sems, rows, size)
    for c in copies:
        c.wait()
    one = dot(back[...], w[:, :QKV], 0, 1)
    x = tok[...].astype(F32)
    factor = lax.rsqrt(jnp.mean(x * x, axis=-1, keepdims=True) + norm_eps)
    normed = x * factor
    experts_pad = ext.shape[0] - 16
    gain = ext[experts_pad : experts_pad + 1, :]
    gain_grad = jnp.sum(one * normed, axis=0, keepdims=True)
    packed = jnp.concatenate(
        [
            ext_grad[:experts_pad, :],
            jnp.broadcast_to(gain_grad, (8, gain_grad.shape[1])),
            ext_grad[experts_pad + 8 :, :],
            jnp.zeros((EXT - experts_pad - 16, gain_grad.shape[1]), F32),
        ],
        axis=0,
    )
    ext_cols[...] = packed.T.astype(BF)
    scaled = one * gain
    inward = factor * (scaled - normed * jnp.mean(scaled * normed, axis=-1, keepdims=True))
    tok_grad[...] = res_grad[...] + inward


def run_first(me, back, tokens, ext, ext_grad, res_grad, pieces, size):
    arrays, plan = pieces
    seq, width = tokens.shape
    rows = width // size
    return pl.pallas_call(
        functools.partial(first_kernel, size, rows, plan),
        name="first_back",
        out_shape=[sds((seq, width), F32), sds((width, EXT), BF)],
        in_specs=[SMEM] + [VMEM] * 5 + [ANY] * len(arrays),
        out_specs=[VMEM] * 2,
        scratch_shapes=[
            pltpu.VMEM((width, QKV + EXT), BF),
            pltpu.SemaphoreType.DMA((len(plan),)),
        ],
        compiler_params=params(),
        cost_estimate=cost(60),
    )(me, back, tokens, ext, ext_grad, res_grad, *arrays)


def project_kernel(size, rows, me, low_all, back_all, ext_cols, *rest):
    grads, (g, sems_g) = rest[:-2], rest[-2:]
    owners, _, seq = low_all.shape
    cols = back_all.shape[1]
    g[:, cols:] = ext_cols[...]
    total = 0.0
    for r in range(owners):
        total = total + dot(low_all[r], back_all[r * seq : (r + 1) * seq, :])
    g[:, :cols] = total.astype(BF)
    if size == 8:
        grads = [grads[4].at[i // 2] if i % 2 else grads[i // 2] for i in range(size)]
    copies_g = store_parts(me[0], lambda s: g.at[s], grads, sems_g, rows, size)
    for c in copies_g:
        c.wait()


def run_project(me, low_all, back_all, ext_cols, size):
    width, cols = low_all.shape[1], back_all.shape[1] + EXT
    rows = width // size
    grads = part_shapes(size, (rows, cols))
    return pl.pallas_call(
        functools.partial(project_kernel, size, rows),
        name="project_back",
        out_shape=grads,
        in_specs=[SMEM] + [VMEM] * 3,
        out_specs=[ANY] * len(grads),
        scratch_shapes=[pltpu.VMEM((width, cols), BF), pltpu.SemaphoreType.DMA((size,))],
        compiler_params=params(),
        cost_estimate=cost(60),
    )(me, low_all, back_all, ext_cols)


def split_groups(per):
    cut = max(1, (2 * per) // 5)
    return [(0, cut), (cut, per)]


def body(
    tokens,
    segment_ids,
    expert_choices,
    attn_gain,
    query_weight,
    key_weight,
    value_weight,
    output_weight,
    ffn_gain,
    router_weight,
    expert_gate,
    expert_up,
    expert_down,
    cotangent,
):
    size = lax.axis_size("dp")
    owners = lax.axis_size("expert")
    paired = size == 8 and owners == 4
    me = lax.axis_index("dp").astype(jnp.int32).reshape(1)
    z = lax.axis_index("expert").astype(jnp.int32).reshape(1)
    seq, width = tokens.shape
    per = expert_gate.shape[0]
    experts = per * owners
    experts_pad = -(-experts // 8) * 8
    capacity = (seq * TOP * 9 + 8 * experts - 1) // (8 * experts)
    cap = -(-capacity // 16) * 16
    slim = query_weight.shape[0]
    segments = segment_ids.reshape(seq, 1)
    (a_first, a_last), (b_first, b_last) = split_groups(per)

    cots = lax.all_gather(cotangent, "expert", axis=0, tiled=True)
    packed = run_pack(query_weight, key_weight, value_weight, router_weight, attn_gain, ffn_gain)
    shards = jnp.stack([expert_gate, expert_up, jnp.swapaxes(expert_down, 1, 2)], axis=1)
    a_shard, b_shard = shards[a_first:a_last], shards[b_first:b_last]

    ids = jnp.arange(experts_pad, dtype=jnp.int32)
    hot = jnp.any(expert_choices[:, None, :] == ids[None, :, None], axis=2)
    hot = hot.astype(BF).T
    at = jnp.arange(seq, dtype=jnp.int32)
    earlier = (at[:, None] < at[None, :]).astype(BF)
    place = jnp.dot(hot, earlier, preferred_element_type=F32)
    place = jnp.where(hot > 0, place, -1.0).astype(BF)
    across = width // seq
    place = jnp.pad(place, ((0, EXTRA * across - experts_pad), (0, 0)))
    place = place.reshape(EXTRA // 8, across, 8, seq).swapaxes(1, 2).reshape(EXTRA, width)

    if paired:
        half = slim // 2
        full = [(0, 0, slim), (2, 0, slim), (4, 0, slim), (6, 0, slim)]
        full += [(m + 1, first, rows) for m, first, rows in full]
        split = [(0, 0, slim), (2, 0, slim), (4, 0, slim), (6, 0, half), (6, half, half)]
        split += [(m + 1, first, rows) for m, first, rows in split]
        order = segment_ids
        qx, qy, q1 = (swap(packed, bit, size) for bit in (2, 4, 1))
        order, qx, qy, q1 = wait(order, qx, qy, q1)
        qa, qb = swap(qx[:half], 4, size), swap(qy[half:], 2, size)
        q3 = swap(qx, 1, size)
        o_shard = hold(order, output_weight)
        ox, oy = swap(o_shard, 2, size), swap(o_shard, 4, size)
        order, qa, qb, q3 = wait(order, qa, qb, q3)
        q5, q6, q7 = swap(hold(order, qy), 1, size), swap(qa, 1, size), swap(qb, 1, size)
        order, q5, q6, q7, ox, oy = wait(order, q5, q6, q7, ox, oy)
        qkv_pieces = ([packed, qx, qy, qa, qb, q1, q3, q5, q6, q7], split)
        oc, o3, o5 = swap(oy, 2, size), swap(ox, 1, size), swap(oy, 1, size)
        ay, o1 = swap(hold(order, a_shard), 4, size), swap(hold(order, output_weight), 1, size)
        low_one, qkv, ctx, probs, extra = run_attention(
            me, hold(order, tokens), segment_ids, segments, qkv_pieces, size, experts_pad + 16
        )
        order, ctx, oc, o3, o5, o1 = wait(order, ctx, oc, o3, o5, o1)
        o7, ax = swap(oc, 1, size), swap(hold(order, a_shard), 2, size)
        order, o7, cots = wait(order, o7, cots)
        out_pieces = ([output_weight, ox, oy, oc, o1, o3, o5, o7], full)
        res, low_two = run_residual(
            me, hold(order, tokens), ctx, extra, place, out_pieces, size
        )
        order, low_two, ay = wait(order, low_two, ay)
        far, near = cross(low_two, 2), cross(low_two, 1)
        held = hold(order, b_shard)
        by, bx = swap(held, 4, size), swap(held, 2, size)
        order, ax = wait(order, ax)
        ac = swap(ax, 4, size)
        order, far, near = wait(order, far, near)
        middle = along(hold(order, low_two), [(1, 2), (2, 1)])
        passed = along(far, [(2, 3), (1, 0)])
        order, by, bx = wait(order, by, bx)
        order, b_left, b_up = wait(order, bx[..., :half, :], by[..., half:, :])
        order, middle, passed = wait(order, middle, passed)
        xs = [low_two, near, far, middle, passed]
        low_all = lax.all_gather(hold(order, low_one), "expert", axis=0, tiled=True)
        ba, bb = swap(b_left, 4, size), swap(b_up, 2, size)
        a1, a3, a5 = (swap(hold(order, v), 1, size) for v in (a_shard, ax, ay))
        pos, p, own_p, xs[3] = run_router(z, hold(order, extra), xs, per, owners)
        xs = xs[:owners]
        order, p, ac, a1, a3, a5 = wait(order, p, ac, a1, a3, a5)
        a7, b3, b5 = swap(ac, 1, size), swap(hold(order, bx), 1, size), swap(hold(order, by), 1, size)
        order, a7 = wait(order, a7)
        b1 = swap(hold(order, b_shard), 1, size)
        a_pieces = ([a_shard, ax, ay, ac, a1, a3, a5, a7], full)
    else:
        qkv_pieces = plain_shards(packed, size)
        out_pieces = plain_shards(output_weight, size)
        a_pieces, b_pieces = plain_shards(a_shard, size), plain_shards(b_shard, size)
        low_one, qkv, ctx, probs, extra = run_attention(
            me, tokens, segment_ids, segments, qkv_pieces, size, experts_pad + 16
        )
        res, low_two = run_residual(me, tokens, ctx, extra, place, out_pieces, size)
        xs = plain_owners(low_two, owners)
        low_all = lax.all_gather(low_one, "expert", axis=0, tiled=True)
        pos, p, own_p, _ = run_router(z, extra, xs, per, owners)
        order = p
    low_all = low_all.reshape(owners, width, seq)

    a_rows = run_experts(
        me, z, pos, hold(order, p), xs, cots, a_pieces, None, size, a_first, a_last - a_first, cap
    )
    if paired:
        order, a_gate, ba, bb, b1, b3, b5 = wait(order, a_rows[2], ba, bb, b1, b3, b5)
        b6, b7 = swap(ba, 1, size), swap(bb, 1, size)
        order, b6, b7 = wait(order, b6, b7)
        b_pieces = ([b_shard, bx, by, ba, bb, b1, b3, b5, b6, b7], split)
    b_rows = run_experts(
        me, z, pos, hold(order, p), xs, cots, b_pieces, a_rows[3], size, b_first, b_last - b_first, cap
    )
    expert_total = lax.psum_scatter(b_rows[3], "dp", scatter_dimension=0, tiled=False)
    expert_total = expert_total.astype(F32)
    expert_outputs = (
        expert_total[:, 0],
        expert_total[:, 1],
        jnp.swapaxes(expert_total[:, 2], 1, 2),
    )
    back_rows = ([a_rows[1], b_rows[1]], [a_rows[2], b_rows[2]], cap, experts_pad)
    last_part = run_combine_back(z, pos, *back_rows, owners - 1, 1)[0]
    if paired:
        order, last_part = wait(order, last_part)
        passed, middle = along(last_part, [(3, 2), (0, 1)]), along(last_part, [(1, 2), (2, 1)])
    else:
        order = last_part
    backs = run_combine_back(z, hold(order, pos), *back_rows, 0, owners - 1)
    backs = [*backs, last_part]
    out_rows = [a_rows[0], b_rows[0]]
    if paired:
        outs = run_combine_out(hold(order, pos), out_rows, cap)
        order, passed, middle, *outs = wait(order, passed, middle, *outs)
        far, near = cross(add(backs[2], passed), 2), cross(hold(order, backs[1]), 1)
        order, far, near = wait(order, far, near)
        backs = [backs[0], near, far, middle]
        last_out = hold(order, outs[3])
        passed, middle = along(last_out, [(3, 2), (0, 1)]), along(last_out, [(1, 2), (2, 1)])
    else:
        outs = run_combine_out(pos, out_rows, cap)
        backs = plain_return(backs, owners)
        outs = plain_return(outs, owners)
        order = backs[0]
    res_grad, ctx_grad, ext_grad, o_own, o_other = run_second(
        me, own_p, hold(order, extra), low_two, res, cotangent, ctx, backs, out_pieces, size, per
    )
    back, blocks = run_heads(ctx_grad, qkv, probs, owners)
    if paired:
        order, blocks, back, passed, middle = wait(order, blocks, back, passed, middle)
    back_all = exchange(blocks)
    if paired:
        o_other = swap(hold(order, o_other), 1, size)
        order, o_other = wait(order, o_other)
        mid = width // 2
        o_up, o_left = add(o_own[2:, :, :mid], o_other[2:, :, :mid]), add(
            o_own[1::2, :, mid:], o_other[1::2, :, mid:]
        )
        relay = add(outs[2], passed)
        order, o_up, o_left, relay = wait(order, o_up, o_left, relay)
        o_up, o_left = swap(o_up, 4, size), swap(o_left, 2, size)
    grad_tokens, ext_cols = run_first(
        me, hold(order, back), tokens, extra, ext_grad, res_grad, qkv_pieces, size
    )
    if paired:
        order, ext_cols, o_up, o_left = wait(order, ext_cols, o_up, o_left)

        def three(*values):
            return sum(v.astype(F32) for v in values)

        o_second = three(o_own[1, :, :mid], o_other[1, :, :mid], o_up[1]).astype(BF)
        o_third = three(o_own[2, :, mid:], o_other[2, :, mid:], o_left[1]).astype(BF)
        o_first = three(o_own[0, :, :mid], o_other[0, :, :mid], o_up[0])
        o_last = three(o_own[0, :, mid:], o_other[0, :, mid:], o_left[0])
        order, back_all, o_second, o_third, o_first, o_last = wait(
            order, back_all, o_second, o_third, o_first, o_last
        )
        o_second, o_third = swap(o_second, 2, size), swap(o_third, 4, size)
        far_out, near_out = cross(hold(order, relay), 2), cross(hold(order, outs[1]), 1)
    parts = run_project(me, low_all, back_all, ext_cols, size)
    if paired:
        near = swap(parts[4], 1, size)
        order, near = wait(order, near)
        pair = [add(parts[m], near[m]) for m in (1, 2, 3)]
        order, o_second, o_third, *pair = wait(order, o_second, o_third, *pair)
        links = [swap(pair[m - 1], 2 * m, size) for m in (1, 2, 3)]
        o_total = jnp.concatenate(
            [three(o_first, o_second).astype(BF), three(o_last, o_third).astype(BF)], axis=1
        )
        o_parts = exchange(o_total)
        order, far_out, near_out = wait(order, far_out, near_out)
        order, o_parts, *links = wait(order, o_parts, *links)
        outs = [outs[0], near_out, far_out, middle]
        total = run_join([parts[0], near[0], *links], o_parts, owners)
        far, near = cross(total, 2), cross(total, 1)
        order, far, near = wait(order, far, near)
        middle_total = along(hold(order, total), [(1, 2), (2, 1)])
        passed_total = along(far, [(2, 3), (1, 0)])
        total = [total, near, far, middle_total, passed_total]
    else:
        total = lax.psum_scatter(parts[0], "dp", scatter_dimension=0, tiled=False)
        total = exchange(jnp.concatenate([total] * owners, axis=0))
    mixed = res
    for part in outs:
        mixed = mixed + part.astype(F32)
    mixed = mixed.astype(BF)
    if paired:
        last, mixed, *expert_outputs = wait(total[4], mixed, *expert_outputs)
        results = run_finish(z, [*total[:4], last], owners, experts)
        query_total, key_total, value_total, out_total, router_total, gain_one, gain_two = results
        router_total = router_total.T
    else:
        o_total = lax.psum_scatter(o_own, "dp", scatter_dimension=0, tiled=False)
        out_total = lax.psum(o_total, "expert").astype(F32)
        total = total.reshape(owners, slim, -1).astype(F32)
        wide, narrow = QW // owners, KW // owners

        def side_by_side(first, last):
            return jnp.concatenate([total[j, :, first:last] for j in range(owners)], axis=1)

        query_total = side_by_side(0, wide)
        key_total = side_by_side(wide, wide + narrow)
        value_total = side_by_side(wide + narrow, wide + 2 * narrow)
        ext_total = jnp.sum(total[:, :, wide + 2 * narrow :], axis=0)
        router_total = ext_total[:, :experts]
        gain_one, gain_two = ext_total[:, experts_pad], ext_total[:, experts_pad + 8]
    return (
        mixed,
        grad_tokens,
        gain_one,
        query_total,
        key_total,
        value_total,
        out_total,
        gain_two,
        router_total,
        *expert_outputs,
    )


def solution(mesh):
    return jax.shard_map(
        body,
        mesh=mesh,
        in_specs=(
            P(("dp", "expert"), None),
            P(("dp", "expert"), None),
            P(("dp", "expert"), None),
            P("dp"),
            P("dp", None),
            P("dp", None),
            P("dp", None),
            P("dp", None),
            P("dp"),
            P("dp", None),
            P("expert", "dp", None),
            P("expert", "dp", None),
            P("expert", None, "dp"),
            P(("dp", "expert"), None),
        ),
        out_specs=(
            P(("dp", "expert"), None),
            P(("dp", "expert"), None),
            P("dp"),
            P("dp", None),
            P("dp", None),
            P("dp", None),
            P("dp", None),
            P("dp"),
            P("dp", None),
            P("expert", "dp", None),
            P("expert", "dp", None),
            P("expert", None, "dp"),
        ),
        check_vma=False,
    )
```

```python
import functools

import jax
import jax.numpy as jnp
from jax import lax
from jax.experimental import pallas as pl
from jax.experimental.pallas import tpu as pltpu
from jax.sharding import PartitionSpec as P

HEADS = 24
KV_HEADS = 8
HEAD_DIM = 64
TOP = 8
GROUPS = HEADS // KV_HEADS
QW = HEADS * HEAD_DIM
KW = KV_HEADS * HEAD_DIM
QKV = QW + 2 * KW
EXT = 128
HALVES = 2
EXTRA = 16
COST_SCALE = 1.0

norm_eps = 1e-06
masked_score = -1e30
BF = jnp.bfloat16
F32 = jnp.float32
ANY = pl.BlockSpec(memory_space=pl.ANY)
VMEM = pl.BlockSpec(memory_space=pltpu.VMEM)
SMEM = pl.BlockSpec(memory_space=pltpu.SMEM)
VMEM_LIMIT = 56 * 1024 * 1024


def dot(a, b, ca=1, cb=0):
    return lax.dot_general(a, b, (((ca,), (cb,)), ((), ())), preferred_element_type=F32)


def params():
    return pltpu.CompilerParams(vmem_limit_bytes=VMEM_LIMIT)


def cost(us):
    return pl.CostEstimate(
        flops=int(us * 1.1e9), bytes_accessed=int(us * 3.6e6 * COST_SCALE), transcendentals=0
    )


def sds(shape, dtype):
    return jax.ShapeDtypeStruct(shape, dtype)


def swap(value, bit, size):
    return lax.ppermute(value, "dp", [(i, i ^ bit) for i in range(size)])


def wait(order, *values):
    return lax.optimization_barrier((order,) + values)


def hold(order, value):
    return lax.optimization_barrier((order, value))[1]


def plain_shards(shard, size):
    rows = shard.shape[-2]
    arrays = [lax.all_gather(shard, "dp", axis=0, tiled=False)]
    return arrays, [(i, 0, rows) for i in range(size)]


def add(a, b):
    return (a.astype(F32) + b.astype(F32)).astype(BF)


def owner_at(z, r, owners):
    return jnp.bitwise_xor(z, r) if owners == 4 else lax.rem(z - r + owners, owners)


def along(value, pairs):
    return lax.ppermute(value, "expert", pairs)


def cross(value, bit):
    return along(value, [(i, i ^ bit) for i in range(4)])


def plain_owners(value, owners):
    turns = [[(i, (i + r) % owners) for i in range(owners)] for r in range(1, owners)]
    return [value] + [along(value, pairs) for pairs in turns]


def plain_return(parts, owners):
    turns = [[(i, (i - r) % owners) for i in range(owners)] for r in range(1, owners)]
    return [parts[0]] + [along(v, pairs) for v, pairs in zip(parts[1:], turns)]


def exchange(value):
    return lax.all_to_all(value, "expert", split_axis=0, concat_axis=0, tiled=True)


def part_shapes(size, shape):
    if size != 8:
        return [sds((size,) + shape, BF)]
    return [sds(shape, BF)] * 4 + [sds((4,) + shape, BF)]


def fetch(me, refs, plan, target, sems, rows, size):
    copies = []
    for n, (i, start, count) in enumerate(plan):
        source = refs[0].at[i] if len(refs) == 1 else refs[n]
        at = (jnp.bitwise_xor(me, i) if size == 8 else i) * rows + start
        if size == 8:
            at = pl.multiple_of(at, rows // 2)
        copies.append(pltpu.make_async_copy(source, target(pl.ds(at, count)), sems.at[n]))
    for c in copies:
        c.start()
    return copies


def pair_refs(own, other, size):
    if size != 8:
        return [own]
    return [(other if i % 2 else own).at[i // 2] for i in range(size)]


def store_parts(me, source, outs, sems, rows, size):
    copies = []
    for i in range(size):
        if len(outs) == 1:
            target, at = outs[0].at[i], i * rows
        else:
            target = outs[i]
            at = pl.multiple_of(jnp.bitwise_xor(me, i) * rows, rows)
        copies.append(pltpu.make_async_copy(source(pl.ds(at, rows)), target, sems.at[i]))
    for c in copies:
        c.start()
    return copies


def pack_kernel(experts, q, k, v, router, gain_one, gain_two, out):
    rows = q.shape[0]
    pad = -(-experts // 8) * 8
    out[:, :QW] = q[...]
    out[:, QW : QW + KW] = k[...]
    out[:, QW + KW : QKV] = v[...]
    gains = [jnp.broadcast_to(g[...].astype(F32)[None, :], (8, rows)) for g in (gain_one, gain_two)]
    parts = [router[...].astype(F32)]
    if pad > experts:
        parts.append(jnp.zeros((pad - experts, rows), F32))
    parts += gains + [jnp.zeros((EXT - pad - 16, rows), F32)]
    out[:, QKV:] = jnp.concatenate(parts, axis=0).T.astype(BF)


def run_pack(q, k, v, router, gain_one, gain_two):
    rows, experts = router.shape
    return pl.pallas_call(
        functools.partial(pack_kernel, experts),
        name="pack",
        out_shape=sds((rows, QKV + EXT), BF),
        in_specs=[VMEM] * 6,
        out_specs=VMEM,
        compiler_params=params(),
        cost_estimate=cost(0.01),
    )(q, k, v, router.T, gain_one, gain_two)


def attention_kernel(size, rows, plan, me, tok, seg_row, seg_col, *rest):
    refs, rest = rest[:-7], rest[-7:]
    low_out, qkv_out, ctx_out, prob_out, ext_out, w, sems = rest
    copies = fetch(me[0], refs, plan, lambda s: w.at[s], sems, rows, size)
    seq = tok.shape[0]
    x = tok[...].astype(F32)
    factor = lax.rsqrt(jnp.mean(x * x, axis=-1, keepdims=True) + norm_eps)
    normed = x * factor
    same = seg_col[...] == seg_row[...]
    key_at = lax.broadcasted_iota(jnp.int32, (seq, seq), 0)
    query_at = lax.broadcasted_iota(jnp.int32, (seq, seq), 1)
    allowed = jnp.where(same & (key_at <= query_at), 0.0, masked_score)
    allowed = jnp.concatenate([allowed] * GROUPS, axis=1)
    for c in copies:
        c.wait()
    ext = w[:, QKV:].astype(F32).T[: ext_out.shape[0], :]
    ext_out[...] = ext
    experts_pad = ext_out.shape[0] - 16
    gain = ext[experts_pad : experts_pad + 1, :]
    low = (normed * gain).astype(BF)
    step = 512
    for j in range(low.shape[1] // step):
        at = slice(j * step, (j + 1) * step)
        low_out[at, :] = low[:, at].astype(F32).T.astype(BF)
    for j in range(QKV // step):
        at = slice(j * step, (j + 1) * step)
        part = dot(low, w[:, at])
        qkv_out[at, :] = part.T.astype(BF)
    for h in range(KV_HEADS):
        q = jnp.concatenate(
            [
                qkv_out[(GROUPS * h + g) * HEAD_DIM : (GROUPS * h + g + 1) * HEAD_DIM, :]
                for g in range(GROUPS)
            ],
            axis=1,
        )
        k = qkv_out[QW + h * HEAD_DIM : QW + (h + 1) * HEAD_DIM, :]
        v = qkv_out[QW + KW + h * HEAD_DIM : QW + KW + (h + 1) * HEAD_DIM, :]
        scores = dot(k, q, 0, 0) * HEAD_DIM ** (-0.5)
        scores = jnp.where(allowed < 0.0, masked_score, scores)
        top = jnp.max(scores, axis=0, keepdims=True)
        shifted = jnp.exp(scores - top)
        probs = (shifted * (1.0 / jnp.sum(shifted, axis=0, keepdims=True))).astype(BF)
        prob_out[h] = probs
        ctx = dot(v, probs).astype(BF)
        for g in range(GROUPS):
            at = (GROUPS * h + g) * HEAD_DIM
            ctx_out[at : at + HEAD_DIM, :] = ctx[:, g * seq : (g + 1) * seq]


def run_attention(me, tokens, seg_row, seg_col, pieces, size, ext_rows):
    seq, width = tokens.shape
    rows = width // size
    arrays, plan = pieces
    return pl.pallas_call(
        functools.partial(attention_kernel, size, rows, plan),
        name="attention",
        out_shape=[
            sds((width, seq), BF),
            sds((QKV, seq), BF),
            sds((QW, seq), BF),
            sds((KV_HEADS, seq, GROUPS * seq), BF),
            sds((ext_rows, width), F32),
        ],
        in_specs=[SMEM, VMEM, VMEM, VMEM] + [ANY] * len(arrays),
        out_specs=[VMEM] * 5,
        scratch_shapes=[
            pltpu.VMEM((width, QKV + EXT), BF),
            pltpu.SemaphoreType.DMA((len(plan),)),
        ],
        compiler_params=params(),
        cost_estimate=cost(0.01),
    )(me, tokens, seg_row, seg_col, *arrays)


def residual_kernel(size, rows, plan, me, tok, ctx, ext, place, *rest):
    refs, (res_out, low_out, w, sems) = rest[:-4], rest[-4:]
    copies = fetch(me[0], refs, plan, lambda s: w.at[s], sems, rows, size)
    experts_pad = ext.shape[0] - 16
    for c in copies:
        c.wait()
    res = tok[...].astype(F32) + dot(ctx[...], w[...], 0, 0)
    res_out[...] = res
    factor = lax.rsqrt(jnp.mean(res * res, axis=-1, keepdims=True) + norm_eps)
    seq = res.shape[0]
    low_out[:seq, :] = (res * factor * ext[experts_pad + 8 : experts_pad + 9, :]).astype(BF)
    low_out[seq:, :] = place[...]


def run_residual(me, tokens, ctx, ext, place, pieces, size):
    seq, width = tokens.shape
    rows = QW // size
    arrays, plan = pieces
    return pl.pallas_call(
        functools.partial(residual_kernel, size, rows, plan),
        name="residual",
        out_shape=[sds((seq, width), F32), sds((seq + EXTRA, width), BF)],
        in_specs=[SMEM, VMEM, VMEM, VMEM, VMEM] + [ANY] * len(arrays),
        out_specs=[VMEM] * 2,
        scratch_shapes=[pltpu.VMEM((QW, width), BF), pltpu.SemaphoreType.DMA((len(plan),))],
        compiler_params=params(),
        cost_estimate=cost(0.01),
    )(me, tokens, ctx, ext, place, *arrays)


def slot_of(block, seq, width):
    across = width // seq
    row, col = block // across * 8, block % across * seq
    return slice(row, row + 8), slice(col, col + seq)


def router_kernel(owners, per, z, ext, *rest):
    given, rest = rest[:-6], rest[-6:]
    pos_out, p_out, own_out, last_out, all_p, all_pos = rest
    if len(given) > owners:
        inner = (z[0] == 1) | (z[0] == 2)

        @pl.when(inner)
        def _():
            last_out[...] = given[owners - 1][...]

        @pl.when(jnp.logical_not(inner))
        def _():
            last_out[...] = given[owners][...]
    else:
        last_out[...] = given[owners - 1][...]
    rows = list(given[: owners - 1]) + [last_out]
    experts_pad = ext.shape[0] - 16
    seq, width = rows[0].shape[0] - EXTRA, rows[0].shape[1]
    router = ext[:experts_pad, :].astype(BF)
    at = z[0] * per
    for r in range(owners):
        logits = dot(router, rows[r][:seq, :], 1, 1)
        spots = rows[r][seq:, :].astype(F32)
        for b in range(experts_pad // 8):
            of, to = slot_of(b, seq, width)
            all_pos[b * 8 : (b + 1) * 8, :] = spots[of, to]
        where = all_pos[...]
        named = where >= 0.0
        logits = jnp.where(named, logits, masked_score)
        top = jnp.max(logits, axis=0, keepdims=True)
        shifted = jnp.where(named, jnp.exp(logits - top), 0.0)
        probs = shifted / jnp.sum(shifted, axis=0, keepdims=True)
        all_p[...] = probs
        if r == 0:
            own_out[...] = probs
        for l in range(per):
            p_out[l, r : r + 1, :] = all_p[pl.ds(at + l, 1), :]
            pos_out[l, r : r + 1, :] = all_pos[pl.ds(at + l, 1), :].astype(jnp.int32)


def run_router(z, ext, rows, per, owners):
    seq = rows[0].shape[0] - EXTRA
    experts_pad = ext.shape[0] - 16
    return pl.pallas_call(
        functools.partial(router_kernel, owners, per),
        name="router",
        out_shape=[
            sds((per, owners, seq), jnp.int32),
            sds((per, owners, seq), F32),
            sds((experts_pad, seq), F32),
            sds(rows[0].shape, BF),
        ],
        in_specs=[SMEM, VMEM] + [VMEM] * len(rows),
        out_specs=[VMEM] * 4,
        scratch_shapes=[pltpu.VMEM((experts_pad, seq), F32)] * 2,
        compiler_params=params(),
        cost_estimate=cost(0.01),
    )(z, ext, *rows)


def load_rows(owners, z, xs, cs, xv, cv, sem_x, sem_c):
    seq = xv.shape[1]
    copies = []
    for r in range(owners):
        start = pl.multiple_of(owner_at(z[0], r, owners) * seq, seq)
        copies.append(pltpu.make_async_copy(xs[r].at[pl.ds(0, seq)], xv.at[r], sem_x.at[r]))
        copies.append(pltpu.make_async_copy(cs.at[pl.ds(start, seq)], cv.at[r], sem_c.at[r]))
    for c in copies:
        c.start()

    def wait(r):
        copies[2 * r].wait()
        copies[2 * r + 1].wait()

    return wait


def pick_rows(owners, cap, number, pos, p, xv, cv, xr, cr, prow, wait_rows):
    seq = xv.shape[1]
    slot = lax.broadcasted_iota(jnp.int32, (cap, seq), 0)
    for r in range(owners):
        hot = pos[number, r : r + 1, :] == slot
        low_hot = jnp.where(hot, 1.0, 0.0).astype(BF)
        at = pl.ds(r * cap, cap)
        if wait_rows is not None:
            wait_rows(r)
        xr[at, :] = dot(low_hot, xv[r]).astype(BF)
        cr[at, :] = dot(low_hot, cv[r]).astype(BF)
        prow[at, :] = jnp.sum(jnp.where(hot, p[number, r : r + 1, :], 0.0), axis=1, keepdims=True)


def through_expert(owners, cap, number, pos, xr, cr, prow, w, hp, gg, ug, gate, gate_out):
    ff = w.shape[2]
    step = ff // HALVES
    gate[...] = jnp.zeros_like(gate)
    for j in range(HALVES):
        cols = slice(j * step, (j + 1) * step)
        gate_pre = dot(xr[...], w[0, :, cols])
        up_pre = dot(xr[...], w[1, :, cols])
        back = dot(cr[...], w[2, :, cols])
        probs = prow[...]
        s = jax.nn.sigmoid(gate_pre)
        silu = gate_pre * s
        hidden = silu * up_pre
        gate[...] += jnp.sum(hidden * back, axis=1, keepdims=True)
        hp[:, cols] = (hidden * probs).astype(BF)
        back = back * probs
        gg[:, cols] = (back * up_pre * (s + silu * (1.0 - s))).astype(BF)
        ug[:, cols] = (back * silu).astype(BF)
    seq = pos.shape[2]
    slot = lax.broadcasted_iota(jnp.int32, (cap, seq), 0)
    for r in range(owners):
        hot = pos[number, r : r + 1, :] == slot
        at = pl.ds(r * cap, cap)
        gate_out[r : r + 1, :] = jnp.sum(jnp.where(hot, gate[at, :], 0.0), axis=0, keepdims=True)


def load_weights(me, refs, plan, w, sems, slot_at, rows, size):
    shards = [ref.at[:, slot_at] if len(refs) == 1 else ref.at[slot_at] for ref in refs]
    return fetch(me, shards, plan, lambda s: w.at[:, s, :], sems, rows, size)


def weight_grads(xr, cr, hp, gg, ug, g, grads, sems, slot_at, rows, size):
    width = xr.shape[1]
    tile = width // HALVES
    for j in range(HALVES):
        cols = slice(j * tile, (j + 1) * tile)
        g[0, cols, :] = dot(xr[:, cols], gg[...], 0, 0).astype(BF)
        g[1, cols, :] = dot(xr[:, cols], ug[...], 0, 0).astype(BF)
        g[2, cols, :] = dot(cr[:, cols], hp[...], 0, 0).astype(BF)
    copies = [
        pltpu.make_async_copy(g.at[:, pl.ds(i * rows, rows), :], grads.at[i, slot_at], sems.at[i])
        for i in range(size)
    ]
    for c in copies:
        c.start()
    return copies


def rows_back(w, gg, ug, bv):
    tile = bv.shape[1] // HALVES
    for j in range(HALVES):
        cols = slice(j * tile, (j + 1) * tile)
        total = dot(gg[...], w[0, cols, :], 1, 1) + dot(ug[...], w[1, cols, :], 1, 1)
        bv[:, cols] = total.astype(BF)


def rows_out(w, hp, ov):
    tile = ov.shape[1] // HALVES
    for j in range(HALVES):
        cols = slice(j * tile, (j + 1) * tile)
        ov[:, cols] = dot(hp[...], w[cols, :], 1, 1).astype(BF)


def experts_kernel(size, rows, owners, cap, first, many, plan, count, me, z, pos, p, cs, *rest):
    xs, refs, rest = rest[:owners], rest[owners : owners + count], rest[owners + count :]
    if first > 0:
        rest = rest[1:]
    out_rows, back_rows, gate_out, grads = rest[:4]
    xv, cv, w, xr, cr, prow, hp, gg, ug, gate, ov, bv, g, sem_x, sem_c, sem_w, sem_g, sem_o = rest[4:]
    wait_rows = load_rows(owners, z, xs, cs, xv, cv, sem_x, sem_c)

    def load(i):
        return load_weights(me[0], refs, plan, w.at[i % 2], sem_w.at[i % 2], i, rows, size)

    coming = load(0)
    leaving = []
    for i in range(many):
        here = i % 2
        number = first + i
        pick_rows(
            owners, cap, number, pos, p, xv, cv, xr, cr, prow, wait_rows if i == 0 else None
        )
        for c in coming:
            c.wait()
        if i + 1 < many:
            coming = load(i + 1)
        if len(leaving) > 1:
            for c in leaving[i - 2]:
                c.wait()
        through_expert(
            owners, cap, number, pos, xr, cr, prow, w.at[here], hp, gg, ug, gate, gate_out.at[i]
        )
        copies = weight_grads(
            xr, cr, hp, gg, ug, g.at[here], grads, sem_g.at[here], number, rows, size
        )
        rows_back(w.at[here], gg, ug, bv.at[here])
        copies.append(pltpu.make_async_copy(bv.at[here], back_rows.at[i], sem_o.at[here, 0]))
        copies[-1].start()
        rows_out(w.at[here, 2], hp, ov.at[here])
        copies.append(pltpu.make_async_copy(ov.at[here], out_rows.at[i], sem_o.at[here, 1]))
        copies[-1].start()
        leaving.append(copies)
    for copies in leaving[-2:]:
        for c in copies:
            c.wait()


def run_experts(me, z, pos, p, xs, cs, pieces, buffer, size, first, many, cap):
    per, owners, seq = pos.shape
    width = xs[0].shape[1]
    refs, plan = pieces
    ff = refs[0].shape[-1]
    rows = width // size
    total = owners * cap
    given = [me, z, pos, p, cs, *xs, *refs] + ([] if buffer is None else [buffer])
    return pl.pallas_call(
        functools.partial(
            experts_kernel, size, rows, owners, cap, first, many, plan, len(refs)
        ),
        name="experts",
        out_shape=[
            sds((many, total, width), BF),
            sds((many, total, width), BF),
            sds((many, owners, seq), F32),
            sds((size, per, 3, rows, ff), BF),
        ],
        in_specs=[SMEM, SMEM, VMEM, VMEM] + [ANY] * (len(given) - 4),
        out_specs=[ANY, ANY, VMEM, ANY],
        input_output_aliases={} if buffer is None else {len(given) - 1: 3},
        scratch_shapes=[
            pltpu.VMEM((owners, seq, width), BF),
            pltpu.VMEM((owners, seq, width), BF),
            pltpu.VMEM((2, 3, width, ff), BF),
            pltpu.VMEM((total, width), BF),
            pltpu.VMEM((total, width), BF),
            pltpu.VMEM((total, 1), F32),
            pltpu.VMEM((total, ff), BF),
            pltpu.VMEM((total, ff), BF),
            pltpu.VMEM((total, ff), BF),
            pltpu.VMEM((total, 1), F32),
            pltpu.VMEM((2, total, width), BF),
            pltpu.VMEM((2, total, width), BF),
            pltpu.VMEM((2, 3, width, ff), BF),
            pltpu.SemaphoreType.DMA((owners,)),
            pltpu.SemaphoreType.DMA((owners,)),
            pltpu.SemaphoreType.DMA((2, len(plan))),
            pltpu.SemaphoreType.DMA((2, size)),
            pltpu.SemaphoreType.DMA((2, 2)),
        ],
        compiler_params=params(),
        cost_estimate=cost(0.01),
    )(*given)


def combined_rows(per, cap, pos, r, rows):
    seq = pos.shape[2]
    slot = lax.broadcasted_iota(jnp.int32, (cap, seq), 0)
    hot = jnp.concatenate(
        [jnp.where(pos[l, pl.ds(r, 1), :] == slot, 1.0, 0.0).astype(BF) for l in range(per)], axis=0
    )
    total, at = 0.0, 0
    for group in rows:
        count = group.shape[0] * cap
        total = total + dot(hot[at : at + count], group[...].reshape(count, -1), 0, 0)
        at += count
    return total.astype(BF)


def combine_back_kernel(start, owners, per, cap, experts_pad, groups, z, pos, *rest):
    rows, gates, rest = rest[:groups], rest[groups : 2 * groups], rest[2 * groups :]
    outs, block = rest[:owners], rest[owners]
    step = pl.program_id(0)
    r = step + start
    seq, width = pos.shape[2], outs[0].shape[1]
    total = combined_rows(per, cap, pos, r, rows)
    block[...] = jnp.zeros_like(block)
    gates = [group.at[l] for group in gates for l in range(group.shape[0])]
    for l in range(per):
        block[pl.ds(z[0] * per + l, 1), :] = gates[l][pl.ds(r, 1), :]
    value = block[...]
    high = value.astype(BF)
    low = (value - high.astype(F32)).astype(BF)
    for o in range(owners):

        @pl.when(step == o)
        def _():
            outs[o][:seq, :] = total
            outs[o][seq:, :] = jnp.zeros((EXTRA, width), BF)
            both = jnp.concatenate([high, low], axis=0).astype(F32)
            for row in range(EXTRA // 8):
                across = width // seq
                blocks = [
                    both[(row * across + b) * 8 : (row * across + b + 1) * 8, :]
                    if row * across + b < 2 * experts_pad // 8
                    else jnp.zeros((8, seq), F32)
                    for b in range(across)
                ]
                outs[o][seq + row * 8 : seq + row * 8 + 8, :] = jnp.concatenate(
                    blocks, axis=1
                ).astype(BF)


def whole(shape):
    return pl.BlockSpec(shape, lambda r: (0,) * len(shape))


def run_combine_back(z, pos, rows, gates, cap, experts_pad, start, owners):
    per, _, seq = pos.shape
    width = rows[0].shape[2]
    shapes = [sds((seq + EXTRA, width), BF)] * owners
    return pl.pallas_call(
        functools.partial(combine_back_kernel, start, owners, per, cap, experts_pad, len(rows)),
        name="combine_back",
        grid=(owners,),
        out_shape=shapes,
        in_specs=[SMEM, whole(pos.shape)]
        + [pl.BlockSpec((a.shape[0], cap, width), lambda r: (0, r + start, 0)) for a in rows]
        + [whole(a.shape) for a in gates],
        out_specs=[whole(s.shape) for s in shapes],
        scratch_shapes=[pltpu.VMEM((experts_pad, seq), F32)],
        compiler_params=params(),
        cost_estimate=cost(0.01),
    )(z, pos, *rows, *gates)


def combine_out_kernel(owners, per, cap, pos, *rest):
    rows, outs = rest[:-owners], rest[-owners:]
    r = pl.program_id(0)
    total = combined_rows(per, cap, pos, r, rows)
    for o in range(owners):

        @pl.when(r == o)
        def _():
            outs[o][...] = total


def run_combine_out(pos, rows, cap):
    per, owners, seq = pos.shape
    width = rows[0].shape[2]
    return pl.pallas_call(
        functools.partial(combine_out_kernel, owners, per, cap),
        name="combine_out",
        grid=(owners,),
        out_shape=[sds((seq, width), BF)] * owners,
        in_specs=[whole(pos.shape)]
        + [pl.BlockSpec((a.shape[0], cap, width), lambda r: (0, r, 0)) for a in rows],
        out_specs=[whole((seq, width))] * owners,
        compiler_params=params(),
        cost_estimate=cost(0.01),
    )(pos, *rows)


def join_kernel(owners, own, *rest):
    more, (parts, out) = rest[:-2], rest[-2:]
    rows, cols = own.shape
    total = own[...].astype(F32)
    for piece in more:
        total = total + piece[...].astype(F32)
    total = total.astype(BF)
    low = parts.shape[0] // owners
    summed = 0.0
    for r in range(owners):
        summed = summed + parts[r * low : (r + 1) * low, :].astype(F32)
    summed = summed.astype(BF)
    wide = summed.shape[1] // owners
    out[:, :cols] = total
    for k in range(owners):
        out[k * low : (k + 1) * low, cols:] = summed[:, k * wide : (k + 1) * wide]


def run_join(pieces, parts, owners):
    rows, cols = pieces[0].shape
    return pl.pallas_call(
        functools.partial(join_kernel, owners),
        name="join",
        out_shape=sds((rows, cols + parts.shape[1] // owners), BF),
        in_specs=[VMEM] * (len(pieces) + 1),
        out_specs=VMEM,
        compiler_params=params(),
        cost_estimate=cost(0.01),
    )(*pieces, parts)


def finish_kernel(owners, z, *rest):
    given, (query, key, value, out, router, gain_one, gain_two, last) = rest[:-8], rest[-8:]
    rows = query.shape[0]
    wide, narrow = QW // owners, KW // owners
    one = wide + 2 * narrow
    low, out_wide = rows // owners, out.shape[1] // owners
    inner = (z[0] == 1) | (z[0] == 2)

    @pl.when(inner)
    def _():
        last[...] = given[3][...]

    @pl.when(jnp.logical_not(inner))
    def _():
        last[...] = given[4][...]

    ext_sum = 0.0
    for r, ref in enumerate((given[0], given[1], given[2], last)):
        j = jnp.bitwise_xor(z[0], r)
        block = ref[...].astype(F32)
        query[:, pl.ds(pl.multiple_of(j * wide, wide), wide)] = block[:, :wide]
        slim = pl.ds(pl.multiple_of(j * narrow, narrow), narrow)
        key[:, slim] = block[:, wide : wide + narrow]
        value[:, slim] = block[:, wide + narrow : one]
        ext_sum = ext_sum + block[:, one : one + EXT]
        to = pl.ds(pl.multiple_of(j * low, low), low)
        for k in range(owners):
            out[to, k * out_wide : (k + 1) * out_wide] = block[
                k * low : (k + 1) * low, one + EXT :
            ]
    ext_sum = ext_sum.T
    experts = router.shape[0]
    pad = -(-experts // 8) * 8
    router[...] = ext_sum[:experts, :]
    gain_one[...] = ext_sum[pad, :]
    gain_two[...] = ext_sum[pad + 8, :]


def run_finish(z, given, owners, experts):
    rows, cols = given[0].shape
    width = (cols - EXT - (QW + 2 * KW) // owners) * owners
    return pl.pallas_call(
        functools.partial(finish_kernel, owners),
        name="finish",
        out_shape=[
            sds((rows, QW), F32),
            sds((rows, KW), F32),
            sds((rows, KW), F32),
            sds((rows, width), F32),
            sds((experts, rows), F32),
            sds((rows,), F32),
            sds((rows,), F32),
        ],
        in_specs=[SMEM] + [VMEM] * len(given),
        out_specs=[VMEM] * 7,
        scratch_shapes=[pltpu.VMEM((rows, cols), BF)],
        compiler_params=params(),
        cost_estimate=cost(0.01),
    )(z, *given)


def second_kernel(
    size, rows, owners, per, plan, count, me, own_p, ext, low_two, res, cot, ctx, *rest
):
    backs, rest = rest[:owners], rest[owners:]
    refs, rest = rest[:count], rest[count:]
    res_grad, ctx_grad, ext_grad, own, other, w, g, gate, sems, sems_g = rest
    copies = fetch(me[0], refs, plan, lambda s: w.at[s], sems, rows, size)
    experts_pad = own_p.shape[0]
    seq, width = res.shape
    arrived = backs[0][seq:, :].astype(F32)
    for r in range(1, owners):
        arrived = arrived + backs[r][seq:, :].astype(F32)
    for b in range(experts_pad // 8):
        high_at = slot_of(b, seq, width)
        low_at = slot_of(b + experts_pad // 8, seq, width)
        gate[b * 8 : (b + 1) * 8, :] = arrived[high_at] + arrived[low_at]
    p = own_p[...]
    gate_grad = gate[...]
    weighted = jnp.sum(p * gate_grad, axis=0, keepdims=True)
    logit_grad = (p * (gate_grad - weighted)).astype(BF)
    router = ext[:experts_pad, :].astype(BF)
    ext_grad[:experts_pad, :] = dot(logit_grad, low_two[:seq, :])
    two = dot(logit_grad, router, 0, 0)
    for r in range(owners):
        two = two + backs[r][:seq, :].astype(F32)
    values = res[...]
    factor = lax.rsqrt(jnp.mean(values * values, axis=-1, keepdims=True) + norm_eps)
    normed = values * factor
    ext_grad[experts_pad:, :] = jnp.broadcast_to(
        jnp.sum(two * normed, axis=0, keepdims=True), (16, normed.shape[1])
    )
    scaled = two * ext[experts_pad + 8 : experts_pad + 9, :]
    inward = factor * (scaled - normed * jnp.mean(scaled * normed, axis=-1, keepdims=True))
    total = cot[...].astype(F32) + inward
    res_grad[...] = total
    low = total.astype(BF)
    step = QW // 4
    for j in range(4):
        at = slice(j * step, (j + 1) * step)
        g[at, :] = dot(ctx[at, :], low).astype(BF)
    copies_g = store_parts(me[0], lambda s: g.at[s], pair_refs(own, other, size), sems_g, rows, size)
    for c in copies:
        c.wait()
    for j in range(4):
        at = slice(j * step, (j + 1) * step)
        ctx_grad[at, :] = dot(w[at, :], low, 1, 1).astype(BF)
    for c in copies_g:
        c.wait()


def run_second(me, own_p, ext, low_two, res, cot, ctx, backs, pieces, size, per):
    owners = len(backs)
    arrays, plan = pieces
    seq, width = res.shape
    rows = QW // size
    experts_pad = own_p.shape[0]
    return pl.pallas_call(
        functools.partial(second_kernel, size, rows, owners, per, plan, len(arrays)),
        name="second_back",
        out_shape=[
            sds((seq, width), F32),
            sds((QW, seq), BF),
            sds((experts_pad + 16, width), F32),
            sds((size if size != 8 else 4, rows, width), BF),
            sds((4, rows, width), BF),
        ],
        in_specs=[SMEM] + [VMEM] * (6 + owners) + [ANY] * len(arrays),
        out_specs=[VMEM] * 3 + [ANY] * 2,
        scratch_shapes=[
            pltpu.VMEM((QW, width), BF),
            pltpu.VMEM((QW, width), BF),
            pltpu.VMEM((experts_pad, seq), F32),
            pltpu.SemaphoreType.DMA((len(plan),)),
            pltpu.SemaphoreType.DMA((size,)),
        ],
        compiler_params=params(),
        cost_estimate=cost(0.01),
    )(me, own_p, ext, low_two, res, cot, ctx, *backs, *arrays)


def heads_kernel(ctx_grad, qkv, probs, back, blocks):
    seq = qkv.shape[1]
    scale = HEAD_DIM ** (-0.5)
    for h in range(KV_HEADS):

        def heads(ref):
            return jnp.concatenate(
                [
                    ref[(GROUPS * h + i) * HEAD_DIM : (GROUPS * h + i + 1) * HEAD_DIM, :]
                    for i in range(GROUPS)
                ],
                axis=1,
            )

        upstream = heads(ctx_grad)
        q = heads(qkv)
        k = qkv[QW + h * HEAD_DIM : QW + (h + 1) * HEAD_DIM, :]
        v = qkv[QW + KW + h * HEAD_DIM : QW + KW + (h + 1) * HEAD_DIM, :]
        low_p = probs[h]
        weights = low_p.astype(F32)
        prob_grad = dot(v, upstream, 0, 0)
        inner = jnp.sum(prob_grad * weights, axis=0, keepdims=True)
        score_grad = (weights * (prob_grad - inner)).astype(BF)
        value_grad = dot(upstream, low_p, 1, 1)
        key_grad = dot(q, score_grad, 1, 1) * scale
        query_grad = dot(k, score_grad) * scale
        back[QW + h * HEAD_DIM : QW + (h + 1) * HEAD_DIM, :] = key_grad.astype(BF)
        back[QW + KW + h * HEAD_DIM : QW + KW + (h + 1) * HEAD_DIM, :] = value_grad.astype(BF)
        for i in range(GROUPS):
            at = (GROUPS * h + i) * HEAD_DIM
            back[at : at + HEAD_DIM, :] = query_grad[:, i * seq : (i + 1) * seq].astype(BF)
    owners = blocks.shape[0] // seq
    wide, slim = QW // owners, KW // owners
    for j in range(owners):
        block = jnp.concatenate(
            [
                back[j * wide : (j + 1) * wide, :],
                back[QW + j * slim : QW + (j + 1) * slim, :],
                back[QW + KW + j * slim : QW + KW + (j + 1) * slim, :],
            ],
            axis=0,
        )
        blocks[j * seq : (j + 1) * seq, :] = block.astype(F32).T.astype(BF)


def run_heads(ctx_grad, qkv, probs, owners):
    seq = qkv.shape[1]
    return pl.pallas_call(
        heads_kernel,
        name="heads_back",
        out_shape=[sds((QKV, seq), BF), sds((owners * seq, QKV // owners), BF)],
        in_specs=[VMEM] * 3,
        out_specs=[VMEM] * 2,
        compiler_params=params(),
        cost_estimate=cost(0.01),
    )(ctx_grad, qkv, probs)


def first_kernel(size, rows, plan, me, back, tok, ext, ext_grad, res_grad, *rest):
    refs, (tok_grad, ext_cols, w, sems) = rest[:-4], rest[-4:]
    copies = fetch(me[0], refs, plan, lambda s: w.at[s], sems, rows, size)
    for c in copies:
        c.wait()
    one = dot(back[...], w[:, :QKV], 0, 1)
    x = tok[...].astype(F32)
    factor = lax.rsqrt(jnp.mean(x * x, axis=-1, keepdims=True) + norm_eps)
    normed = x * factor
    experts_pad = ext.shape[0] - 16
    gain = ext[experts_pad : experts_pad + 1, :]
    gain_grad = jnp.sum(one * normed, axis=0, keepdims=True)
    packed = jnp.concatenate(
        [
            ext_grad[:experts_pad, :],
            jnp.broadcast_to(gain_grad, (8, gain_grad.shape[1])),
            ext_grad[experts_pad + 8 :, :],
            jnp.zeros((EXT - experts_pad - 16, gain_grad.shape[1]), F32),
        ],
        axis=0,
    )
    ext_cols[...] = packed.T.astype(BF)
    scaled = one * gain
    inward = factor * (scaled - normed * jnp.mean(scaled * normed, axis=-1, keepdims=True))
    tok_grad[...] = res_grad[...] + inward


def run_first(me, back, tokens, ext, ext_grad, res_grad, pieces, size):
    arrays, plan = pieces
    seq, width = tokens.shape
    rows = width // size
    return pl.pallas_call(
        functools.partial(first_kernel, size, rows, plan),
        name="first_back",
        out_shape=[sds((seq, width), F32), sds((width, EXT), BF)],
        in_specs=[SMEM] + [VMEM] * 5 + [ANY] * len(arrays),
        out_specs=[VMEM] * 2,
        scratch_shapes=[
            pltpu.VMEM((width, QKV + EXT), BF),
            pltpu.SemaphoreType.DMA((len(plan),)),
        ],
        compiler_params=params(),
        cost_estimate=cost(60),
    )(me, back, tokens, ext, ext_grad, res_grad, *arrays)


def project_kernel(size, rows, me, low_all, back_all, ext_cols, *rest):
    grads, (g, sems_g) = rest[:-2], rest[-2:]
    owners, _, seq = low_all.shape
    cols = back_all.shape[1]
    g[:, cols:] = ext_cols[...]
    total = 0.0
    for r in range(owners):
        total = total + dot(low_all[r], back_all[r * seq : (r + 1) * seq, :])
    g[:, :cols] = total.astype(BF)
    if size == 8:
        grads = [grads[4].at[i // 2] if i % 2 else grads[i // 2] for i in range(size)]
    copies_g = store_parts(me[0], lambda s: g.at[s], grads, sems_g, rows, size)
    for c in copies_g:
        c.wait()


def run_project(me, low_all, back_all, ext_cols, size):
    width, cols = low_all.shape[1], back_all.shape[1] + EXT
    rows = width // size
    grads = part_shapes(size, (rows, cols))
    return pl.pallas_call(
        functools.partial(project_kernel, size, rows),
        name="project_back",
        out_shape=grads,
        in_specs=[SMEM] + [VMEM] * 3,
        out_specs=[ANY] * len(grads),
        scratch_shapes=[pltpu.VMEM((width, cols), BF), pltpu.SemaphoreType.DMA((size,))],
        compiler_params=params(),
        cost_estimate=cost(60),
    )(me, low_all, back_all, ext_cols)


def split_groups(per):
    cut = max(1, (2 * per) // 5)
    return [(0, cut), (cut, per)]


def body(
    tokens,
    segment_ids,
    expert_choices,
    attn_gain,
    query_weight,
    key_weight,
    value_weight,
    output_weight,
    ffn_gain,
    router_weight,
    expert_gate,
    expert_up,
    expert_down,
    cotangent,
):
    size = lax.axis_size("dp")
    owners = lax.axis_size("expert")
    paired = size == 8 and owners == 4
    me = lax.axis_index("dp").astype(jnp.int32).reshape(1)
    z = lax.axis_index("expert").astype(jnp.int32).reshape(1)
    seq, width = tokens.shape
    per = expert_gate.shape[0]
    experts = per * owners
    experts_pad = -(-experts // 8) * 8
    capacity = (seq * TOP * 9 + 8 * experts - 1) // (8 * experts)
    cap = -(-capacity // 16) * 16
    slim = query_weight.shape[0]
    segments = segment_ids.reshape(seq, 1)
    (a_first, a_last), (b_first, b_last) = split_groups(per)

    cots = lax.all_gather(cotangent, "expert", axis=0, tiled=True)
    packed = run_pack(query_weight, key_weight, value_weight, router_weight, attn_gain, ffn_gain)
    shards = jnp.stack([expert_gate, expert_up, jnp.swapaxes(expert_down, 1, 2)], axis=1)
    a_shard, b_shard = shards[a_first:a_last], shards[b_first:b_last]

    ids = jnp.arange(experts_pad, dtype=jnp.int32)
    hot = jnp.any(expert_choices[:, None, :] == ids[None, :, None], axis=2)
    hot = hot.astype(BF).T
    at = jnp.arange(seq, dtype=jnp.int32)
    earlier = (at[:, None] < at[None, :]).astype(BF)
    place = jnp.dot(hot, earlier, preferred_element_type=F32)
    place = jnp.where(hot > 0, place, -1.0).astype(BF)
    across = width // seq
    place = jnp.pad(place, ((0, EXTRA * across - experts_pad), (0, 0)))
    place = place.reshape(EXTRA // 8, across, 8, seq).swapaxes(1, 2).reshape(EXTRA, width)

    if paired:
        half = slim // 2
        full = [(0, 0, slim), (2, 0, slim), (4, 0, slim), (6, 0, slim)]
        full += [(m + 1, first, rows) for m, first, rows in full]
        split = [(0, 0, slim), (2, 0, slim), (4, 0, slim), (6, 0, half), (6, half, half)]
        split += [(m + 1, first, rows) for m, first, rows in split]
        order = segment_ids
        qx, qy, q1 = (swap(packed, bit, size) for bit in (2, 4, 1))
        order, qx, qy, q1 = wait(order, qx, qy, q1)
        qa, qb = swap(qx[:half], 4, size), swap(qy[half:], 2, size)
        q3 = swap(qx, 1, size)
        o_shard = hold(order, output_weight)
        ox, oy = swap(o_shard, 2, size), swap(o_shard, 4, size)
        order, qa, qb, q3, a_shard, b_shard, segments, place = wait(
            order, qa, qb, q3, a_shard, b_shard, segments, place
        )
        q5, q6, q7 = swap(hold(order, qy), 1, size), swap(qa, 1, size), swap(qb, 1, size)
        order, q5, q6, q7, ox, oy = wait(order, q5, q6, q7, ox, oy)
        qkv_pieces = ([packed, qx, qy, qa, qb, q1, q3, q5, q6, q7], split)
        oc, o3, o5 = swap(oy, 2, size), swap(ox, 1, size), swap(oy, 1, size)
        ay, o1 = swap(hold(order, a_shard), 4, size), swap(hold(order, output_weight), 1, size)
        low_one, qkv, ctx, probs, extra = run_attention(
            me, hold(order, tokens), segment_ids, segments, qkv_pieces, size, experts_pad + 16
        )
        order, ctx, oc, o3, o5, o1 = wait(order, ctx, oc, o3, o5, o1)
        o7, ax = swap(oc, 1, size), swap(hold(order, a_shard), 2, size)
        order, o7, cots = wait(order, o7, cots)
        out_pieces = ([output_weight, ox, oy, oc, o1, o3, o5, o7], full)
        res, low_two = run_residual(
            me, hold(order, tokens), ctx, extra, place, out_pieces, size
        )
        order, low_two, ay = wait(order, low_two, ay)
        far, near = cross(low_two, 2), cross(low_two, 1)
        held = hold(order, b_shard)
        by, bx = swap(held, 4, size), swap(held, 2, size)
        order, ax = wait(order, ax)
        ac = swap(ax, 4, size)
        order, far, near = wait(order, far, near)
        middle = along(hold(order, low_two), [(1, 2), (2, 1)])
        passed = along(far, [(2, 3), (1, 0)])
        order, by, bx = wait(order, by, bx)
        order, b_left, b_up = wait(order, bx[..., :half, :], by[..., half:, :])
        order, middle, passed = wait(order, middle, passed)
        xs = [low_two, near, far, middle, passed]
        low_all = lax.all_gather(hold(order, low_one), "expert", axis=0, tiled=True)
        ba, bb = swap(b_left, 4, size), swap(b_up, 2, size)
        a1, a3, a5 = (swap(hold(order, v), 1, size) for v in (a_shard, ax, ay))
        pos, p, own_p, xs[3] = run_router(z, hold(order, extra), xs, per, owners)
        xs = xs[:owners]
        order, p, ac, a1, a3, a5 = wait(order, p, ac, a1, a3, a5)
        a7, b3, b5 = swap(ac, 1, size), swap(hold(order, bx), 1, size), swap(hold(order, by), 1, size)
        order, a7 = wait(order, a7)
        b1 = swap(hold(order, b_shard), 1, size)
        a_pieces = ([a_shard, ax, ay, ac, a1, a3, a5, a7], full)
    else:
        qkv_pieces = plain_shards(packed, size)
        out_pieces = plain_shards(output_weight, size)
        a_pieces, b_pieces = plain_shards(a_shard, size), plain_shards(b_shard, size)
        low_one, qkv, ctx, probs, extra = run_attention(
            me, tokens, segment_ids, segments, qkv_pieces, size, experts_pad + 16
        )
        res, low_two = run_residual(me, tokens, ctx, extra, place, out_pieces, size)
        xs = plain_owners(low_two, owners)
        low_all = lax.all_gather(low_one, "expert", axis=0, tiled=True)
        pos, p, own_p, _ = run_router(z, extra, xs, per, owners)
        order = p
    low_all = low_all.reshape(owners, width, seq)

    a_rows = run_experts(
        me, z, pos, hold(order, p), xs, cots, a_pieces, None, size, a_first, a_last - a_first, cap
    )
    if paired:
        order, a_gate, ba, bb, b1, b3, b5 = wait(order, a_rows[2], ba, bb, b1, b3, b5)
        b6, b7 = swap(ba, 1, size), swap(bb, 1, size)
        order, b6, b7 = wait(order, b6, b7)
        b_pieces = ([b_shard, bx, by, ba, bb, b1, b3, b5, b6, b7], split)
    b_rows = run_experts(
        me, z, pos, hold(order, p), xs, cots, b_pieces, a_rows[3], size, b_first, b_last - b_first, cap
    )
    expert_total = lax.psum_scatter(b_rows[3], "dp", scatter_dimension=0, tiled=False)
    expert_total = expert_total.astype(F32)
    expert_outputs = (
        expert_total[:, 0],
        expert_total[:, 1],
        jnp.swapaxes(expert_total[:, 2], 1, 2),
    )
    back_rows = ([a_rows[1], b_rows[1]], [a_rows[2], b_rows[2]], cap, experts_pad)
    last_part = run_combine_back(z, pos, *back_rows, owners - 1, 1)[0]
    if paired:
        order, last_part = wait(order, last_part)
        passed, middle = along(last_part, [(3, 2), (0, 1)]), along(last_part, [(1, 2), (2, 1)])
    else:
        order = last_part
    backs = run_combine_back(z, hold(order, pos), *back_rows, 0, owners - 1)
    backs = [*backs, last_part]
    out_rows = [a_rows[0], b_rows[0]]
    if paired:
        outs = run_combine_out(hold(order, pos), out_rows, cap)
        order, passed, middle, *outs = wait(order, passed, middle, *outs)
        far, near = cross(add(backs[2], passed), 2), cross(hold(order, backs[1]), 1)
        order, far, near = wait(order, far, near)
        backs = [backs[0], near, far, middle]
        last_out = hold(order, outs[3])
        passed, middle = along(last_out, [(3, 2), (0, 1)]), along(last_out, [(1, 2), (2, 1)])
    else:
        outs = run_combine_out(pos, out_rows, cap)
        backs = plain_return(backs, owners)
        outs = plain_return(outs, owners)
        order = backs[0]
    res_grad, ctx_grad, ext_grad, o_own, o_other = run_second(
        me, own_p, hold(order, extra), low_two, res, cotangent, ctx, backs, out_pieces, size, per
    )
    back, blocks = run_heads(ctx_grad, qkv, probs, owners)
    if paired:
        order, blocks, back, passed, middle = wait(order, blocks, back, passed, middle)
    back_all = exchange(blocks)
    if paired:
        o_other = swap(hold(order, o_other), 1, size)
        order, o_other = wait(order, o_other)
        mid = width // 2
        o_up, o_left = add(o_own[2:, :, :mid], o_other[2:, :, :mid]), add(
            o_own[1::2, :, mid:], o_other[1::2, :, mid:]
        )
        relay = add(outs[2], passed)
        order, o_up, o_left, relay = wait(order, o_up, o_left, relay)
        o_up, o_left = swap(o_up, 4, size), swap(o_left, 2, size)
    grad_tokens, ext_cols = run_first(
        me, hold(order, back), tokens, extra, ext_grad, res_grad, qkv_pieces, size
    )
    if paired:
        order, ext_cols, o_up, o_left = wait(order, ext_cols, o_up, o_left)

        def three(*values):
            return sum(v.astype(F32) for v in values)

        o_second = three(o_own[1, :, :mid], o_other[1, :, :mid], o_up[1]).astype(BF)
        o_third = three(o_own[2, :, mid:], o_other[2, :, mid:], o_left[1]).astype(BF)
        o_first = three(o_own[0, :, :mid], o_other[0, :, :mid], o_up[0])
        o_last = three(o_own[0, :, mid:], o_other[0, :, mid:], o_left[0])
        order, back_all, o_second, o_third, o_first, o_last = wait(
            order, back_all, o_second, o_third, o_first, o_last
        )
        o_second, o_third = swap(o_second, 2, size), swap(o_third, 4, size)
        far_out, near_out = cross(hold(order, relay), 2), cross(hold(order, outs[1]), 1)
    parts = run_project(me, low_all, back_all, ext_cols, size)
    if paired:
        near = swap(parts[4], 1, size)
        order, near = wait(order, near)
        pair = [add(parts[m], near[m]) for m in (1, 2, 3)]
        order, o_second, o_third, *pair = wait(order, o_second, o_third, *pair)
        links = [swap(pair[m - 1], 2 * m, size) for m in (1, 2, 3)]
        o_total = jnp.concatenate(
            [three(o_first, o_second).astype(BF), three(o_last, o_third).astype(BF)], axis=1
        )
        o_parts = exchange(o_total)
        order, far_out, near_out = wait(order, far_out, near_out)
        order, o_parts, *links = wait(order, o_parts, *links)
        outs = [outs[0], near_out, far_out, middle]
        total = run_join([parts[0], near[0], *links], o_parts, owners)
        far, near = cross(total, 2), cross(total, 1)
        order, far, near = wait(order, far, near)
        middle_total = along(hold(order, total), [(1, 2), (2, 1)])
        passed_total = along(far, [(2, 3), (1, 0)])
        total = [total, near, far, middle_total, passed_total]
    else:
        total = lax.psum_scatter(parts[0], "dp", scatter_dimension=0, tiled=False)
        total = exchange(jnp.concatenate([total] * owners, axis=0))
    mixed = res
    for part in outs:
        mixed = mixed + part.astype(F32)
    mixed = mixed.astype(BF)
    if paired:
        last, mixed, *expert_outputs = wait(total[4], mixed, *expert_outputs)
        results = run_finish(z, [*total[:4], last], owners, experts)
        query_total, key_total, value_total, out_total, router_total, gain_one, gain_two = results
        router_total = router_total.T
    else:
        o_total = lax.psum_scatter(o_own, "dp", scatter_dimension=0, tiled=False)
        out_total = lax.psum(o_total, "expert").astype(F32)
        total = total.reshape(owners, slim, -1).astype(F32)
        wide, narrow = QW // owners, KW // owners

        def side_by_side(first, last):
            return jnp.concatenate([total[j, :, first:last] for j in range(owners)], axis=1)

        query_total = side_by_side(0, wide)
        key_total = side_by_side(wide, wide + narrow)
        value_total = side_by_side(wide + narrow, wide + 2 * narrow)
        ext_total = jnp.sum(total[:, :, wide + 2 * narrow :], axis=0)
        router_total = ext_total[:, :experts]
        gain_one, gain_two = ext_total[:, experts_pad], ext_total[:, experts_pad + 8]
    return (
        mixed,
        grad_tokens,
        gain_one,
        query_total,
        key_total,
        value_total,
        out_total,
        gain_two,
        router_total,
        *expert_outputs,
    )


def solution(mesh):
    return jax.shard_map(
        body,
        mesh=mesh,
        in_specs=(
            P(("dp", "expert"), None),
            P(("dp", "expert"), None),
            P(("dp", "expert"), None),
            P("dp"),
            P("dp", None),
            P("dp", None),
            P("dp", None),
            P("dp", None),
            P("dp"),
            P("dp", None),
            P("expert", "dp", None),
            P("expert", "dp", None),
            P("expert", None, "dp"),
            P(("dp", "expert"), None),
        ),
        out_specs=(
            P(("dp", "expert"), None),
            P(("dp", "expert"), None),
            P("dp"),
            P("dp", None),
            P("dp", None),
            P("dp", None),
            P("dp", None),
            P("dp"),
            P("dp", None),
            P("expert", "dp", None),
            P("expert", "dp", None),
            P("expert", None, "dp"),
        ),
        check_vma=False,
    )
```
